32 devices in a mesh: ctx: 2 (over core), exp: 4 (over y, x), req: 4 (over z).
Axes of the slice: x: 2, y: 2, z: 4, core: 2. Of those that a mesh axis runs over, the one named last changes fastest.
Arguments:
- queries: bfloat16 [64, 2, 128, 576], P('req', None, ('ctx', 'exp')), parts along dimension 0, may hold values from -21 to 21
- latent_cache: bfloat16 [64, 4096, 576], P('req', ('ctx', 'exp')), parts along dimension 0, may hold values from -4 to 4
- context_lengths: int32 [64], P('req'), parts along dimension 0, may hold values from 16 to 4095, as said below
- value_up: bfloat16 [128, 512, 128], P(('ctx', 'exp')), may hold values from -0.25 to 0.25
- out_proj: bfloat16 [16384, 7168], P(('ctx', 'exp')), may hold values from -0.09375 to 0.09375
- residual: bfloat16 [128, 7168], P(('req', 'exp')), parts along dimension 0, may hold values from -3 to 3
- norm_gain: bfloat16 [7168], replicated, may hold values from 0.099609375 to 1.8984375
- router: bfloat16 [7168, 4], replicated, may hold values from -0.125 to 0.125
- routes: int32 [128, 2], P(('req', 'exp')), parts along dimension 0, may hold values from 0 to 3, all different within a row; in each aligned block of 8 rows (0 to 7, 8 to 15, ...) at most 4 rows name the same one
- expert_gate: bfloat16 [4, 7168, 1024], P('exp', None, 'ctx'), may hold values from -0.0625 to 0.0625
- expert_up: bfloat16 [4, 7168, 1024], P('exp', None, 'ctx'), may hold values from -0.0625 to 0.0625
- expert_down: bfloat16 [4, 1024, 7168], P('exp', 'ctx'), may hold values from -0.375 to 0.375
Outputs:
- output: bfloat16 [128, 7168], P(('req', 'exp'), 'ctx'), parts along dimension 0
The draws below stay inside these ranges and needn't reach their ends.
There are 4 independent parts, one for each index of `req`. The reference program is written for one: setup_inputs(seed, part) draws one part's arguments, and reference() takes and returns one part's arrays. A program takes and returns all parts, laid end to end along the dimension named above; an argument that names none is the same for every part. Nothing has to cross between parts.
Inputs may be any that keep to these rules, and one draw needn't show every extreme that they name: Verify row j of request r sees context positions below context_lengths[r] + j; in every draw one request has 4095. `routes`: each row names 2 different experts; in each aligned block of 8 rows (the rows of one index of exp) no expert is named by more than 4 rows.
All inputs are finite; a program needn't handle non-finite values.
Results may differ from the reference program's by a relative error of at most 0.028.
Values may be sent and summed in bfloat16 or wider, within the bound.
A program may use at most 128 MiB of HBM per device.

```python
import math
import jax
import jax.numpy as jnp
import numpy as np
from jax import lax

D = 7168
HEADS = 128
LAT = 512
ROPE = 64
VDIM = 128
FF = 1024
TOP = 2
REQS = 16
CTX = 4096
ROWS = 32
ROW_DEV = 8
EXPERTS = 4
CAP = 4


def cache_values(key, width):
    normal_part = jnp.clip(jax.random.normal(key, (REQS, CTX, LAT + ROPE), jnp.float32), -4.0, 4.0)
    flat_part = jax.random.uniform(key, (REQS, CTX, LAT + ROPE), jnp.float32, minval=-1.7, maxval=1.7)
    return jnp.where(width > 0.0, flat_part, normal_part)


def draw_latent_cache(key, part):
    values = cache_values(key, 0.0)
    return values.astype(jnp.bfloat16)


def draw_queries(key, part):
    key = jax.random.fold_in(key, 2)
    values = jnp.clip(jax.random.normal(key, (REQS, 2, HEADS, LAT + ROPE), jnp.float32), -4.0, 4.0)
    return values.astype(jnp.bfloat16)


def draw_context_lengths(key, part):
    key = jax.random.fold_in(key, 3)
    lengths = jax.random.randint(key, (REQS,), 16, CTX)
    longest = jax.random.randint(jax.random.fold_in(key, 4), (), 0, REQS)
    return jnp.where(jnp.arange(REQS) == longest, CTX - 1, lengths).astype(jnp.int32)


def shard_levels(stream_key, shape, split, low, high):
    gain = 1.0
    for position, blocks in split:
        heights = jax.random.uniform(jax.random.fold_in(jax.random.fold_in(stream_key, 6), position), (blocks,), jnp.float32, low / len(split), high / len(split))
        gain = gain * jnp.repeat(jnp.exp(heights), shape[position] // blocks).reshape((-1,) + (1,) * (len(shape) - 1 - position))
    return gain


def routed_block(rng, own, number, rows, number_of, top, limit, lean):
    ranking = jax.random.permutation(rng, number_of)
    crowded, usual = load_shares(number_of, rows * top, limit, lean, True), load_shares(number_of, rows * top, limit, lean, False)
    places = jnp.arange(number_of)

    def named(sizes, offset_by):
        used = int((sizes > 0).sum())
        fixed = max(1, used // 4)
        moved = fixed + (places - fixed + offset_by * (used - fixed)) % max(1, number_of - fixed)
        return jnp.zeros((number_of,), jnp.int32).at[ranking[jnp.where(places < fixed, places, moved)]].set(jnp.asarray(sizes, jnp.int32))

    sizes = jnp.where(number % 4 == 0, named(crowded, number // 4), named(usual, number - number // 4 - 1))
    mixed = jax.random.permutation(jax.random.fold_in(own, 3), number_of)
    giver, taker = mixed[0:number_of // 2 * 2:2], mixed[1:number_of // 2 * 2:2]
    room = jnp.minimum(sizes[giver] - 1, limit - sizes[taker]) // 2
    room = jnp.where((giver == ranking[0]) | (taker == ranking[0]) | (sizes[taker] == 0), 0, jnp.maximum(room, 0))
    moved = jax.random.randint(jax.random.fold_in(own, 4), (number_of // 2,), 0, 1 << 20) % (room + 1)
    sizes = sizes.at[giver].add(-moved).at[taker].add(moved)
    items = jnp.searchsorted(jnp.cumsum(sizes), jnp.arange(rows * top), side="right").astype(jnp.int32)
    listing = items.reshape(top, rows).T
    listing = listing[jax.random.permutation(jax.random.fold_in(own, 1), rows)]
    offset_by = jax.random.randint(jax.random.fold_in(own, 2), (rows, 1), 0, top)
    return jnp.take_along_axis(listing, (jnp.arange(top)[None, :] + offset_by) % top, axis=1)


def load_shares(number_of, total, most, lean, full):
    loads = [(1 << 20) // math.isqrt(standing ** lean) + 1 for standing in range(1, number_of + 1)]
    largest = most if full else min(most, max(-(-total // number_of), total * loads[0] // sum(loads)))
    least = 1 if total - largest >= number_of - 1 else 0
    holding, rest = [largest] + [least] * (number_of - 1), total - largest - least * (number_of - 1)
    while rest > 0:
        free = [i for i in range(1, number_of) if holding[i] < largest] or [i for i in range(1, number_of) if holding[i] < most]
        whole, remaining = sum([loads[i] for i in free]), rest
        for i in free:
            more = min(most - holding[i], max(1, remaining * loads[i] // whole), rest)
            holding[i] = holding[i] + more
            rest = rest - more
    return np.array(holding)


def centred(rng, dims, spread, reach, cuts=(), kind=jnp.bfloat16):
    level = shard_levels(rng, dims, cuts, -0.22, 0.18) if cuts else 1.0
    drawn = jax.random.normal(rng, dims, jnp.float32) * spread * level
    return jnp.minimum(jnp.maximum(drawn, -reach), reach).astype(kind)


def setup_inputs(seed: int = 0, part: int = 0) -> dict:
    key_of = jax.random.split(jax.random.key(seed), 13)
    part_keys = jax.random.split(jax.random.fold_in(key_of[12], part), 13)
    queries = draw_queries(jax.random.fold_in(jax.random.fold_in(key_of[12], part), 71), part)
    latent_cache = draw_latent_cache(jax.random.fold_in(jax.random.fold_in(key_of[12], part), 71), part)
    context_lengths = draw_context_lengths(jax.random.fold_in(jax.random.fold_in(key_of[12], part), 71), part)
    value_up = centred(key_of[3], (HEADS, LAT, VDIM), LAT ** -0.5, 0.25, ((0, 8),))
    out_proj = centred(key_of[4], (HEADS * VDIM, D), (HEADS * VDIM // 4) ** -0.5, 0.09375, ((0, 8),))
    residual = centred(part_keys[5], (ROWS, D), 0.5, 3.0, ((0, 4),))
    norm_gain = jnp.clip(1.0 + 0.18 * jax.random.normal(key_of[6], (D,), jnp.float32), 0.099609375, 1.8984375).astype(jnp.bfloat16)
    router = centred(key_of[7], (D, EXPERTS), (D // 4) ** -0.5, 0.125)
    routes_keys = jax.random.split(jax.random.fold_in(part_keys[8], 1), ROWS // ROW_DEV)
    routes_turns = jax.random.permutation(jax.random.fold_in(part_keys[8], 3), ROWS // ROW_DEV)
    routes = jax.vmap(lambda own, number: routed_block(jax.random.fold_in(part_keys[8], 2), own, number, ROW_DEV, EXPERTS, TOP, CAP, 2))(routes_keys, routes_turns).reshape((ROWS, TOP))
    expert_gate = centred(key_of[9], (EXPERTS, D, FF), D ** -0.5, 0.0625, ((0, 4), (2, 2)))
    expert_up = centred(key_of[10], (EXPERTS, D, FF), D ** -0.5, 0.0625, ((0, 4), (2, 2)))
    expert_down = centred(key_of[11], (EXPERTS, FF, D), (FF // 4) ** -0.5, 0.375, ((0, 4), (1, 2)))
    return dict(queries=queries, latent_cache=latent_cache, context_lengths=context_lengths, value_up=value_up, out_proj=out_proj, residual=residual, norm_gain=norm_gain, router=router, routes=routes, expert_gate=expert_gate, expert_up=expert_up, expert_down=expert_down)


route_scale = 2.5

def reference(queries, latent_cache, context_lengths, value_up, out_proj, residual, norm_gain, router, routes, expert_gate, expert_up, expert_down):
    score_scale = 1.0 / math.sqrt(VDIM + ROPE)
    positions = jnp.arange(CTX, dtype=jnp.int32)
    offsets = jnp.arange(2, dtype=jnp.int32)

    def attend(inputs):
        query_rows, cache_rows, length = inputs
        scores = jnp.einsum('jhd,td->jht', query_rows.astype(jnp.float32), cache_rows.astype(jnp.float32)) * score_scale
        visible = positions[None, None, :] < (length + offsets)[:, None, None]
        masked = jnp.where(visible, scores, -1e+30)
        row_max = lax.optimization_barrier(jnp.max(masked, axis=-1, keepdims=True))
        weights = jnp.where(visible, jnp.exp(masked - row_max), 0.0)
        weight_sum = lax.optimization_barrier(jnp.sum(weights, axis=-1))
        rounded = lax.optimization_barrier(weights.astype(jnp.bfloat16)).astype(jnp.float32)
        latents = cache_rows[:, :LAT].astype(jnp.float32)
        weighted = jnp.einsum('jht,tl->jhl', rounded, latents)
        return (weighted / weight_sum[..., None]).astype(jnp.bfloat16)
    context = lax.map(attend, (queries, latent_cache, context_lengths))
    head_out = jnp.einsum('rjhl,hlv->rjhv', context.astype(jnp.float32), value_up.astype(jnp.float32)).astype(jnp.bfloat16)
    head_out = head_out.reshape(ROWS, HEADS * VDIM)
    attention = jnp.dot(head_out, out_proj, preferred_element_type=jnp.float32)
    hidden = (residual.astype(jnp.float32) + attention).astype(jnp.bfloat16)
    hidden_wide = hidden.astype(jnp.float32)
    inverse = lax.rsqrt(lax.optimization_barrier(jnp.mean(hidden_wide * hidden_wide, axis=-1, keepdims=True)) + 1e-06)
    normed = (hidden_wide * inverse * norm_gain.astype(jnp.float32)).astype(jnp.bfloat16)
    affinity = jax.nn.sigmoid(jnp.dot(normed, router, preferred_element_type=jnp.float32))
    chosen = (routes[:, :, None] == jnp.arange(EXPERTS, dtype=jnp.int32)[None, None, :]).astype(jnp.float32)
    picked = lax.optimization_barrier(jnp.sum(chosen * affinity[:, None, :], axis=-1))
    gate_weights = route_scale * picked / lax.optimization_barrier(jnp.sum(picked, axis=-1, keepdims=True))
    mixing = lax.optimization_barrier(jnp.sum(gate_weights[:, :, None] * chosen, axis=1))

    def expert(expert_id):
        gate_part = jnp.dot(normed, expert_gate[expert_id], preferred_element_type=jnp.float32)
        up_part = jnp.dot(normed, expert_up[expert_id], preferred_element_type=jnp.float32)
        active = (jax.nn.silu(gate_part) * up_part).astype(jnp.bfloat16)
        return jnp.dot(active, expert_down[expert_id], preferred_element_type=jnp.float32)
    expert_rows = lax.map(expert, jnp.arange(EXPERTS, dtype=jnp.int32))
    mixture = jnp.einsum('re,erd->rd', mixing, expert_rows, precision=lax.Precision.HIGHEST)
    return (hidden_wide + mixture).astype(jnp.bfloat16)
```

```python
import functools
import math

import jax
import jax.numpy as jnp
from jax import lax
from jax.experimental import pallas as pl
from jax.experimental.pallas import tpu as pltpu
from jax.sharding import PartitionSpec as P

route_scale = 2.5


def on_device(
    queries,
    latent_cache,
    context_lengths,
    value_up,
    out_proj,
    residual,
    norm_gain,
    router,
    routes,
    expert_gate,
    expert_up,
    expert_down,
):
    latent_width = value_up.shape[1]
    value_width = value_up.shape[2]
    rope_width = queries.shape[3] - latent_width
    score_scale = 1.0 / math.sqrt(value_width + rope_width)
    heads_here = queries.shape[2]
    block_len = latent_cache.shape[1]
    device = lax.axis_index(("ctx", "exp"))
    all_queries = lax.all_gather(queries, ("ctx", "exp"), axis=2, tiled=True)
    scores = (
        jnp.einsum("rjhd,rtd->rjht", all_queries, latent_cache, preferred_element_type=jnp.float32)
        * score_scale
    )
    positions = device * block_len + jnp.arange(block_len, dtype=jnp.int32)
    visible_upto = context_lengths[:, None] + jnp.arange(2, dtype=jnp.int32)[None, :]
    visible = positions[None, None, None, :] < visible_upto[:, :, None, None]
    masked = jnp.where(visible, scores, -1e30)
    row_max = lax.pmax(jnp.max(masked, axis=-1), ("ctx", "exp"))
    weights = jnp.where(visible, jnp.exp(masked - row_max[..., None]), 0.0)
    weight_sum = jnp.sum(weights, axis=-1)
    latents = latent_cache[:, :, :latent_width]
    weighted = jnp.einsum(
        "rjht,rtl->rjhl", weights.astype(jnp.bfloat16), latents, preferred_element_type=jnp.float32
    )
    summed, sum_all = lax.psum((weighted, weight_sum), ("ctx", "exp"))
    own_weighted = lax.dynamic_slice_in_dim(summed, device * heads_here, heads_here, 2)
    own_sum = lax.dynamic_slice_in_dim(sum_all, device * heads_here, heads_here, 2)
    context = (own_weighted / own_sum[..., None]).astype(jnp.bfloat16)
    head_out = jnp.einsum(
        "rjhl,hlv->rjhv", context, value_up, preferred_element_type=jnp.float32
    ).astype(jnp.bfloat16)
    row_total = head_out.shape[0] * head_out.shape[1]
    head_out = head_out.reshape(row_total, heads_here * value_width)
    own_rows = residual.shape[0]
    owner_index = lax.axis_index("exp")
    attention_all = lax.psum(
        jnp.dot(head_out, out_proj, preferred_element_type=jnp.float32), ("ctx", "exp")
    )
    attention = lax.dynamic_slice_in_dim(attention_all, owner_index * own_rows, own_rows, 0)
    hidden = (residual.astype(jnp.float32) + attention).astype(jnp.bfloat16)
    hidden_wide = hidden.astype(jnp.float32)
    inverse = lax.rsqrt(jnp.mean(hidden_wide * hidden_wide, axis=-1, keepdims=True) + 1e-06)
    normed = (hidden_wide * inverse * norm_gain.astype(jnp.float32)).astype(jnp.bfloat16)
    affinity = jax.nn.sigmoid(jnp.dot(normed, router, preferred_element_type=jnp.float32))
    expert_count = router.shape[1]
    top_count = routes.shape[1]
    capacity = max(2, own_rows * top_count // expert_count)
    chosen = (
        routes[:, :, None] == jnp.arange(expert_count, dtype=jnp.int32)[None, None, :]
    ).astype(jnp.float32)
    picked = jnp.sum(chosen * affinity[:, None, :], axis=-1)
    gate_weights = route_scale * picked / jnp.sum(picked, axis=-1, keepdims=True)
    per_row = jnp.sum(chosen, axis=1)
    earlier = jnp.cumsum(per_row, axis=0) - per_row
    slot_index = jnp.sum(chosen * earlier[:, None, :], axis=-1)
    slot_hot = (
        slot_index[:, :, None] == jnp.arange(capacity, dtype=jnp.float32)[None, None, :]
    ).astype(jnp.float32)
    placement = chosen[:, :, :, None] * slot_hot[:, :, None, :]
    row_place = jnp.sum(placement, axis=1).reshape(own_rows, expert_count * capacity)
    gate_place = jnp.sum(placement * gate_weights[:, :, None, None], axis=1).reshape(
        own_rows, expert_count * capacity
    )
    model_width = normed.shape[1]
    outgoing = jnp.einsum(
        "rs,rd->sd", row_place.astype(jnp.bfloat16), normed, preferred_element_type=jnp.float32
    ).astype(jnp.bfloat16)
    outgoing = outgoing.reshape(expert_count, capacity, model_width)
    arrived = lax.all_to_all(outgoing, "exp", split_axis=0, concat_axis=0, tiled=True)
    gate_part = jnp.einsum(
        "scd,df->scf", arrived, expert_gate[0], preferred_element_type=jnp.float32
    )
    up_part = jnp.einsum("scd,df->scf", arrived, expert_up[0], preferred_element_type=jnp.float32)
    active = (jax.nn.silu(gate_part) * up_part).astype(jnp.bfloat16)
    partial_out = jnp.einsum(
        "scf,fd->scd", active, expert_down[0], preferred_element_type=jnp.float32
    )
    col_width = model_width // lax.axis_size("ctx")
    ctx_index = lax.axis_index("ctx")
    own_cols = lax.dynamic_slice_in_dim(hidden_wide, ctx_index * col_width, col_width, 1)
    full_sum = lax.psum(partial_out.astype(jnp.bfloat16), "ctx").astype(jnp.float32)
    returned = lax.all_to_all(
        full_sum.astype(jnp.bfloat16), "exp", split_axis=0, concat_axis=0, tiled=True
    ).astype(full_sum.dtype)
    returned = lax.dynamic_slice_in_dim(returned, ctx_index * col_width, col_width, 2)
    mixture = jnp.dot(
        gate_place,
        returned.reshape(expert_count * capacity, col_width),
        precision=lax.Precision.HIGHEST,
    )
    return (own_cols + mixture).astype(jnp.bfloat16)


MESH = pl.DeviceIdType.MESH
F32 = jnp.float32
BF16 = jnp.bfloat16
PAIR = 2
SLOTS = 5
BLOCKS = 8
AHEAD = 3


def lay_out(chunks):
    places, count = {}, 0
    for name, number in (
        ("own", 3), ("diag", 2), ("core", 4), ("stat", 7), ("fold", 1), ("cross", 2), ("last", 2),
    ):
        places[name] = (count, number)
        count += number * chunks
    for name, number in (("route", 3), ("swap", 2), ("rows", 6), ("hid", 4), ("hidfwd", 3)):
        places[name] = (count, number)
        count += number
    return places, count


def contract(a, b, da, db):
    return lax.dot_general(a, b, (((da,), (db,)), ((), ())), preferred_element_type=F32)


def layer_kernel(
    lens, q_hbm, cache_hbm, vu_hbm, op_hbm, res, gain, router_hbm, routes, eg_hbm, eu_hbm, ed_hbm,
    out,
    qbuf, cbuf, acc, mown, stat, norm, crx, x2, y2, x3, y3, ctx2, vu, ho, wslot, eg, eu, router,
    chosen, pbuf, prx, tsum, rrx, hid, xn, act, gcol,
    send, recv, csem, wsem, osem,
):
    chunks, _, heads_rows, width = q_hbm.shape
    heads = heads_rows // 2
    block_len, latent = cache_hbm.shape[2], vu.shape[1]
    vdim = vu.shape[2]
    places, _ = lay_out(chunks)
    scale = 1.0 / math.sqrt(vdim + width - latent)
    half = hid.shape[3]
    cols = half * 2 // BLOCKS
    per_half = BLOCKS // 2
    c = lax.axis_index("ctx")
    e = lax.axis_index("exp")
    ey, ex = e // 2, e % 2
    me = c * 4 + e
    ex_n = e + 1 - 2 * ex
    ey_n = e + 2 - 4 * ey
    ed_n = 3 - e
    others = (ex_n, ey_n, ed_n)
    peers = [(1 - c, e)] + [(c, o) for o in others] + [(1 - c, o) for o in others]

    def remote(kind, g, k, src, dst, to):
        first, stride = places[kind]
        place = first + g * stride + k
        return pltpu.make_async_remote_copy(
            src_ref=src, dst_ref=dst, send_sem=send.at[place], recv_sem=recv.at[place],
            device_id={"ctx": to[0], "exp": to[1]}, device_id_type=MESH,
        )

    core_to, x_to, y_to = (1 - c, e), (c, ex_n), (c, ey_n)

    def own_copy(g, k):
        return remote("own", g, k, q_hbm.at[g], qbuf.at[g, me], (core_to, x_to, y_to)[k])

    def diag_copy(g, k):
        source = c * 4 + (ex_n if k == 0 else ey_n)
        view = qbuf.at[g, source, k]
        return remote("diag", g, k, view, view, (y_to, x_to)[k])

    def core_copy(g, k):
        source = c * 4 + (ex_n, ey_n, ed_n, ed_n)[k]
        view = qbuf.at[g, source] if k < 2 else qbuf.at[g, source, k - 2]
        return remote("core", g, k, view, view, core_to)

    def stat_copy(g, k):
        return remote("stat", g, k, stat.at[g, me], stat.at[g, me], peers[k])

    def fold_copy(g):
        return remote("fold", g, 0, norm.at[g, 1 - c], crx.at[g], core_to)

    def cross_copy(g, k):
        if k == 0:
            return remote("cross", g, 0, crx.at[g, :, 1 - ex, 0], x2.at[g], x_to)
        return remote("cross", g, 1, crx.at[g, 1 - ey, :, 1], y2.at[g], y_to)

    def last_copy(g, k):
        if k == 0:
            return remote("last", g, 0, x2.at[g, 1 - ey], y3.at[g], y_to)
        return remote("last", g, 1, y2.at[g, 1 - ex], x3.at[g], x_to)

    def route_copy(k):
        return remote("route", 0, k, chosen.at[e], chosen.at[e], (c, others[k]))

    def swap_copy(p):
        return remote("swap", 0, p, pbuf.at[p, 0], prx.at[p], core_to)

    def rows_copy(p, k):
        return remote("rows", 0, p * 3 + k, tsum.at[p, others[k]], rrx.at[p, k], (c, others[k]))

    def hid_copy(k):
        to = (x_to, y_to, (c, ed_n), core_to)[k]
        return remote("hid", 0, k, hid.at[e, c], hid.at[e, c], to)

    def hidfwd_copy(k):
        view = hid.at[others[k], c]
        return remote("hidfwd", 0, k, view, view, core_to)

    def cache_copy(g):
        return pltpu.make_async_copy(cache_hbm.at[g], cbuf.at[g % 2], csem.at[g % 2])

    def column(i):
        side = jnp.where(i < per_half, 1 - c, c)
        return pl.multiple_of((side * per_half + i % per_half) * cols, cols)

    def op_copy(i):
        return pltpu.make_async_copy(
            op_hbm.at[:, pl.ds(column(i), cols)], wslot.at[i % SLOTS], osem.at[i % SLOTS]
        )

    depth = ed_hbm.shape[0]

    def down_copy(i):
        place = pl.ds(pl.multiple_of((i % 4) * depth, depth), depth)
        return pltpu.make_async_copy(
            ed_hbm.at[:, pl.ds(column(i), cols)], wslot.at[3 + i // 4, place], wsem.at[4 + i]
        )

    own_q = pltpu.make_async_copy(q_hbm, qbuf.at[:, me], wsem.at[0])
    vu_copy = pltpu.make_async_copy(vu_hbm, vu, wsem.at[1])
    eg_copy = pltpu.make_async_copy(eg_hbm, eg, wsem.at[2])
    eu_copy = pltpu.make_async_copy(eu_hbm, eu, wsem.at[3])
    router_copy = pltpu.make_async_copy(router_hbm, router, wsem.at[4 + BLOCKS])

    own_q.start()
    cache_copy(0).start()
    lanes = lax.broadcasted_iota(jnp.int32, chosen.shape[1:], 1)
    named = (routes[:, 0:1] == lanes) | (routes[:, 1:2] == lanes)
    chosen[e] = named.astype(F32)

    barrier = pltpu.get_barrier_semaphore()
    for to in peers:
        pl.semaphore_signal(
            barrier, inc=1, device_id={"ctx": to[0], "exp": to[1]}, device_id_type=MESH
        )
    pl.semaphore_wait(barrier, len(peers))

    for g in range(AHEAD):
        for k in range(3):
            own_copy(g, k).start()
    for k in range(3):
        route_copy(k).start()
    vu_copy.start()
    router_copy.start()
    own_q.wait()

    rows = 8 * heads_rows

    def attend(g):
        cache_copy(g).wait()

        @pl.when(g + 1 < chunks)
        def _():
            cache_copy(g + 1).start()

        for r in range(PAIR):
            q = qbuf[g, :, r].reshape(rows, width)
            keys = cbuf[g % 2, r]
            s = contract(keys, q, 1, 1) * scale
            position = me * block_len + lax.broadcasted_iota(jnp.int32, s.shape, 0)
            later = lax.broadcasted_iota(jnp.int32, s.shape, 1) // heads % 2
            visible = position < lens[g * PAIR + r] + later
            s = jnp.where(visible, s, -1e30)
            m = jnp.max(s, axis=0, keepdims=True)
            p = jnp.where(visible, jnp.exp(s - m), 0.0)
            total = jnp.sum(p, axis=0, keepdims=True)
            acc[g % 2, r] = contract(p.astype(BF16), keys[:, :latent], 0, 0)
            mown[g % 2, r : r + 1] = m
            z = jnp.where(total > 0.0, m + jnp.log(jnp.maximum(total, 1e-30)), -1e30)
            stat[g, me, r : r + 1] = z
        for k in range(7):
            stat_copy(g, k).start()

    def normalise(g):
        for k in range(7):
            stat_copy(g, k).wait_recv()
        for r in range(PAIR):
            z = stat[g, :, r]
            top = jnp.max(z, axis=0, keepdims=True)
            whole = top + jnp.log(jnp.sum(jnp.exp(z - top), axis=0, keepdims=True))
            factor = jnp.exp(mown[g % 2, r : r + 1] - whole)
            factor = jnp.transpose(jnp.broadcast_to(factor, (128, rows)))
            for k in range(latent // 128):
                part = acc[g % 2, r, :, k * 128 : (k + 1) * 128] * factor
                norm[g, :, :, :, r, :, k * 128 : (k + 1) * 128] = part.astype(BF16).reshape(
                    2, 2, 2, heads_rows, 128
                )
        fold_copy(g).start()

    def fold(g):
        fold_copy(g).wait_recv()
        crx[g] = (crx[g].astype(F32) + norm[g, c].astype(F32)).astype(BF16)
        cross_copy(g, 0).start()
        cross_copy(g, 1).start()

    def cross(g):
        cross_copy(g, 0).wait_recv()
        x2[g] = (x2[g].astype(F32) + crx[g, :, ex, 0].astype(F32)).astype(BF16)
        last_copy(g, 0).start()
        cross_copy(g, 1).wait_recv()
        y2[g] = (y2[g].astype(F32) + crx[g, ey, :, 1].astype(F32)).astype(BF16)
        last_copy(g, 1).start()

    def last(g):
        last_copy(g, 0).wait_recv()
        ctx2[g % 2, 0] = (x2[g, ey].astype(F32) + y3[g].astype(F32)).astype(BF16)
        last_copy(g, 1).wait_recv()
        ctx2[g % 2, 1] = (y2[g, ex].astype(F32) + x3[g].astype(F32)).astype(BF16)

        @pl.when(g % 2 == 1)
        def _():
            both = ctx2[...].reshape(4 * heads_rows, latent)
            for h in range(heads):
                every = jnp.dot(both, vu[h], preferred_element_type=F32).reshape(8, heads, vdim)
                mine = lax.broadcasted_iota(jnp.int32, every.shape, 1) == h
                place = pl.ds(pl.multiple_of((g // 2) * 8, 8), 8)
                ho[place, h * vdim : (h + 1) * vdim] = jnp.sum(
                    jnp.where(mine, every, 0.0), axis=1
                )

    vu_copy.wait()

    def step(s, _):
        def at(lag, run):
            @pl.when((s >= lag) & (s < chunks + lag))
            def _():
                run(s - lag)

        @pl.when(s + AHEAD < chunks)
        def _():
            for k in range(3):
                own_copy(s + AHEAD, k).start()

        def forward(g):
            own_copy(g, 1).wait_recv()
            diag_copy(g, 0).start()
            core_copy(g, 0).start()
            own_copy(g, 2).wait_recv()
            diag_copy(g, 1).start()
            core_copy(g, 1).start()

        def forward_diag(g):
            for k in range(2):
                diag_copy(g, k).wait_recv()
                core_copy(g, 2 + k).start()

        def attend_when_here(g):
            own_copy(g, 0).wait_recv()
            for k in range(4):
                core_copy(g, k).wait_recv()
            attend(g)

        at(0, forward)
        at(1, forward_diag)
        at(3, normalise)
        at(4, fold)
        at(5, cross)
        at(6, last)
        at(2, attend_when_here)

        @pl.when(s < SLOTS)
        def _():
            op_copy(s).start()

        @pl.when(s == SLOTS)
        def _():
            eg_copy.start()

        @pl.when(s == SLOTS + 1)
        def _():
            eu_copy.start()

        return 0

    lax.fori_loop(0, chunks + 6, step, 0)

    own_rows = res.shape[0]

    def project(i, _):
        op_copy(i).wait()
        part = jnp.dot(ho[...].astype(BF16), wslot[i % SLOTS], preferred_element_type=F32)
        place = pl.ds(pl.multiple_of((i % per_half) * cols, cols), cols)
        pbuf[0, i // per_half, :, :, place] = part.astype(BF16).reshape(4, own_rows, cols)

        @pl.when(i + SLOTS < BLOCKS)
        def _():
            op_copy(i + SLOTS).start()

        @pl.when(i == per_half - 1)
        def _():
            swap_copy(0).start()

        return 0

    lax.fori_loop(0, BLOCKS, project, 0)
    for i in range(BLOCKS):
        down_copy(i).start()

    def reduce_rows(p):
        swap_copy(p).wait_recv()
        tsum[p] = (prx[p].astype(F32) + pbuf[p, 1].astype(F32)).astype(BF16)
        for k in (2, 0, 1):
            rows_copy(p, k).start()
        total = tsum[p, e].astype(F32)
        for k in range(3):
            rows_copy(p, k).wait_recv()
            total = total + rrx[p, k].astype(F32)
        return total

    own_cols = pl.ds(pl.multiple_of(c * half, half), half)
    hid[e, c] = (res[:, own_cols].astype(F32) + reduce_rows(0)).astype(BF16)
    for k in (2, 0, 1, 3):
        hid_copy(k).start()
    for k in range(3):
        hid_copy(k).wait_recv()
        hidfwd_copy(k).start()
    hid_copy(3).wait_recv()
    for k in range(3):
        hidfwd_copy(k).wait_recv()
        route_copy(k).wait_recv()
    router_copy.wait()
    eg_copy.wait()
    eu_copy.wait()

    sides = [hid[:, side].astype(F32).reshape(4 * own_rows, half) for side in range(2)]
    squares = sum(jnp.sum(v * v, axis=-1, keepdims=True) for v in sides)
    inverse = lax.rsqrt(squares / (2 * half) + 1e-06)
    for side in range(2):
        spread = gain[:, side * half : (side + 1) * half].astype(F32)
        xn[side] = (sides[side] * inverse * spread).astype(BF16)
    span = [slice(side * half, (side + 1) * half) for side in range(2)]
    both_sides = lambda w: sum(
        jnp.dot(xn[side], w[span[side], :], preferred_element_type=F32) for side in range(2)
    )
    affinity = jax.nn.sigmoid(both_sides(router))
    picked = affinity * chosen[...].reshape(4 * own_rows, 128)[:, : affinity.shape[1]]
    weights = route_scale * picked / jnp.sum(picked, axis=-1, keepdims=True)
    mine = lax.broadcasted_iota(jnp.int32, weights.shape, 1) == e
    gcol[...] = jnp.broadcast_to(
        jnp.sum(jnp.where(mine, weights, 0.0), axis=-1, keepdims=True), gcol.shape
    )
    gate_part = both_sides(eg)
    up_part = both_sides(eu)
    act[...] = (gate_part / (1.0 + jnp.exp(-gate_part)) * up_part).astype(BF16)

    for i in range(BLOCKS):
        down_copy(i).wait()
        block = wslot[3 + i // 4, (i % 4) * depth : (i % 4 + 1) * depth]
        part = jnp.dot(act[...], block, preferred_element_type=F32) * gcol[:, 0:1]
        place = slice((i % per_half) * cols, (i % per_half + 1) * cols)
        pbuf[1, i // per_half, :, :, place] = part.astype(BF16).reshape(4, own_rows, cols)
        if i == per_half - 1:
            swap_copy(1).start()
    out[...] = (hid[e, c].astype(F32) + reduce_rows(1)).astype(BF16)

    def drain(g, _):
        for k in range(3):
            own_copy(g, k).wait_send()
        for k in range(2):
            diag_copy(g, k).wait_send()
            cross_copy(g, k).wait_send()
            last_copy(g, k).wait_send()
        for k in range(4):
            core_copy(g, k).wait_send()
        for k in range(7):
            stat_copy(g, k).wait_send()
        fold_copy(g).wait_send()
        return 0

    lax.fori_loop(0, chunks, drain, 0)
    for k in range(3):
        route_copy(k).wait_send()
        hidfwd_copy(k).wait_send()
        rows_copy(0, k).wait_send()
        rows_copy(1, k).wait_send()
    for k in range(4):
        hid_copy(k).wait_send()
    for p in range(2):
        swap_copy(p).wait_send()


def fused_on_device(
    queries, latent_cache, context_lengths, value_up, out_proj, residual, norm_gain, router,
    routes, expert_gate, expert_up, expert_down,
):
    reqs, verify, heads, width = queries.shape
    chunks = reqs // PAIR
    hr = verify * heads
    _, block_len, _ = latent_cache.shape
    _, latent, vdim = value_up.shape
    own_rows, model = residual.shape
    half = model // 2
    ff = expert_down.shape[1]
    rows = 8 * hr
    _, count = lay_out(chunks)
    vmem, anywhere = pl.BlockSpec(memory_space=pltpu.VMEM), pl.BlockSpec(memory_space=pl.ANY)
    scratch = [
        pltpu.VMEM((chunks, 8, PAIR, hr, width), BF16),
        pltpu.VMEM((2, PAIR, block_len, width), BF16),
        pltpu.VMEM((2, PAIR, rows, latent), F32),
        pltpu.VMEM((2, PAIR, rows), F32),
        pltpu.VMEM((chunks, 8, PAIR, rows), F32),
        pltpu.VMEM((chunks, 2, 2, 2, PAIR, hr, latent), BF16),
        pltpu.VMEM((chunks, 2, 2, PAIR, hr, latent), BF16),
        pltpu.VMEM((chunks, 2, hr, latent), BF16),
        pltpu.VMEM((chunks, 2, hr, latent), BF16),
        pltpu.VMEM((chunks, hr, latent), BF16),
        pltpu.VMEM((chunks, hr, latent), BF16),
        pltpu.VMEM((2, PAIR, hr, latent), BF16),
        pltpu.VMEM((heads, latent, vdim), BF16),
        pltpu.VMEM((reqs * verify, heads * vdim), F32),
        pltpu.VMEM((SLOTS, heads * vdim, model // BLOCKS), BF16),
        pltpu.VMEM((model, ff), BF16),
        pltpu.VMEM((model, ff), BF16),
        pltpu.VMEM(router.shape, BF16),
        pltpu.VMEM((4, own_rows, 128), F32),
        pltpu.VMEM((2, 2, 4, own_rows, half), BF16),
        pltpu.VMEM((2, 4, own_rows, half), BF16),
        pltpu.VMEM((2, 4, own_rows, half), BF16),
        pltpu.VMEM((2, 3, own_rows, half), BF16),
        pltpu.VMEM((4, 2, own_rows, half), BF16),
        pltpu.VMEM((2, 4 * own_rows, half), BF16),
        pltpu.VMEM((4 * own_rows, ff), BF16),
        pltpu.VMEM((4 * own_rows, 128), F32),
        pltpu.SemaphoreType.DMA((count,)),
        pltpu.SemaphoreType.DMA((count,)),
        pltpu.SemaphoreType.DMA((2,)),
        pltpu.SemaphoreType.DMA((5 + BLOCKS,)),
        pltpu.SemaphoreType.DMA((SLOTS,)),
    ]
    return pl.pallas_call(
        layer_kernel,
        out_shape=jax.ShapeDtypeStruct((own_rows, half), BF16),
        in_specs=[pl.BlockSpec(memory_space=pltpu.SMEM)] + [anywhere] * 4 + [vmem] * 2
        + [anywhere, vmem] + [anywhere] * 3,
        out_specs=vmem,
        scratch_shapes=scratch,
        compiler_params=pltpu.CompilerParams(
            collective_id=0, has_side_effects=True, vmem_limit_bytes=62 * 1024 * 1024
        ),
        cost_estimate=pl.CostEstimate(
            flops=6_000_000_000, bytes_accessed=64_000_000, transcendentals=2_000_000
        ),
    )(
        context_lengths,
        queries.reshape(chunks, PAIR, hr, width),
        latent_cache.reshape(chunks, PAIR, block_len, width),
        value_up,
        out_proj,
        residual,
        norm_gain.reshape(1, model),
        router,
        routes,
        expert_gate[0],
        expert_up[0],
        expert_down[0],
    )


def solution(mesh):
    grouped = mesh.shape["ctx"] == 2 and mesh.shape["exp"] == 4
    body = fused_on_device if grouped else on_device
    return jax.shard_map(
        body,
        mesh=mesh,
        in_specs=(
            P("req", None, ("ctx", "exp"), None),
            P("req", ("ctx", "exp"), None),
            P("req"),
            P(("ctx", "exp"), None, None),
            P(("ctx", "exp"), None),
            P(("req", "exp"), None),
            P(),
            P(),
            P(("req", "exp"), None),
            P("exp", None, "ctx"),
            P("exp", None, "ctx"),
            P("exp", "ctx", None),
        ),
        out_specs=P(("req", "exp"), "ctx"),
        check_vma=False,
    )
```

```python
import functools
import math

import jax
import jax.numpy as jnp
from jax import lax
from jax.experimental import pallas as pl
from jax.experimental.pallas import tpu as pltpu
from jax.sharding import PartitionSpec as P

route_scale = 2.5


def on_device(
    queries,
    latent_cache,
    context_lengths,
    value_up,
    out_proj,
    residual,
    norm_gain,
    router,
    routes,
    expert_gate,
    expert_up,
    expert_down,
):
    latent_width = value_up.shape[1]
    value_width = value_up.shape[2]
    rope_width = queries.shape[3] - latent_width
    score_scale = 1.0 / math.sqrt(value_width + rope_width)
    heads_here = queries.shape[2]
    block_len = latent_cache.shape[1]
    device = lax.axis_index(("ctx", "exp"))
    all_queries = lax.all_gather(queries, ("ctx", "exp"), axis=2, tiled=True)
    scores = (
        jnp.einsum("rjhd,rtd->rjht", all_queries, latent_cache, preferred_element_type=jnp.float32)
        * score_scale
    )
    positions = device * block_len + jnp.arange(block_len, dtype=jnp.int32)
    visible_upto = context_lengths[:, None] + jnp.arange(2, dtype=jnp.int32)[None, :]
    visible = positions[None, None, None, :] < visible_upto[:, :, None, None]
    masked = jnp.where(visible, scores, -1e30)
    row_max = lax.pmax(jnp.max(masked, axis=-1), ("ctx", "exp"))
    weights = jnp.where(visible, jnp.exp(masked - row_max[..., None]), 0.0)
    weight_sum = jnp.sum(weights, axis=-1)
    latents = latent_cache[:, :, :latent_width]
    weighted = jnp.einsum(
        "rjht,rtl->rjhl", weights.astype(jnp.bfloat16), latents, preferred_element_type=jnp.float32
    )
    summed, sum_all = lax.psum((weighted, weight_sum), ("ctx", "exp"))
    own_weighted = lax.dynamic_slice_in_dim(summed, device * heads_here, heads_here, 2)
    own_sum = lax.dynamic_slice_in_dim(sum_all, device * heads_here, heads_here, 2)
    context = (own_weighted / own_sum[..., None]).astype(jnp.bfloat16)
    head_out = jnp.einsum(
        "rjhl,hlv->rjhv", context, value_up, preferred_element_type=jnp.float32
    ).astype(jnp.bfloat16)
    row_total = head_out.shape[0] * head_out.shape[1]
    head_out = head_out.reshape(row_total, heads_here * value_width)
    own_rows = residual.shape[0]
    owner_index = lax.axis_index("exp")
    attention_all = lax.psum(
        jnp.dot(head_out, out_proj, preferred_element_type=jnp.float32), ("ctx", "exp")
    )
    attention = lax.dynamic_slice_in_dim(attention_all, owner_index * own_rows, own_rows, 0)
    hidden = (residual.astype(jnp.float32) + attention).astype(jnp.bfloat16)
    hidden_wide = hidden.astype(jnp.float32)
    inverse = lax.rsqrt(jnp.mean(hidden_wide * hidden_wide, axis=-1, keepdims=True) + 1e-06)
    normed = (hidden_wide * inverse * norm_gain.astype(jnp.float32)).astype(jnp.bfloat16)
    affinity = jax.nn.sigmoid(jnp.dot(normed, router, preferred_element_type=jnp.float32))
    expert_count = router.shape[1]
    top_count = routes.shape[1]
    capacity = max(2, own_rows * top_count // expert_count)
    chosen = (
        routes[:, :, None] == jnp.arange(expert_count, dtype=jnp.int32)[None, None, :]
    ).astype(jnp.float32)
    picked = jnp.sum(chosen * affinity[:, None, :], axis=-1)
    gate_weights = route_scale * picked / jnp.sum(picked, axis=-1, keepdims=True)
    per_row = jnp.sum(chosen, axis=1)
    earlier = jnp.cumsum(per_row, axis=0) - per_row
    slot_index = jnp.sum(chosen * earlier[:, None, :], axis=-1)
    slot_hot = (
        slot_index[:, :, None] == jnp.arange(capacity, dtype=jnp.float32)[None, None, :]
    ).astype(jnp.float32)
    placement = chosen[:, :, :, None] * slot_hot[:, :, None, :]
    row_place = jnp.sum(placement, axis=1).reshape(own_rows, expert_count * capacity)
    gate_place = jnp.sum(placement * gate_weights[:, :, None, None], axis=1).reshape(
        own_rows, expert_count * capacity
    )
    model_width = normed.shape[1]
    outgoing = jnp.einsum(
        "rs,rd->sd", row_place.astype(jnp.bfloat16), normed, preferred_element_type=jnp.float32
    ).astype(jnp.bfloat16)
    outgoing = outgoing.reshape(expert_count, capacity, model_width)
    arrived = lax.all_to_all(outgoing, "exp", split_axis=0, concat_axis=0, tiled=True)
    gate_part = jnp.einsum(
        "scd,df->scf", arrived, expert_gate[0], preferred_element_type=jnp.float32
    )
    up_part = jnp.einsum("scd,df->scf", arrived, expert_up[0], preferred_element_type=jnp.float32)
    active = (jax.nn.silu(gate_part) * up_part).astype(jnp.bfloat16)
    partial_out = jnp.einsum(
        "scf,fd->scd", active, expert_down[0], preferred_element_type=jnp.float32
    )
    col_width = model_width // lax.axis_size("ctx")
    ctx_index = lax.axis_index("ctx")
    own_cols = lax.dynamic_slice_in_dim(hidden_wide, ctx_index * col_width, col_width, 1)
    full_sum = lax.psum(partial_out.astype(jnp.bfloat16), "ctx").astype(jnp.float32)
    returned = lax.all_to_all(
        full_sum.astype(jnp.bfloat16), "exp", split_axis=0, concat_axis=0, tiled=True
    ).astype(full_sum.dtype)
    returned = lax.dynamic_slice_in_dim(returned, ctx_index * col_width, col_width, 2)
    mixture = jnp.dot(
        gate_place,
        returned.reshape(expert_count * capacity, col_width),
        precision=lax.Precision.HIGHEST,
    )
    return (own_cols + mixture).astype(jnp.bfloat16)


MESH = pl.DeviceIdType.MESH
F32 = jnp.float32
BF16 = jnp.bfloat16
PAIR = 2
SLOTS = 5
BLOCKS = 8
AHEAD = 3


def lay_out(chunks):
    places, count = {}, 0
    for name, number in (
        ("own", 3), ("diag", 2), ("core", 4), ("stat", 7), ("fold", 1), ("cross", 2), ("last", 2),
    ):
        places[name] = (count, number)
        count += number * chunks
    for name, number in (("route", 3), ("swap", 2), ("rows", 6), ("hid", 4), ("hidfwd", 3)):
        places[name] = (count, number)
        count += number
    return places, count


def contract(a, b, da, db):
    return lax.dot_general(a, b, (((da,), (db,)), ((), ())), preferred_element_type=F32)


def layer_kernel(
    lens, q_hbm, cache_hbm, vu_hbm, op_hbm, res, gain, router, routes, eg_hbm, eu_hbm, ed_hbm,
    out,
    qbuf, cbuf, acc, mown, stat, norm, crx, x2, y2, x3, y3, ctx2, vu, ho, wslot, eg, eu,
    chosen, pbuf, prx, tsum, rrx, hid, xn, act, gcol,
    send, recv, csem, wsem, osem,
):
    chunks, _, heads_rows, width = q_hbm.shape
    heads = heads_rows // 2
    block_len, latent = cache_hbm.shape[3], vu.shape[1]
    vdim = vu.shape[2]
    places, _ = lay_out(chunks)
    scale = 1.0 / math.sqrt(vdim + width - latent)
    half = hid.shape[3]
    cols = half * 2 // BLOCKS
    per_half = BLOCKS // 2
    c = lax.axis_index("ctx")
    e = lax.axis_index("exp")
    ey, ex = e // 2, e % 2
    me = c * 4 + e
    ex_n = e + 1 - 2 * ex
    ey_n = e + 2 - 4 * ey
    ed_n = 3 - e
    others = (ex_n, ey_n, ed_n)
    peers = [(1 - c, e)] + [(c, o) for o in others] + [(1 - c, o) for o in others]

    def remote(kind, g, k, src, dst, to):
        first, stride = places[kind]
        place = first + g * stride + k
        return pltpu.make_async_remote_copy(
            src_ref=src, dst_ref=dst, send_sem=send.at[place], recv_sem=recv.at[place],
            device_id={"ctx": to[0], "exp": to[1]}, device_id_type=MESH,
        )

    core_to, x_to, y_to = (1 - c, e), (c, ex_n), (c, ey_n)

    def own_copy(g, k):
        return remote("own", g, k, q_hbm.at[g], qbuf.at[g, me], (core_to, x_to, y_to)[k])

    def diag_copy(g, k):
        source = c * 4 + (ex_n if k == 0 else ey_n)
        view = qbuf.at[g, source, k]
        return remote("diag", g, k, view, view, (y_to, x_to)[k])

    def core_copy(g, k):
        source = c * 4 + (ex_n, ey_n, ed_n, ed_n)[k]
        view = qbuf.at[g, source] if k < 2 else qbuf.at[g, source, k - 2]
        return remote("core", g, k, view, view, core_to)

    def stat_copy(g, k):
        return remote("stat", g, k, stat.at[g, me], stat.at[g, me], peers[k])

    def fold_copy(g):
        return remote("fold", g, 0, norm.at[g, 1 - c], crx.at[g], core_to)

    def cross_copy(g, k):
        if k == 0:
            return remote("cross", g, 0, crx.at[g, :, 1 - ex, 0], x2.at[g], x_to)
        return remote("cross", g, 1, crx.at[g, 1 - ey, :, 1], y2.at[g], y_to)

    def last_copy(g, k):
        if k == 0:
            return remote("last", g, 0, x2.at[g, 1 - ey], y3.at[g], y_to)
        return remote("last", g, 1, y2.at[g, 1 - ex], x3.at[g], x_to)

    def route_copy(k):
        return remote("route", 0, k, chosen.at[e], chosen.at[e], (c, others[k]))

    def swap_copy(p):
        return remote("swap", 0, p, pbuf.at[p, 0], prx.at[p], core_to)

    def rows_copy(p, k):
        return remote("rows", 0, p * 3 + k, tsum.at[p, others[k]], rrx.at[p, k], (c, others[k]))

    def hid_copy(k):
        to = (x_to, y_to, (c, ed_n), core_to)[k]
        return remote("hid", 0, k, hid.at[e, c], hid.at[e, c], to)

    def hidfwd_copy(k):
        view = hid.at[others[k], c]
        return remote("hidfwd", 0, k, view, view, core_to)

    def cache_copy(g):
        return pltpu.make_async_copy(cache_hbm.at[g], cbuf.at[g % 2], csem.at[g % 2])

    def column(i):
        side = jnp.where(i < per_half, 1 - c, c)
        return pl.multiple_of((side * per_half + i % per_half) * cols, cols)

    def op_copy(i):
        return pltpu.make_async_copy(
            op_hbm.at[:, pl.ds(column(i), cols)], wslot.at[i % SLOTS], osem.at[i % SLOTS]
        )

    depth = ed_hbm.shape[0]

    def down_copy(i):
        place = pl.ds(pl.multiple_of((i % 4) * depth, depth), depth)
        return pltpu.make_async_copy(
            ed_hbm.at[:, pl.ds(column(i), cols)], wslot.at[3 + i // 4, place], wsem.at[4 + i]
        )

    own_q = pltpu.make_async_copy(q_hbm, qbuf.at[:, me], wsem.at[0])
    vu_copy = pltpu.make_async_copy(vu_hbm, vu, wsem.at[1])
    eg_copy = pltpu.make_async_copy(eg_hbm, eg, wsem.at[2])
    eu_copy = pltpu.make_async_copy(eu_hbm, eu, wsem.at[3])

    own_q.start()
    cache_copy(0).start()
    lanes = lax.broadcasted_iota(jnp.int32, chosen.shape[1:], 1)
    square = (routes.shape[1], routes.shape[1])
    diagonal = lax.broadcasted_iota(jnp.int32, square, 0) == lax.broadcasted_iota(jnp.int32, square, 1)
    named = jnp.zeros(lanes.shape, F32)
    for k in range(routes.shape[0]):
        choice = jnp.where(diagonal, routes[k : k + 1, :].astype(F32), 0.0)
        named = named + (jnp.sum(choice, axis=1, keepdims=True) == lanes.astype(F32)).astype(F32)
    chosen[e] = named

    barrier = pltpu.get_barrier_semaphore()
    for to in peers:
        pl.semaphore_signal(
            barrier, inc=1, device_id={"ctx": to[0], "exp": to[1]}, device_id_type=MESH
        )
    pl.semaphore_wait(barrier, len(peers))

    for g in range(AHEAD):
        for k in range(3):
            own_copy(g, k).start()
    for k in range(3):
        route_copy(k).start()
    vu_copy.start()
    own_q.wait()

    rows = 8 * heads_rows

    def attend(g):
        cache_copy(g).wait()

        @pl.when(g + 1 < chunks)
        def _():
            cache_copy(g + 1).start()

        for r in range(PAIR):
            q = qbuf[g, :, r].reshape(rows, width)
            keys = cbuf[g % 2, r]
            s = jnp.dot(q, keys, preferred_element_type=F32) * scale
            position = me * block_len + lax.broadcasted_iota(jnp.int32, s.shape, 1)
            later = lax.broadcasted_iota(jnp.int32, s.shape, 0) // heads % 2
            visible = position < lens[g * PAIR + r] + later
            s = jnp.where(visible, s, -1e30)
            m = jnp.max(s, axis=1, keepdims=True)
            p = jnp.where(visible, jnp.exp(s - m), 0.0)
            total = jnp.sum(p, axis=1, keepdims=True)
            acc[g % 2, r] = contract(p.astype(BF16), keys[:latent], 1, 1)
            z = jnp.where(total > 0.0, m + jnp.log(jnp.maximum(total, 1e-30)), -1e30)
            first = lax.broadcasted_iota(jnp.int32, (rows, 128), 1) < 64
            flat = jnp.transpose(jnp.where(first, m, z))
            mown[g % 2, r : r + 1] = flat[0:1]
            stat[g, me, r : r + 1] = flat[64:65]
        for k in range(7):
            stat_copy(g, k).start()

    def normalise(g):
        for k in range(7):
            stat_copy(g, k).wait_recv()
        for r in range(PAIR):
            z = stat[g, :, r]
            top = jnp.max(z, axis=0, keepdims=True)
            whole = top + jnp.log(jnp.sum(jnp.exp(z - top), axis=0, keepdims=True))
            factor = jnp.exp(mown[g % 2, r : r + 1] - whole)
            factor = jnp.transpose(jnp.broadcast_to(factor, (128, rows)))
            for k in range(latent // 128):
                part = acc[g % 2, r, :, k * 128 : (k + 1) * 128] * factor
                norm[g, :, :, :, r, :, k * 128 : (k + 1) * 128] = part.astype(BF16).reshape(
                    2, 2, 2, heads_rows, 128
                )
        fold_copy(g).start()

    def fold(g):
        fold_copy(g).wait_recv()
        crx[g] = (crx[g].astype(F32) + norm[g, c].astype(F32)).astype(BF16)
        cross_copy(g, 0).start()
        cross_copy(g, 1).start()

    def cross(g):
        cross_copy(g, 0).wait_recv()
        x2[g] = (x2[g].astype(F32) + crx[g, :, ex, 0].astype(F32)).astype(BF16)
        last_copy(g, 0).start()
        cross_copy(g, 1).wait_recv()
        y2[g] = (y2[g].astype(F32) + crx[g, ey, :, 1].astype(F32)).astype(BF16)
        last_copy(g, 1).start()

    def last(g):
        last_copy(g, 0).wait_recv()
        ctx2[g % 2, 0] = (x2[g, ey].astype(F32) + y3[g].astype(F32)).astype(BF16)
        last_copy(g, 1).wait_recv()
        ctx2[g % 2, 1] = (y2[g, ex].astype(F32) + x3[g].astype(F32)).astype(BF16)

        @pl.when(g % 2 == 1)
        def _():
            both = ctx2[...].reshape(4 * heads_rows, latent)
            for h in range(heads):
                every = jnp.dot(both, vu[h], preferred_element_type=F32).reshape(8, heads, vdim)
                mine = lax.broadcasted_iota(jnp.int32, every.shape, 1) == h
                place = pl.ds(pl.multiple_of((g // 2) * 8, 8), 8)
                ho[place, h * vdim : (h + 1) * vdim] = jnp.sum(
                    jnp.where(mine, every, 0.0), axis=1
                )

    vu_copy.wait()

    def step(s, _):
        def at(lag, run):
            @pl.when((s >= lag) & (s < chunks + lag))
            def _():
                run(s - lag)

        @pl.when(s + AHEAD < chunks)
        def _():
            for k in range(3):
                own_copy(s + AHEAD, k).start()

        def forward(g):
            own_copy(g, 1).wait_recv()
            diag_copy(g, 0).start()
            core_copy(g, 0).start()
            own_copy(g, 2).wait_recv()
            diag_copy(g, 1).start()
            core_copy(g, 1).start()

        def forward_diag(g):
            for k in range(2):
                diag_copy(g, k).wait_recv()
                core_copy(g, 2 + k).start()

        def attend_when_here(g):
            own_copy(g, 0).wait_recv()
            for k in range(4):
                core_copy(g, k).wait_recv()
            attend(g)

        at(0, forward)
        at(1, forward_diag)
        at(3, normalise)
        at(4, fold)
        at(5, cross)
        at(6, last)
        at(2, attend_when_here)

        @pl.when(s < SLOTS)
        def _():
            op_copy(s).start()

        @pl.when(s == SLOTS)
        def _():
            eg_copy.start()

        @pl.when(s == SLOTS + 1)
        def _():
            eu_copy.start()

        return 0

    lax.fori_loop(0, chunks + 6, step, 0)

    own_rows = res.shape[0]

    def project(i, _):
        op_copy(i).wait()
        part = jnp.dot(ho[...].astype(BF16), wslot[i % SLOTS], preferred_element_type=F32)
        place = pl.ds(pl.multiple_of((i % per_half) * cols, cols), cols)
        pbuf[0, i // per_half, :, :, place] = part.astype(BF16).reshape(4, own_rows, cols)

        @pl.when(i + SLOTS < BLOCKS)
        def _():
            op_copy(i + SLOTS).start()

        @pl.when(i == per_half - 1)
        def _():
            swap_copy(0).start()

        return 0

    lax.fori_loop(0, BLOCKS, project, 0)
    for i in range(BLOCKS):
        down_copy(i).start()

    def reduce_rows(p):
        swap_copy(p).wait_recv()
        tsum[p] = (prx[p].astype(F32) + pbuf[p, 1].astype(F32)).astype(BF16)
        for k in (2, 0, 1):
            rows_copy(p, k).start()
        total = tsum[p, e].astype(F32)
        for k in range(3):
            rows_copy(p, k).wait_recv()
            total = total + rrx[p, k].astype(F32)
        return total

    own_cols = pl.ds(pl.multiple_of(c * half, half), half)
    hid[e, c] = (res[:, own_cols].astype(F32) + reduce_rows(0)).astype(BF16)
    for k in (2, 0, 1, 3):
        hid_copy(k).start()
    for k in range(3):
        hid_copy(k).wait_recv()
        hidfwd_copy(k).start()
    hid_copy(3).wait_recv()
    for k in range(3):
        hidfwd_copy(k).wait_recv()
        route_copy(k).wait_recv()
    eg_copy.wait()
    eu_copy.wait()

    sides = [hid[:, side].astype(F32).reshape(4 * own_rows, half) for side in range(2)]
    squares = sum(jnp.sum(v * v, axis=-1, keepdims=True) for v in sides)
    inverse = lax.rsqrt(squares / (2 * half) + 1e-06)
    for side in range(2):
        for k in range(half // 128):
            spread = gain[side * (half // 128) + k : side * (half // 128) + k + 1, :].astype(F32)
            piece = sides[side][:, k * 128 : (k + 1) * 128]
            xn[side, :, k * 128 : (k + 1) * 128] = (piece * inverse * spread).astype(BF16)
    span = [slice(side * half, (side + 1) * half) for side in range(2)]
    both_sides = lambda w: sum(
        jnp.dot(xn[side], w[span[side], :], preferred_element_type=F32) for side in range(2)
    )
    affinity = jax.nn.sigmoid(
        sum(contract(xn[side], router[:, span[side]], 1, 1) for side in range(2))
    )
    picked = affinity * chosen[...].reshape(4 * own_rows, 128)[:, : affinity.shape[1]]
    weights = route_scale * picked / jnp.sum(picked, axis=-1, keepdims=True)
    mine = lax.broadcasted_iota(jnp.int32, weights.shape, 1) == e
    gcol[...] = jnp.broadcast_to(
        jnp.sum(jnp.where(mine, weights, 0.0), axis=-1, keepdims=True), gcol.shape
    )
    gate_part = both_sides(eg)
    up_part = both_sides(eu)
    act[...] = (gate_part / (1.0 + jnp.exp(-gate_part)) * up_part).astype(BF16)

    for i in range(BLOCKS):
        down_copy(i).wait()
        block = wslot[3 + i // 4, (i % 4) * depth : (i % 4 + 1) * depth]
        part = jnp.dot(act[...], block, preferred_element_type=F32) * gcol[:, 0:1]
        place = slice((i % per_half) * cols, (i % per_half + 1) * cols)
        pbuf[1, i // per_half, :, :, place] = part.astype(BF16).reshape(4, own_rows, cols)
        if i == per_half - 1:
            swap_copy(1).start()
    out[...] = (hid[e, c].astype(F32) + reduce_rows(1)).astype(BF16)

    def drain(g, _):
        for k in range(3):
            own_copy(g, k).wait_send()
        for k in range(2):
            diag_copy(g, k).wait_send()
            cross_copy(g, k).wait_send()
            last_copy(g, k).wait_send()
        for k in range(4):
            core_copy(g, k).wait_send()
        for k in range(7):
            stat_copy(g, k).wait_send()
        fold_copy(g).wait_send()
        return 0

    lax.fori_loop(0, chunks, drain, 0)
    for k in range(3):
        route_copy(k).wait_send()
        hidfwd_copy(k).wait_send()
        rows_copy(0, k).wait_send()
        rows_copy(1, k).wait_send()
    for k in range(4):
        hid_copy(k).wait_send()
    for p in range(2):
        swap_copy(p).wait_send()


def fused_on_device(
    queries, latent_cache, context_lengths, value_up, out_proj, residual, norm_gain, router,
    routes, expert_gate, expert_up, expert_down,
):
    reqs, verify, heads, width = queries.shape
    chunks = reqs // PAIR
    hr = verify * heads
    _, block_len, _ = latent_cache.shape
    _, latent, vdim = value_up.shape
    own_rows, model = residual.shape
    half = model // 2
    ff = expert_down.shape[1]
    rows = 8 * hr
    _, count = lay_out(chunks)
    vmem, anywhere = pl.BlockSpec(memory_space=pltpu.VMEM), pl.BlockSpec(memory_space=pl.ANY)
    scratch = [
        pltpu.VMEM((chunks, 8, PAIR, hr, width), BF16),
        pltpu.VMEM((2, PAIR, width, block_len), BF16),
        pltpu.VMEM((2, PAIR, rows, latent), F32),
        pltpu.VMEM((2, PAIR, rows), F32),
        pltpu.VMEM((chunks, 8, PAIR, rows), F32),
        pltpu.VMEM((chunks, 2, 2, 2, PAIR, hr, latent), BF16),
        pltpu.VMEM((chunks, 2, 2, PAIR, hr, latent), BF16),
        pltpu.VMEM((chunks, 2, hr, latent), BF16),
        pltpu.VMEM((chunks, 2, hr, latent), BF16),
        pltpu.VMEM((chunks, hr, latent), BF16),
        pltpu.VMEM((chunks, hr, latent), BF16),
        pltpu.VMEM((2, PAIR, hr, latent), BF16),
        pltpu.VMEM((heads, latent, vdim), BF16),
        pltpu.VMEM((reqs * verify, heads * vdim), F32),
        pltpu.VMEM((SLOTS, heads * vdim, model // BLOCKS), BF16),
        pltpu.VMEM((model, ff), BF16),
        pltpu.VMEM((model, ff), BF16),
        pltpu.VMEM((4, own_rows, 128), F32),
        pltpu.VMEM((2, 2, 4, own_rows, half), BF16),
        pltpu.VMEM((2, 4, own_rows, half), BF16),
        pltpu.VMEM((2, 4, own_rows, half), BF16),
        pltpu.VMEM((2, 3, own_rows, half), BF16),
        pltpu.VMEM((4, 2, own_rows, half), BF16),
        pltpu.VMEM((2, 4 * own_rows, half), BF16),
        pltpu.VMEM((4 * own_rows, ff), BF16),
        pltpu.VMEM((4 * own_rows, 128), F32),
        pltpu.SemaphoreType.DMA((count,)),
        pltpu.SemaphoreType.DMA((count,)),
        pltpu.SemaphoreType.DMA((2,)),
        pltpu.SemaphoreType.DMA((4 + BLOCKS,)),
        pltpu.SemaphoreType.DMA((SLOTS,)),
    ]
    return pl.pallas_call(
        layer_kernel,
        out_shape=jax.ShapeDtypeStruct((own_rows, half), BF16),
        in_specs=[pl.BlockSpec(memory_space=pltpu.SMEM)] + [anywhere] * 4 + [vmem] * 2
        + [vmem] * 2 + [anywhere] * 3,
        out_specs=vmem,
        scratch_shapes=scratch,
        compiler_params=pltpu.CompilerParams(
            collective_id=0, has_side_effects=True, vmem_limit_bytes=62 * 1024 * 1024
        ),
        cost_estimate=pl.CostEstimate(
            flops=6_000_000_000, bytes_accessed=64_000_000, transcendentals=2_000_000
        ),
    )(
        context_lengths,
        queries.reshape(chunks, PAIR, hr, width),
        jnp.swapaxes(latent_cache, 1, 2).reshape(chunks, PAIR, width, block_len),
        value_up,
        out_proj,
        residual,
        norm_gain.reshape(model // 128, 128),
        router.T,
        routes.T,
        expert_gate[0],
        expert_up[0],
        expert_down[0],
    )


def solution(mesh):
    grouped = mesh.shape["ctx"] == 2 and mesh.shape["exp"] == 4
    body = fused_on_device if grouped else on_device
    return jax.shard_map(
        body,
        mesh=mesh,
        in_specs=(
            P("req", None, ("ctx", "exp"), None),
            P("req", ("ctx", "exp"), None),
            P("req"),
            P(("ctx", "exp"), None, None),
            P(("ctx", "exp"), None),
            P(("req", "exp"), None),
            P(),
            P(),
            P(("req", "exp"), None),
            P("exp", None, "ctx"),
            P("exp", None, "ctx"),
            P("exp", "ctx", None),
        ),
        out_specs=P(("req", "exp"), "ctx"),
        check_vma=False,
    )
```

```python
import functools
import math

import jax
import jax.numpy as jnp
from jax import lax
from jax.experimental import pallas as pl
from jax.experimental.pallas import tpu as pltpu
from jax.sharding import PartitionSpec as P

route_scale = 2.5


def on_device(
    queries,
    latent_cache,
    context_lengths,
    value_up,
    out_proj,
    residual,
    norm_gain,
    router,
    routes,
    expert_gate,
    expert_up,
    expert_down,
):
    latent_width = value_up.shape[1]
    value_width = value_up.shape[2]
    rope_width = queries.shape[3] - latent_width
    score_scale = 1.0 / math.sqrt(value_width + rope_width)
    heads_here = queries.shape[2]
    block_len = latent_cache.shape[1]
    device = lax.axis_index(("ctx", "exp"))
    all_queries = lax.all_gather(queries, ("ctx", "exp"), axis=2, tiled=True)
    scores = (
        jnp.einsum("rjhd,rtd->rjht", all_queries, latent_cache, preferred_element_type=jnp.float32)
        * score_scale
    )
    positions = device * block_len + jnp.arange(block_len, dtype=jnp.int32)
    visible_upto = context_lengths[:, None] + jnp.arange(2, dtype=jnp.int32)[None, :]
    visible = positions[None, None, None, :] < visible_upto[:, :, None, None]
    masked = jnp.where(visible, scores, -1e30)
    row_max = lax.pmax(jnp.max(masked, axis=-1), ("ctx", "exp"))
    weights = jnp.where(visible, jnp.exp(masked - row_max[..., None]), 0.0)
    weight_sum = jnp.sum(weights, axis=-1)
    latents = latent_cache[:, :, :latent_width]
    weighted = jnp.einsum(
        "rjht,rtl->rjhl", weights.astype(jnp.bfloat16), latents, preferred_element_type=jnp.float32
    )
    summed, sum_all = lax.psum((weighted, weight_sum), ("ctx", "exp"))
    own_weighted = lax.dynamic_slice_in_dim(summed, device * heads_here, heads_here, 2)
    own_sum = lax.dynamic_slice_in_dim(sum_all, device * heads_here, heads_here, 2)
    context = (own_weighted / own_sum[..., None]).astype(jnp.bfloat16)
    head_out = jnp.einsum(
        "rjhl,hlv->rjhv", context, value_up, preferred_element_type=jnp.float32
    ).astype(jnp.bfloat16)
    row_total = head_out.shape[0] * head_out.shape[1]
    head_out = head_out.reshape(row_total, heads_here * value_width)
    own_rows = residual.shape[0]
    owner_index = lax.axis_index("exp")
    attention_all = lax.psum(
        jnp.dot(head_out, out_proj, preferred_element_type=jnp.float32), ("ctx", "exp")
    )
    attention = lax.dynamic_slice_in_dim(attention_all, owner_index * own_rows, own_rows, 0)
    hidden = (residual.astype(jnp.float32) + attention).astype(jnp.bfloat16)
    hidden_wide = hidden.astype(jnp.float32)
    inverse = lax.rsqrt(jnp.mean(hidden_wide * hidden_wide, axis=-1, keepdims=True) + 1e-06)
    normed = (hidden_wide * inverse * norm_gain.astype(jnp.float32)).astype(jnp.bfloat16)
    affinity = jax.nn.sigmoid(jnp.dot(normed, router, preferred_element_type=jnp.float32))
    expert_count = router.shape[1]
    top_count = routes.shape[1]
    capacity = max(2, own_rows * top_count // expert_count)
    chosen = (
        routes[:, :, None] == jnp.arange(expert_count, dtype=jnp.int32)[None, None, :]
    ).astype(jnp.float32)
    picked = jnp.sum(chosen * affinity[:, None, :], axis=-1)
    gate_weights = route_scale * picked / jnp.sum(picked, axis=-1, keepdims=True)
    per_row = jnp.sum(chosen, axis=1)
    earlier = jnp.cumsum(per_row, axis=0) - per_row
    slot_index = jnp.sum(chosen * earlier[:, None, :], axis=-1)
    slot_hot = (
        slot_index[:, :, None] == jnp.arange(capacity, dtype=jnp.float32)[None, None, :]
    ).astype(jnp.float32)
    placement = chosen[:, :, :, None] * slot_hot[:, :, None, :]
    row_place = jnp.sum(placement, axis=1).reshape(own_rows, expert_count * capacity)
    gate_place = jnp.sum(placement * gate_weights[:, :, None, None], axis=1).reshape(
        own_rows, expert_count * capacity
    )
    model_width = normed.shape[1]
    outgoing = jnp.einsum(
        "rs,rd->sd", row_place.astype(jnp.bfloat16), normed, preferred_element_type=jnp.float32
    ).astype(jnp.bfloat16)
    outgoing = outgoing.reshape(expert_count, capacity, model_width)
    arrived = lax.all_to_all(outgoing, "exp", split_axis=0, concat_axis=0, tiled=True)
    gate_part = jnp.einsum(
        "scd,df->scf", arrived, expert_gate[0], preferred_element_type=jnp.float32
    )
    up_part = jnp.einsum("scd,df->scf", arrived, expert_up[0], preferred_element_type=jnp.float32)
    active = (jax.nn.silu(gate_part) * up_part).astype(jnp.bfloat16)
    partial_out = jnp.einsum(
        "scf,fd->scd", active, expert_down[0], preferred_element_type=jnp.float32
    )
    col_width = model_width // lax.axis_size("ctx")
    ctx_index = lax.axis_index("ctx")
    own_cols = lax.dynamic_slice_in_dim(hidden_wide, ctx_index * col_width, col_width, 1)
    full_sum = lax.psum(partial_out.astype(jnp.bfloat16), "ctx").astype(jnp.float32)
    returned = lax.all_to_all(
        full_sum.astype(jnp.bfloat16), "exp", split_axis=0, concat_axis=0, tiled=True
    ).astype(full_sum.dtype)
    returned = lax.dynamic_slice_in_dim(returned, ctx_index * col_width, col_width, 2)
    mixture = jnp.dot(
        gate_place,
        returned.reshape(expert_count * capacity, col_width),
        precision=lax.Precision.HIGHEST,
    )
    return (own_cols + mixture).astype(jnp.bfloat16)


MESH = pl.DeviceIdType.MESH
F32 = jnp.float32
BF16 = jnp.bfloat16
PAIR = 2
SLOTS = 5
BLOCKS = 8
AHEAD = 3


def lay_out(chunks):
    places, count = {}, 0
    for name, number in (
        ("own", 3), ("diag", 2), ("core", 4), ("stat", 7), ("fold", 1), ("cross", 2), ("last", 2),
    ):
        places[name] = (count, number)
        count += number * chunks
    for name, number in (("route", 3), ("swap", 2), ("rows", 6), ("hid", 4), ("hidfwd", 3)):
        places[name] = (count, number)
        count += number
    return places, count


def contract(a, b, da, db):
    return lax.dot_general(a, b, (((da,), (db,)), ((), ())), preferred_element_type=F32)


def layer_kernel(
    lens, q_hbm, cache_hbm, vu_hbm, op_hbm, res, gain, router, routes, eg_hbm, eu_hbm, ed_hbm,
    out,
    qbuf, cbuf, acc, mown, stat, norm, crx, x2, y2, x3, y3, ctx2, vu, ho, wslot, eg, eu,
    sbuf, wbuf, mz, chosen, pbuf, prx, tsum, rrx, hid, xn, act, gcol,
    send, recv, csem, wsem, osem,
):
    chunks, _, heads_rows, width = q_hbm.shape
    heads = heads_rows // 2
    block_len, latent = cache_hbm.shape[3], vu.shape[1]
    vdim = vu.shape[2]
    places, _ = lay_out(chunks)
    scale = 1.0 / math.sqrt(vdim + width - latent)
    half = hid.shape[3]
    cols = half * 2 // BLOCKS
    per_half = BLOCKS // 2
    c = lax.axis_index("ctx")
    e = lax.axis_index("exp")
    ey, ex = e // 2, e % 2
    me = c * 4 + e
    ex_n = e + 1 - 2 * ex
    ey_n = e + 2 - 4 * ey
    ed_n = 3 - e
    others = (ex_n, ey_n, ed_n)
    peers = [(1 - c, e)] + [(c, o) for o in others] + [(1 - c, o) for o in others]

    def remote(kind, g, k, src, dst, to):
        first, stride = places[kind]
        place = first + g * stride + k
        return pltpu.make_async_remote_copy(
            src_ref=src, dst_ref=dst, send_sem=send.at[place], recv_sem=recv.at[place],
            device_id={"ctx": to[0], "exp": to[1]}, device_id_type=MESH,
        )

    core_to, x_to, y_to = (1 - c, e), (c, ex_n), (c, ey_n)

    def own_copy(g, k):
        return remote("own", g, k, q_hbm.at[g], qbuf.at[g, me], (core_to, x_to, y_to)[k])

    def diag_copy(g, k):
        source = c * 4 + (ex_n if k == 0 else ey_n)
        view = qbuf.at[g, source, k]
        return remote("diag", g, k, view, view, (y_to, x_to)[k])

    def core_copy(g, k):
        source = c * 4 + (ex_n, ey_n, ed_n, ed_n)[k]
        view = qbuf.at[g, source] if k < 2 else qbuf.at[g, source, k - 2]
        return remote("core", g, k, view, view, core_to)

    def stat_copy(g, k):
        return remote("stat", g, k, stat.at[g, me], stat.at[g, me], peers[k])

    def fold_copy(g):
        return remote("fold", g, 0, norm.at[g, 1 - c], crx.at[g], core_to)

    def cross_copy(g, k):
        if k == 0:
            return remote("cross", g, 0, crx.at[g, :, 1 - ex, 0], x2.at[g], x_to)
        return remote("cross", g, 1, crx.at[g, 1 - ey, :, 1], y2.at[g], y_to)

    def last_copy(g, k):
        if k == 0:
            return remote("last", g, 0, x2.at[g, 1 - ey], y3.at[g], y_to)
        return remote("last", g, 1, y2.at[g, 1 - ex], x3.at[g], x_to)

    def route_copy(k):
        return remote("route", 0, k, chosen.at[e], chosen.at[e], (c, others[k]))

    def swap_copy(p):
        return remote("swap", 0, p, pbuf.at[p, 0], prx.at[p], core_to)

    def rows_copy(p, k):
        return remote("rows", 0, p * 3 + k, tsum.at[p, others[k]], rrx.at[p, k], (c, others[k]))

    def hid_copy(k):
        to = (x_to, y_to, (c, ed_n), core_to)[k]
        return remote("hid", 0, k, hid.at[e, c], hid.at[e, c], to)

    def hidfwd_copy(k):
        view = hid.at[others[k], c]
        return remote("hidfwd", 0, k, view, view, core_to)

    def cache_copy(g):
        return pltpu.make_async_copy(cache_hbm.at[g], cbuf.at[g % 2], csem.at[g % 2])

    def column(i):
        side = jnp.where(i < per_half, 1 - c, c)
        return pl.multiple_of((side * per_half + i % per_half) * cols, cols)

    def op_copy(i):
        return pltpu.make_async_copy(
            op_hbm.at[:, pl.ds(column(i), cols)], wslot.at[i % SLOTS], osem.at[i % SLOTS]
        )

    depth = ed_hbm.shape[0]

    def down_copy(i):
        place = pl.ds(pl.multiple_of((i % 4) * depth, depth), depth)
        return pltpu.make_async_copy(
            ed_hbm.at[:, pl.ds(column(i), cols)], wslot.at[3 + i // 4, place], wsem.at[4 + i]
        )

    own_q = pltpu.make_async_copy(q_hbm, qbuf.at[:, me], wsem.at[0])
    vu_copy = pltpu.make_async_copy(vu_hbm, vu, wsem.at[1])
    eg_copy = pltpu.make_async_copy(eg_hbm, eg, wsem.at[2])
    eu_copy = pltpu.make_async_copy(eu_hbm, eu, wsem.at[3])

    own_q.start()
    cache_copy(0).start()
    lanes = lax.broadcasted_iota(jnp.int32, chosen.shape[1:], 1)
    square = (routes.shape[1], routes.shape[1])
    diagonal = lax.broadcasted_iota(jnp.int32, square, 0) == lax.broadcasted_iota(jnp.int32, square, 1)
    named = jnp.zeros(lanes.shape, F32)
    for k in range(routes.shape[0]):
        choice = jnp.where(diagonal, routes[k : k + 1, :].astype(F32), 0.0)
        named = named + (jnp.sum(choice, axis=1, keepdims=True) == lanes.astype(F32)).astype(F32)
    chosen[e] = named

    barrier = pltpu.get_barrier_semaphore()
    for to in peers:
        pl.semaphore_signal(
            barrier, inc=1, device_id={"ctx": to[0], "exp": to[1]}, device_id_type=MESH
        )
    pl.semaphore_wait(barrier, len(peers))

    for g in range(AHEAD):
        for k in range(3):
            own_copy(g, k).start()
    for k in range(3):
        route_copy(k).start()
    vu_copy.start()
    own_q.wait()

    rows = 8 * heads_rows

    def attend(g):
        cache_copy(g).wait()

        @pl.when(g + 1 < chunks)
        def _():
            cache_copy(g + 1).start()

        first = lax.broadcasted_iota(jnp.int32, (heads_rows, 128), 1) < 64
        position = me * block_len + lax.broadcasted_iota(jnp.int32, (1, block_len), 1)
        for r in range(PAIR):
            q = qbuf[g, :, r].reshape(rows, width)
            sbuf[r] = jnp.dot(q, cbuf[g % 2, r], preferred_element_type=F32)
        for r in range(PAIR):
            length = lens[g * PAIR + r]
            bias = jnp.concatenate(
                [
                    jnp.broadcast_to(
                        jnp.where(position < length + j, 0.0, -1e30), (heads, block_len)
                    )
                    for j in range(2)
                ],
                axis=0,
            )
            for d in range(8):
                place = slice(d * heads_rows, (d + 1) * heads_rows)
                s = sbuf[r, place] + bias
                m = jnp.max(s, axis=1, keepdims=True)
                p = jnp.exp((s - m) * scale)
                total = jnp.sum(p, axis=1, keepdims=True)
                wbuf[r, place] = p.astype(BF16)
                m = m * scale
                z = jnp.where(m > -1e25, m + jnp.log(total), -1e30)
                mz[r, place] = jnp.where(first, jnp.where(m > -1e25, m, -1e30), z)
            acc[g % 2, r] = contract(wbuf[r], cbuf[g % 2, r, :latent], 1, 1)
            flat = jnp.transpose(mz[r])
            mown[g % 2, r : r + 1] = flat[0:1]
            stat[g, me, r : r + 1] = flat[64:65]
        for k in range(7):
            stat_copy(g, k).start()

    def normalise(g):
        for k in range(7):
            stat_copy(g, k).wait_recv()
        for r in range(PAIR):
            z = stat[g, :, r]
            top = jnp.max(z, axis=0, keepdims=True)
            whole = top + jnp.log(jnp.sum(jnp.exp(z - top), axis=0, keepdims=True))
            factor = jnp.exp(mown[g % 2, r : r + 1] - whole)
            factor = jnp.transpose(jnp.broadcast_to(factor, (128, rows)))
            for k in range(latent // 128):
                part = acc[g % 2, r, :, k * 128 : (k + 1) * 128] * factor
                norm[g, :, :, :, r, :, k * 128 : (k + 1) * 128] = part.astype(BF16).reshape(
                    2, 2, 2, heads_rows, 128
                )
        fold_copy(g).start()

    def fold(g):
        fold_copy(g).wait_recv()
        crx[g] = (crx[g].astype(F32) + norm[g, c].astype(F32)).astype(BF16)
        cross_copy(g, 0).start()
        cross_copy(g, 1).start()

    def cross(g):
        cross_copy(g, 0).wait_recv()
        x2[g] = (x2[g].astype(F32) + crx[g, :, ex, 0].astype(F32)).astype(BF16)
        last_copy(g, 0).start()
        cross_copy(g, 1).wait_recv()
        y2[g] = (y2[g].astype(F32) + crx[g, ey, :, 1].astype(F32)).astype(BF16)
        last_copy(g, 1).start()

    def last(g):
        last_copy(g, 0).wait_recv()
        ctx2[g % 2, 0] = (x2[g, ey].astype(F32) + y3[g].astype(F32)).astype(BF16)
        last_copy(g, 1).wait_recv()
        ctx2[g % 2, 1] = (y2[g, ex].astype(F32) + x3[g].astype(F32)).astype(BF16)

        @pl.when(g % 2 == 1)
        def _():
            both = ctx2[...].reshape(4 * heads_rows, latent)
            for h in range(heads):
                every = jnp.dot(both, vu[h], preferred_element_type=F32).reshape(8, heads, vdim)
                mine = lax.broadcasted_iota(jnp.int32, every.shape, 1) == h
                place = pl.ds(pl.multiple_of((g // 2) * 8, 8), 8)
                ho[place, h * vdim : (h + 1) * vdim] = jnp.sum(
                    jnp.where(mine, every, 0.0), axis=1
                )

    vu_copy.wait()

    def step(s, _):
        def at(lag, run):
            @pl.when((s >= lag) & (s < chunks + lag))
            def _():
                run(s - lag)

        def forward(g):
            own_copy(g, 1).wait_recv()
            diag_copy(g, 0).start()
            core_copy(g, 0).start()
            own_copy(g, 2).wait_recv()
            diag_copy(g, 1).start()
            core_copy(g, 1).start()

        def forward_diag(g):
            for k in range(2):
                diag_copy(g, k).wait_recv()
                core_copy(g, 2 + k).start()

        def attend_when_here(g):
            own_copy(g, 0).wait_recv()
            for k in range(4):
                core_copy(g, k).wait_recv()
            attend(g)

        at(0, forward)
        at(1, forward_diag)

        @pl.when(s + AHEAD < chunks)
        def _():
            for k in range(3):
                own_copy(s + AHEAD, k).start()

        at(3, normalise)
        at(4, fold)
        at(5, cross)
        at(6, last)
        at(2, attend_when_here)

        @pl.when(s < SLOTS)
        def _():
            op_copy(s).start()

        @pl.when(s == SLOTS)
        def _():
            eg_copy.start()

        @pl.when(s == SLOTS + 1)
        def _():
            eu_copy.start()

        return 0

    lax.fori_loop(0, chunks + 6, step, 0)

    own_rows = res.shape[0]

    def project(i, _):
        op_copy(i).wait()
        part = jnp.dot(ho[...].astype(BF16), wslot[i % SLOTS], preferred_element_type=F32)
        place = pl.ds(pl.multiple_of((i % per_half) * cols, cols), cols)
        pbuf[0, i // per_half, :, :, place] = part.astype(BF16).reshape(4, own_rows, cols)

        @pl.when(i + SLOTS < BLOCKS)
        def _():
            op_copy(i + SLOTS).start()

        @pl.when(i == per_half - 1)
        def _():
            swap_copy(0).start()

        return 0

    lax.fori_loop(0, BLOCKS, project, 0)
    for i in range(BLOCKS):
        down_copy(i).start()

    def reduce_rows(p):
        swap_copy(p).wait_recv()
        tsum[p] = (prx[p].astype(F32) + pbuf[p, 1].astype(F32)).astype(BF16)
        for k in (2, 0, 1):
            rows_copy(p, k).start()
        total = tsum[p, e].astype(F32)
        for k in range(3):
            rows_copy(p, k).wait_recv()
            total = total + rrx[p, k].astype(F32)
        return total

    own_cols = pl.ds(pl.multiple_of(c * half, half), half)
    hid[e, c] = (res[:, own_cols].astype(F32) + reduce_rows(0)).astype(BF16)
    for k in (2, 0, 1, 3):
        hid_copy(k).start()
    for k in range(3):
        hid_copy(k).wait_recv()
        hidfwd_copy(k).start()
    hid_copy(3).wait_recv()
    for k in range(3):
        hidfwd_copy(k).wait_recv()
        route_copy(k).wait_recv()
    eg_copy.wait()
    eu_copy.wait()

    sides = [hid[:, side].astype(F32).reshape(4 * own_rows, half) for side in range(2)]
    squares = sum(jnp.sum(v * v, axis=-1, keepdims=True) for v in sides)
    inverse = lax.rsqrt(squares / (2 * half) + 1e-06)
    for side in range(2):
        for k in range(half // 128):
            spread = gain[side * (half // 128) + k : side * (half // 128) + k + 1, :].astype(F32)
            piece = sides[side][:, k * 128 : (k + 1) * 128]
            xn[side, :, k * 128 : (k + 1) * 128] = (piece * inverse * spread).astype(BF16)
    span = [slice(side * half, (side + 1) * half) for side in range(2)]
    both_sides = lambda w: sum(
        jnp.dot(xn[side], w[span[side], :], preferred_element_type=F32) for side in range(2)
    )
    affinity = jax.nn.sigmoid(
        sum(contract(xn[side], router[:, span[side]], 1, 1) for side in range(2))
    )
    picked = affinity * chosen[...].reshape(4 * own_rows, 128)[:, : affinity.shape[1]]
    weights = route_scale * picked / jnp.sum(picked, axis=-1, keepdims=True)
    mine = lax.broadcasted_iota(jnp.int32, weights.shape, 1) == e
    gcol[...] = jnp.broadcast_to(
        jnp.sum(jnp.where(mine, weights, 0.0), axis=-1, keepdims=True), gcol.shape
    )
    gate_part = both_sides(eg)
    up_part = both_sides(eu)
    act[...] = (gate_part / (1.0 + jnp.exp(-gate_part)) * up_part).astype(BF16)

    for i in range(BLOCKS):
        down_copy(i).wait()
        block = wslot[3 + i // 4, (i % 4) * depth : (i % 4 + 1) * depth]
        part = jnp.dot(act[...], block, preferred_element_type=F32) * gcol[:, 0:1]
        place = slice((i % per_half) * cols, (i % per_half + 1) * cols)
        pbuf[1, i // per_half, :, :, place] = part.astype(BF16).reshape(4, own_rows, cols)
        if i == per_half - 1:
            swap_copy(1).start()
    out[...] = (hid[e, c].astype(F32) + reduce_rows(1)).astype(BF16)

    def drain(g, _):
        for k in range(3):
            own_copy(g, k).wait_send()
        for k in range(2):
            diag_copy(g, k).wait_send()
            cross_copy(g, k).wait_send()
            last_copy(g, k).wait_send()
        for k in range(4):
            core_copy(g, k).wait_send()
        for k in range(7):
            stat_copy(g, k).wait_send()
        fold_copy(g).wait_send()
        return 0

    lax.fori_loop(0, chunks, drain, 0)
    for k in range(3):
        route_copy(k).wait_send()
        hidfwd_copy(k).wait_send()
        rows_copy(0, k).wait_send()
        rows_copy(1, k).wait_send()
    for k in range(4):
        hid_copy(k).wait_send()
    for p in range(2):
        swap_copy(p).wait_send()


def fused_on_device(
    queries, latent_cache, context_lengths, value_up, out_proj, residual, norm_gain, router,
    routes, expert_gate, expert_up, expert_down,
):
    reqs, verify, heads, width = queries.shape
    chunks = reqs // PAIR
    hr = verify * heads
    _, block_len, _ = latent_cache.shape
    _, latent, vdim = value_up.shape
    own_rows, model = residual.shape
    half = model // 2
    ff = expert_down.shape[1]
    rows = 8 * hr
    _, count = lay_out(chunks)
    vmem, anywhere = pl.BlockSpec(memory_space=pltpu.VMEM), pl.BlockSpec(memory_space=pl.ANY)
    scratch = [
        pltpu.VMEM((chunks, 8, PAIR, hr, width), BF16),
        pltpu.VMEM((2, PAIR, width, block_len), BF16),
        pltpu.VMEM((2, PAIR, rows, latent), F32),
        pltpu.VMEM((2, PAIR, rows), F32),
        pltpu.VMEM((chunks, 8, PAIR, rows), F32),
        pltpu.VMEM((chunks, 2, 2, 2, PAIR, hr, latent), BF16),
        pltpu.VMEM((chunks, 2, 2, PAIR, hr, latent), BF16),
        pltpu.VMEM((chunks, 2, hr, latent), BF16),
        pltpu.VMEM((chunks, 2, hr, latent), BF16),
        pltpu.VMEM((chunks, hr, latent), BF16),
        pltpu.VMEM((chunks, hr, latent), BF16),
        pltpu.VMEM((2, PAIR, hr, latent), BF16),
        pltpu.VMEM((heads, latent, vdim), BF16),
        pltpu.VMEM((reqs * verify, heads * vdim), F32),
        pltpu.VMEM((SLOTS, heads * vdim, model // BLOCKS), BF16),
        pltpu.VMEM((model, ff), BF16),
        pltpu.VMEM((model, ff), BF16),
        pltpu.VMEM((PAIR, rows, block_len), F32),
        pltpu.VMEM((PAIR, rows, block_len), BF16),
        pltpu.VMEM((PAIR, rows, 128), F32),
        pltpu.VMEM((4, own_rows, 128), F32),
        pltpu.VMEM((2, 2, 4, own_rows, half), BF16),
        pltpu.VMEM((2, 4, own_rows, half), BF16),
        pltpu.VMEM((2, 4, own_rows, half), BF16),
        pltpu.VMEM((2, 3, own_rows, half), BF16),
        pltpu.VMEM((4, 2, own_rows, half), BF16),
        pltpu.VMEM((2, 4 * own_rows, half), BF16),
        pltpu.VMEM((4 * own_rows, ff), BF16),
        pltpu.VMEM((4 * own_rows, 128), F32),
        pltpu.SemaphoreType.DMA((count,)),
        pltpu.SemaphoreType.DMA((count,)),
        pltpu.SemaphoreType.DMA((2,)),
        pltpu.SemaphoreType.DMA((4 + BLOCKS,)),
        pltpu.SemaphoreType.DMA((SLOTS,)),
    ]
    return pl.pallas_call(
        layer_kernel,
        out_shape=jax.ShapeDtypeStruct((own_rows, half), BF16),
        in_specs=[pl.BlockSpec(memory_space=pltpu.SMEM)] + [anywhere] * 4 + [vmem] * 2
        + [vmem] * 2 + [anywhere] * 3,
        out_specs=vmem,
        scratch_shapes=scratch,
        compiler_params=pltpu.CompilerParams(
            collective_id=0, has_side_effects=True, vmem_limit_bytes=62 * 1024 * 1024
        ),
        cost_estimate=pl.CostEstimate(
            flops=6_000_000_000, bytes_accessed=64_000_000, transcendentals=2_000_000
        ),
    )(
        context_lengths,
        queries.reshape(chunks, PAIR, hr, width),
        jnp.swapaxes(latent_cache, 1, 2).reshape(chunks, PAIR, width, block_len),
        value_up,
        out_proj,
        residual,
        norm_gain.reshape(model // 128, 128),
        router.T,
        routes.T,
        expert_gate[0],
        expert_up[0],
        expert_down[0],
    )


def solution(mesh):
    grouped = mesh.shape["ctx"] == 2 and mesh.shape["exp"] == 4
    body = fused_on_device if grouped else on_device
    return jax.shard_map(
        body,
        mesh=mesh,
        in_specs=(
            P("req", None, ("ctx", "exp"), None),
            P("req", ("ctx", "exp"), None),
            P("req"),
            P(("ctx", "exp"), None, None),
            P(("ctx", "exp"), None),
            P(("req", "exp"), None),
            P(),
            P(),
            P(("req", "exp"), None),
            P("exp", None, "ctx"),
            P("exp", None, "ctx"),
            P("exp", "ctx", None),
        ),
        out_specs=P(("req", "exp"), "ctx"),
        check_vma=False,
    )
```

```python
import functools
import math

import jax
import jax.numpy as jnp
from jax import lax
from jax.experimental import pallas as pl
from jax.experimental.pallas import tpu as pltpu
from jax.sharding import PartitionSpec as P

route_scale = 2.5


def on_device(
    queries,
    latent_cache,
    context_lengths,
    value_up,
    out_proj,
    residual,
    norm_gain,
    router,
    routes,
    expert_gate,
    expert_up,
    expert_down,
):
    latent_width = value_up.shape[1]
    value_width = value_up.shape[2]
    rope_width = queries.shape[3] - latent_width
    score_scale = 1.0 / math.sqrt(value_width + rope_width)
    heads_here = queries.shape[2]
    block_len = latent_cache.shape[1]
    device = lax.axis_index(("ctx", "exp"))
    all_queries = lax.all_gather(queries, ("ctx", "exp"), axis=2, tiled=True)
    scores = (
        jnp.einsum("rjhd,rtd->rjht", all_queries, latent_cache, preferred_element_type=jnp.float32)
        * score_scale
    )
    positions = device * block_len + jnp.arange(block_len, dtype=jnp.int32)
    visible_upto = context_lengths[:, None] + jnp.arange(2, dtype=jnp.int32)[None, :]
    visible = positions[None, None, None, :] < visible_upto[:, :, None, None]
    masked = jnp.where(visible, scores, -1e30)
    row_max = lax.pmax(jnp.max(masked, axis=-1), ("ctx", "exp"))
    weights = jnp.where(visible, jnp.exp(masked - row_max[..., None]), 0.0)
    weight_sum = jnp.sum(weights, axis=-1)
    latents = latent_cache[:, :, :latent_width]
    weighted = jnp.einsum(
        "rjht,rtl->rjhl", weights.astype(jnp.bfloat16), latents, preferred_element_type=jnp.float32
    )
    summed, sum_all = lax.psum((weighted, weight_sum), ("ctx", "exp"))
    own_weighted = lax.dynamic_slice_in_dim(summed, device * heads_here, heads_here, 2)
    own_sum = lax.dynamic_slice_in_dim(sum_all, device * heads_here, heads_here, 2)
    context = (own_weighted / own_sum[..., None]).astype(jnp.bfloat16)
    head_out = jnp.einsum(
        "rjhl,hlv->rjhv", context, value_up, preferred_element_type=jnp.float32
    ).astype(jnp.bfloat16)
    row_total = head_out.shape[0] * head_out.shape[1]
    head_out = head_out.reshape(row_total, heads_here * value_width)
    own_rows = residual.shape[0]
    owner_index = lax.axis_index("exp")
    attention_all = lax.psum(
        jnp.dot(head_out, out_proj, preferred_element_type=jnp.float32), ("ctx", "exp")
    )
    attention = lax.dynamic_slice_in_dim(attention_all, owner_index * own_rows, own_rows, 0)
    hidden = (residual.astype(jnp.float32) + attention).astype(jnp.bfloat16)
    hidden_wide = hidden.astype(jnp.float32)
    inverse = lax.rsqrt(jnp.mean(hidden_wide * hidden_wide, axis=-1, keepdims=True) + 1e-06)
    normed = (hidden_wide * inverse * norm_gain.astype(jnp.float32)).astype(jnp.bfloat16)
    affinity = jax.nn.sigmoid(jnp.dot(normed, router, preferred_element_type=jnp.float32))
    expert_count = router.shape[1]
    top_count = routes.shape[1]
    capacity = max(2, own_rows * top_count // expert_count)
    chosen = (
        routes[:, :, None] == jnp.arange(expert_count, dtype=jnp.int32)[None, None, :]
    ).astype(jnp.float32)
    picked = jnp.sum(chosen * affinity[:, None, :], axis=-1)
    gate_weights = route_scale * picked / jnp.sum(picked, axis=-1, keepdims=True)
    per_row = jnp.sum(chosen, axis=1)
    earlier = jnp.cumsum(per_row, axis=0) - per_row
    slot_index = jnp.sum(chosen * earlier[:, None, :], axis=-1)
    slot_hot = (
        slot_index[:, :, None] == jnp.arange(capacity, dtype=jnp.float32)[None, None, :]
    ).astype(jnp.float32)
    placement = chosen[:, :, :, None] * slot_hot[:, :, None, :]
    row_place = jnp.sum(placement, axis=1).reshape(own_rows, expert_count * capacity)
    gate_place = jnp.sum(placement * gate_weights[:, :, None, None], axis=1).reshape(
        own_rows, expert_count * capacity
    )
    model_width = normed.shape[1]
    outgoing = jnp.einsum(
        "rs,rd->sd", row_place.astype(jnp.bfloat16), normed, preferred_element_type=jnp.float32
    ).astype(jnp.bfloat16)
    outgoing = outgoing.reshape(expert_count, capacity, model_width)
    arrived = lax.all_to_all(outgoing, "exp", split_axis=0, concat_axis=0, tiled=True)
    gate_part = jnp.einsum(
        "scd,df->scf", arrived, expert_gate[0], preferred_element_type=jnp.float32
    )
    up_part = jnp.einsum("scd,df->scf", arrived, expert_up[0], preferred_element_type=jnp.float32)
    active = (jax.nn.silu(gate_part) * up_part).astype(jnp.bfloat16)
    partial_out = jnp.einsum(
        "scf,fd->scd", active, expert_down[0], preferred_element_type=jnp.float32
    )
    col_width = model_width // lax.axis_size("ctx")
    ctx_index = lax.axis_index("ctx")
    own_cols = lax.dynamic_slice_in_dim(hidden_wide, ctx_index * col_width, col_width, 1)
    full_sum = lax.psum(partial_out.astype(jnp.bfloat16), "ctx").astype(jnp.float32)
    returned = lax.all_to_all(
        full_sum.astype(jnp.bfloat16), "exp", split_axis=0, concat_axis=0, tiled=True
    ).astype(full_sum.dtype)
    returned = lax.dynamic_slice_in_dim(returned, ctx_index * col_width, col_width, 2)
    mixture = jnp.dot(
        gate_place,
        returned.reshape(expert_count * capacity, col_width),
        precision=lax.Precision.HIGHEST,
    )
    return (own_cols + mixture).astype(jnp.bfloat16)


MESH = pl.DeviceIdType.MESH
F32 = jnp.float32
BF16 = jnp.bfloat16
PAIR = 2
SLOTS = 5
BLOCKS = 8
AHEAD = 3


def lay_out(chunks):
    places, count = {}, 0
    for name, number in (
        ("own", 3), ("diag", 2), ("core", 4), ("stat", 7), ("fold", 1), ("cross", 2), ("last", 2),
    ):
        places[name] = (count, number)
        count += number * chunks
    for name, number in (("route", 3), ("swap", 2), ("rows", 6), ("hid", 4), ("hidfwd", 3)):
        places[name] = (count, number)
        count += number
    return places, count


def contract(a, b, da, db):
    return lax.dot_general(a, b, (((da,), (db,)), ((), ())), preferred_element_type=F32)


def layer_kernel(
    lens, q_hbm, cache_hbm, vu_hbm, op_hbm, res, gain, router, routes, eg_hbm, eu_hbm, ed_hbm,
    out,
    qbuf, cbuf, acc, mown, stat, norm, crx, x2, y2, x3, y3, ctx2, vu, ho, wslot, eg, eu,
    sbuf, wbuf, mz, chosen, pbuf, prx, tsum, rrx, hid, xn, act, gcol,
    send, recv, csem, wsem, osem,
):
    chunks, _, heads_rows, width = q_hbm.shape
    heads = heads_rows // 2
    block_len, latent = cache_hbm.shape[3], vu.shape[1]
    vdim = vu.shape[2]
    places, _ = lay_out(chunks)
    scale = 1.0 / math.sqrt(vdim + width - latent)
    half = hid.shape[3]
    cols = half * 2 // BLOCKS
    per_half = BLOCKS // 2
    c = lax.axis_index("ctx")
    e = lax.axis_index("exp")
    ey, ex = e // 2, e % 2
    me = c * 4 + e
    ex_n = e + 1 - 2 * ex
    ey_n = e + 2 - 4 * ey
    ed_n = 3 - e
    others = (ex_n, ey_n, ed_n)
    peers = [(1 - c, e)] + [(c, o) for o in others] + [(1 - c, o) for o in others]

    def remote(kind, g, k, src, dst, to):
        first, stride = places[kind]
        place = first + g * stride + k
        return pltpu.make_async_remote_copy(
            src_ref=src, dst_ref=dst, send_sem=send.at[place], recv_sem=recv.at[place],
            device_id={"ctx": to[0], "exp": to[1]}, device_id_type=MESH,
        )

    core_to, x_to, y_to = (1 - c, e), (c, ex_n), (c, ey_n)

    def own_copy(g, k):
        return remote("own", g, k, q_hbm.at[g], qbuf.at[g, me], (core_to, x_to, y_to)[k])

    def diag_copy(g, k):
        source = c * 4 + (ex_n if k == 0 else ey_n)
        view = qbuf.at[g, source, k]
        return remote("diag", g, k, view, view, (y_to, x_to)[k])

    def core_copy(g, k):
        source = c * 4 + (ex_n, ey_n, ed_n, ed_n)[k]
        view = qbuf.at[g, source] if k < 2 else qbuf.at[g, source, k - 2]
        return remote("core", g, k, view, view, core_to)

    def stat_copy(g, k):
        return remote("stat", g, k, stat.at[g, me], stat.at[g, me], peers[k])

    def fold_copy(g):
        return remote("fold", g, 0, norm.at[g, 1 - c], crx.at[g], core_to)

    def cross_copy(g, k):
        if k == 0:
            return remote("cross", g, 0, crx.at[g, :, 1 - ex, 0], x2.at[g], x_to)
        return remote("cross", g, 1, crx.at[g, 1 - ey, :, 1], y2.at[g], y_to)

    def last_copy(g, k):
        if k == 0:
            return remote("last", g, 0, x2.at[g, 1 - ey], y3.at[g], y_to)
        return remote("last", g, 1, y2.at[g, 1 - ex], x3.at[g], x_to)

    def route_copy(k):
        return remote("route", 0, k, chosen.at[e], chosen.at[e], (c, others[k]))

    def swap_copy(p):
        return remote("swap", 0, p, pbuf.at[p, 0], prx.at[p], core_to)

    def rows_copy(p, k):
        return remote("rows", 0, p * 3 + k, tsum.at[p, others[k]], rrx.at[p, k], (c, others[k]))

    def hid_copy(k):
        to = (x_to, y_to, (c, ed_n), core_to)[k]
        return remote("hid", 0, k, hid.at[e, c], hid.at[e, c], to)

    def hidfwd_copy(k):
        view = hid.at[others[k], c]
        return remote("hidfwd", 0, k, view, view, core_to)

    def cache_copy(g):
        return pltpu.make_async_copy(cache_hbm.at[g], cbuf.at[g % 2], csem.at[g % 2])

    def column(i):
        side = jnp.where(i < per_half, 1 - c, c)
        return pl.multiple_of((side * per_half + i % per_half) * cols, cols)

    def op_copy(i):
        return pltpu.make_async_copy(
            op_hbm.at[:, pl.ds(column(i), cols)], wslot.at[i % SLOTS], osem.at[i % SLOTS]
        )

    depth = ed_hbm.shape[0]

    def down_copy(i):
        place = pl.ds(pl.multiple_of((i % 4) * depth, depth), depth)
        return pltpu.make_async_copy(
            ed_hbm.at[:, pl.ds(column(i), cols)], wslot.at[3 + i // 4, place], wsem.at[4 + i]
        )

    own_q = pltpu.make_async_copy(q_hbm, qbuf.at[:, me], wsem.at[0])
    vu_copy = pltpu.make_async_copy(vu_hbm, vu, wsem.at[1])
    eg_copy = pltpu.make_async_copy(eg_hbm, eg, wsem.at[2])
    eu_copy = pltpu.make_async_copy(eu_hbm, eu, wsem.at[3])

    own_q.start()
    cache_copy(0).start()
    lanes = lax.broadcasted_iota(jnp.int32, chosen.shape[1:], 1)
    square = (routes.shape[1], routes.shape[1])
    diagonal = lax.broadcasted_iota(jnp.int32, square, 0) == lax.broadcasted_iota(jnp.int32, square, 1)
    named = jnp.zeros(lanes.shape, F32)
    for k in range(routes.shape[0]):
        choice = jnp.where(diagonal, routes[k : k + 1, :].astype(F32), 0.0)
        named = named + (jnp.sum(choice, axis=1, keepdims=True) == lanes.astype(F32)).astype(F32)
    chosen[e] = named

    barrier = pltpu.get_barrier_semaphore()
    for to in peers:
        pl.semaphore_signal(
            barrier, inc=1, device_id={"ctx": to[0], "exp": to[1]}, device_id_type=MESH
        )
    pl.semaphore_wait(barrier, len(peers))

    for g in range(AHEAD):
        for k in range(3):
            own_copy(g, k).start()
    for k in range(3):
        route_copy(k).start()
    vu_copy.start()
    own_q.wait()

    rows = 8 * heads_rows

    def attend(g):
        cache_copy(g).wait()

        @pl.when(g + 1 < chunks)
        def _():
            cache_copy(g + 1).start()

        first = lax.broadcasted_iota(jnp.int32, (heads_rows, 128), 1) < 64
        position = me * block_len + lax.broadcasted_iota(jnp.int32, (1, block_len), 1)
        for r in range(PAIR):
            q = qbuf[g, :, r].reshape(rows, width)
            sbuf[r] = jnp.dot(q, cbuf[g % 2, r], preferred_element_type=F32)
        for r in range(PAIR):
            length = lens[g * PAIR + r]
            bias = jnp.concatenate(
                [
                    jnp.broadcast_to(
                        jnp.where(position < length + j, 0.0, -1e30), (heads, block_len)
                    )
                    for j in range(2)
                ],
                axis=0,
            )
            for d in range(8):
                place = slice(d * heads_rows, (d + 1) * heads_rows)
                s = sbuf[r, place] + bias
                m = jnp.max(s, axis=1, keepdims=True)
                p = jnp.exp((s - m) * scale)
                total = jnp.sum(p, axis=1, keepdims=True)
                wbuf[r, place] = p.astype(BF16)
                m = m * scale
                z = jnp.where(m > -1e25, m + jnp.log(total), -1e30)
                mz[r, place] = jnp.where(first, jnp.where(m > -1e25, m, -1e30), z)
            acc[g % 2, r] = contract(wbuf[r], cbuf[g % 2, r, :latent], 1, 1)
            flat = jnp.transpose(mz[r])
            mown[g % 2, r : r + 1] = flat[0:1]
            stat[g, me, r : r + 1] = flat[64:65]
        for k in range(7):
            stat_copy(g, k).start()

    def normalise(g):
        for k in range(7):
            stat_copy(g, k).wait_recv()
        for r in range(PAIR):
            z = stat[g, :, r]
            top = jnp.max(z, axis=0, keepdims=True)
            whole = top + jnp.log(jnp.sum(jnp.exp(z - top), axis=0, keepdims=True))
            factor = jnp.exp(mown[g % 2, r : r + 1] - whole)
            factor = jnp.transpose(jnp.broadcast_to(factor, (128, rows)))
            for k in range(latent // 128):
                part = acc[g % 2, r, :, k * 128 : (k + 1) * 128] * factor
                norm[g, :, :, :, r, :, k * 128 : (k + 1) * 128] = part.astype(BF16).reshape(
                    2, 2, 2, heads_rows, 128
                )
        fold_copy(g).start()

    def fold(g):
        fold_copy(g).wait_recv()
        crx[g] = (crx[g].astype(F32) + norm[g, c].astype(F32)).astype(BF16)
        cross_copy(g, 0).start()
        cross_copy(g, 1).start()

    def cross(g):
        cross_copy(g, 0).wait_recv()
        x2[g] = (x2[g].astype(F32) + crx[g, :, ex, 0].astype(F32)).astype(BF16)
        last_copy(g, 0).start()
        cross_copy(g, 1).wait_recv()
        y2[g] = (y2[g].astype(F32) + crx[g, ey, :, 1].astype(F32)).astype(BF16)
        last_copy(g, 1).start()

    def last(g):
        last_copy(g, 0).wait_recv()
        ctx2[g % 2, 0] = (x2[g, ey].astype(F32) + y3[g].astype(F32)).astype(BF16)
        last_copy(g, 1).wait_recv()
        ctx2[g % 2, 1] = (y2[g, ex].astype(F32) + x3[g].astype(F32)).astype(BF16)

        @pl.when(g % 2 == 1)
        def _():
            both = ctx2[...].reshape(4 * heads_rows, latent)
            for h in range(heads):
                every = jnp.dot(both, vu[h], preferred_element_type=F32).reshape(8, heads, vdim)
                mine = lax.broadcasted_iota(jnp.int32, every.shape, 1) == h
                place = pl.ds(pl.multiple_of((g // 2) * 8, 8), 8)
                ho[place, h * vdim : (h + 1) * vdim] = jnp.sum(
                    jnp.where(mine, every, 0.0), axis=1
                )

    vu_copy.wait()

    def step(s, _):
        def at(lag, run):
            @pl.when((s >= lag) & (s < chunks + lag))
            def _():
                run(s - lag)

        def forward(g):
            own_copy(g, 1).wait_recv()
            diag_copy(g, 0).start()
            core_copy(g, 0).start()
            own_copy(g, 2).wait_recv()
            diag_copy(g, 1).start()
            core_copy(g, 1).start()

        def forward_diag(g):
            for k in range(2):
                diag_copy(g, k).wait_recv()
                core_copy(g, 2 + k).start()

        def attend_when_here(g):
            own_copy(g, 0).wait_recv()
            for k in range(4):
                core_copy(g, k).wait_recv()
            attend(g)

        at(0, forward)
        at(1, forward_diag)

        @pl.when(s + AHEAD < chunks)
        def _():
            for k in range(3):
                own_copy(s + AHEAD, k).start()

        at(4, normalise)
        at(5, fold)
        at(6, cross)
        at(7, last)
        at(2, attend_when_here)

        @pl.when(s < SLOTS)
        def _():
            op_copy(s).start()

        @pl.when(s == SLOTS)
        def _():
            eg_copy.start()

        @pl.when(s == SLOTS + 1)
        def _():
            eu_copy.start()

        return 0

    lax.fori_loop(0, chunks + 7, step, 0)

    own_rows = res.shape[0]

    def project(i, _):
        op_copy(i).wait()
        part = jnp.dot(ho[...].astype(BF16), wslot[i % SLOTS], preferred_element_type=F32)
        place = pl.ds(pl.multiple_of((i % per_half) * cols, cols), cols)
        pbuf[0, i // per_half, :, :, place] = part.astype(BF16).reshape(4, own_rows, cols)

        @pl.when(i + SLOTS < BLOCKS)
        def _():
            op_copy(i + SLOTS).start()

        @pl.when(i == per_half - 1)
        def _():
            swap_copy(0).start()

        return 0

    lax.fori_loop(0, BLOCKS, project, 0)
    for i in range(BLOCKS):
        down_copy(i).start()

    def reduce_rows(p):
        swap_copy(p).wait_recv()
        tsum[p] = (prx[p].astype(F32) + pbuf[p, 1].astype(F32)).astype(BF16)
        for k in (2, 0, 1):
            rows_copy(p, k).start()
        total = tsum[p, e].astype(F32)
        for k in range(3):
            rows_copy(p, k).wait_recv()
            total = total + rrx[p, k].astype(F32)
        return total

    own_cols = pl.ds(pl.multiple_of(c * half, half), half)
    hid[e, c] = (res[:, own_cols].astype(F32) + reduce_rows(0)).astype(BF16)
    for k in (2, 0, 1, 3):
        hid_copy(k).start()
    for k in range(3):
        hid_copy(k).wait_recv()
        hidfwd_copy(k).start()
    hid_copy(3).wait_recv()
    for k in range(3):
        hidfwd_copy(k).wait_recv()
        route_copy(k).wait_recv()
    eg_copy.wait()
    eu_copy.wait()

    sides = [hid[:, side].astype(F32).reshape(4 * own_rows, half) for side in range(2)]
    squares = sum(jnp.sum(v * v, axis=-1, keepdims=True) for v in sides)
    inverse = lax.rsqrt(squares / (2 * half) + 1e-06)
    for side in range(2):
        for k in range(half // 128):
            spread = gain[side * (half // 128) + k : side * (half // 128) + k + 1, :].astype(F32)
            piece = sides[side][:, k * 128 : (k + 1) * 128]
            xn[side, :, k * 128 : (k + 1) * 128] = (piece * inverse * spread).astype(BF16)
    span = [slice(side * half, (side + 1) * half) for side in range(2)]
    both_sides = lambda w: sum(
        jnp.dot(xn[side], w[span[side], :], preferred_element_type=F32) for side in range(2)
    )
    affinity = jax.nn.sigmoid(
        sum(contract(xn[side], router[:, span[side]], 1, 1) for side in range(2))
    )
    picked = affinity * chosen[...].reshape(4 * own_rows, 128)[:, : affinity.shape[1]]
    weights = route_scale * picked / jnp.sum(picked, axis=-1, keepdims=True)
    mine = lax.broadcasted_iota(jnp.int32, weights.shape, 1) == e
    gcol[...] = jnp.broadcast_to(
        jnp.sum(jnp.where(mine, weights, 0.0), axis=-1, keepdims=True), gcol.shape
    )
    gate_part = both_sides(eg)
    up_part = both_sides(eu)
    act[...] = (gate_part / (1.0 + jnp.exp(-gate_part)) * up_part).astype(BF16)

    for i in range(BLOCKS):
        down_copy(i).wait()
        block = wslot[3 + i // 4, (i % 4) * depth : (i % 4 + 1) * depth]
        part = jnp.dot(act[...], block, preferred_element_type=F32) * gcol[:, 0:1]
        place = slice((i % per_half) * cols, (i % per_half + 1) * cols)
        pbuf[1, i // per_half, :, :, place] = part.astype(BF16).reshape(4, own_rows, cols)
        if i == per_half - 1:
            swap_copy(1).start()
    out[...] = (hid[e, c].astype(F32) + reduce_rows(1)).astype(BF16)

    def drain(g, _):
        for k in range(3):
            own_copy(g, k).wait_send()
        for k in range(2):
            diag_copy(g, k).wait_send()
            cross_copy(g, k).wait_send()
            last_copy(g, k).wait_send()
        for k in range(4):
            core_copy(g, k).wait_send()
        for k in range(7):
            stat_copy(g, k).wait_send()
        fold_copy(g).wait_send()
        return 0

    lax.fori_loop(0, chunks, drain, 0)
    for k in range(3):
        route_copy(k).wait_send()
        hidfwd_copy(k).wait_send()
        rows_copy(0, k).wait_send()
        rows_copy(1, k).wait_send()
    for k in range(4):
        hid_copy(k).wait_send()
    for p in range(2):
        swap_copy(p).wait_send()


def fused_on_device(
    queries, latent_cache, context_lengths, value_up, out_proj, residual, norm_gain, router,
    routes, expert_gate, expert_up, expert_down,
):
    reqs, verify, heads, width = queries.shape
    chunks = reqs // PAIR
    hr = verify * heads
    _, block_len, _ = latent_cache.shape
    _, latent, vdim = value_up.shape
    own_rows, model = residual.shape
    half = model // 2
    ff = expert_down.shape[1]
    rows = 8 * hr
    _, count = lay_out(chunks)
    vmem, anywhere = pl.BlockSpec(memory_space=pltpu.VMEM), pl.BlockSpec(memory_space=pl.ANY)
    scratch = [
        pltpu.VMEM((chunks, 8, PAIR, hr, width), BF16),
        pltpu.VMEM((2, PAIR, width, block_len), BF16),
        pltpu.VMEM((2, PAIR, rows, latent), F32),
        pltpu.VMEM((2, PAIR, rows), F32),
        pltpu.VMEM((chunks, 8, PAIR, rows), F32),
        pltpu.VMEM((chunks, 2, 2, 2, PAIR, hr, latent), BF16),
        pltpu.VMEM((chunks, 2, 2, PAIR, hr, latent), BF16),
        pltpu.VMEM((chunks, 2, hr, latent), BF16),
        pltpu.VMEM((chunks, 2, hr, latent), BF16),
        pltpu.VMEM((chunks, hr, latent), BF16),
        pltpu.VMEM((chunks, hr, latent), BF16),
        pltpu.VMEM((2, PAIR, hr, latent), BF16),
        pltpu.VMEM((heads, latent, vdim), BF16),
        pltpu.VMEM((reqs * verify, heads * vdim), F32),
        pltpu.VMEM((SLOTS, heads * vdim, model // BLOCKS), BF16),
        pltpu.VMEM((model, ff), BF16),
        pltpu.VMEM((model, ff), BF16),
        pltpu.VMEM((PAIR, rows, block_len), F32),
        pltpu.VMEM((PAIR, rows, block_len), BF16),
        pltpu.VMEM((PAIR, rows, 128), F32),
        pltpu.VMEM((4, own_rows, 128), F32),
        pltpu.VMEM((2, 2, 4, own_rows, half), BF16),
        pltpu.VMEM((2, 4, own_rows, half), BF16),
        pltpu.VMEM((2, 4, own_rows, half), BF16),
        pltpu.VMEM((2, 3, own_rows, half), BF16),
        pltpu.VMEM((4, 2, own_rows, half), BF16),
        pltpu.VMEM((2, 4 * own_rows, half), BF16),
        pltpu.VMEM((4 * own_rows, ff), BF16),
        pltpu.VMEM((4 * own_rows, 128), F32),
        pltpu.SemaphoreType.DMA((count,)),
        pltpu.SemaphoreType.DMA((count,)),
        pltpu.SemaphoreType.DMA((2,)),
        pltpu.SemaphoreType.DMA((4 + BLOCKS,)),
        pltpu.SemaphoreType.DMA((SLOTS,)),
    ]
    return pl.pallas_call(
        layer_kernel,
        out_shape=jax.ShapeDtypeStruct((own_rows, half), BF16),
        in_specs=[pl.BlockSpec(memory_space=pltpu.SMEM)] + [anywhere] * 4 + [vmem] * 2
        + [vmem] * 2 + [anywhere] * 3,
        out_specs=vmem,
        scratch_shapes=scratch,
        compiler_params=pltpu.CompilerParams(
            collective_id=0, has_side_effects=True, vmem_limit_bytes=62 * 1024 * 1024
        ),
        cost_estimate=pl.CostEstimate(
            flops=6_000_000_000, bytes_accessed=64_000_000, transcendentals=2_000_000
        ),
    )(
        context_lengths,
        queries.reshape(chunks, PAIR, hr, width),
        jnp.swapaxes(latent_cache, 1, 2).reshape(chunks, PAIR, width, block_len),
        value_up,
        out_proj,
        residual,
        norm_gain.reshape(model // 128, 128),
        router.T,
        routes.T,
        expert_gate[0],
        expert_up[0],
        expert_down[0],
    )


def solution(mesh):
    grouped = mesh.shape["ctx"] == 2 and mesh.shape["exp"] == 4
    body = fused_on_device if grouped else on_device
    return jax.shard_map(
        body,
        mesh=mesh,
        in_specs=(
            P("req", None, ("ctx", "exp"), None),
            P("req", ("ctx", "exp"), None),
            P("req"),
            P(("ctx", "exp"), None, None),
            P(("ctx", "exp"), None),
            P(("req", "exp"), None),
            P(),
            P(),
            P(("req", "exp"), None),
            P("exp", None, "ctx"),
            P("exp", None, "ctx"),
            P("exp", "ctx", None),
        ),
        out_specs=P(("req", "exp"), "ctx"),
        check_vma=False,
    )
```

```python
import functools
import math

import jax
import jax.numpy as jnp
from jax import lax
from jax.experimental import pallas as pl
from jax.experimental.pallas import tpu as pltpu
from jax.sharding import PartitionSpec as P

route_scale = 2.5


def on_device(
    queries,
    latent_cache,
    context_lengths,
    value_up,
    out_proj,
    residual,
    norm_gain,
    router,
    routes,
    expert_gate,
    expert_up,
    expert_down,
):
    latent_width = value_up.shape[1]
    value_width = value_up.shape[2]
    rope_width = queries.shape[3] - latent_width
    score_scale = 1.0 / math.sqrt(value_width + rope_width)
    heads_here = queries.shape[2]
    block_len = latent_cache.shape[1]
    device = lax.axis_index(("ctx", "exp"))
    all_queries = lax.all_gather(queries, ("ctx", "exp"), axis=2, tiled=True)
    scores = (
        jnp.einsum("rjhd,rtd->rjht", all_queries, latent_cache, preferred_element_type=jnp.float32)
        * score_scale
    )
    positions = device * block_len + jnp.arange(block_len, dtype=jnp.int32)
    visible_upto = context_lengths[:, None] + jnp.arange(2, dtype=jnp.int32)[None, :]
    visible = positions[None, None, None, :] < visible_upto[:, :, None, None]
    masked = jnp.where(visible, scores, -1e30)
    row_max = lax.pmax(jnp.max(masked, axis=-1), ("ctx", "exp"))
    weights = jnp.where(visible, jnp.exp(masked - row_max[..., None]), 0.0)
    weight_sum = jnp.sum(weights, axis=-1)
    latents = latent_cache[:, :, :latent_width]
    weighted = jnp.einsum(
        "rjht,rtl->rjhl", weights.astype(jnp.bfloat16), latents, preferred_element_type=jnp.float32
    )
    summed, sum_all = lax.psum((weighted, weight_sum), ("ctx", "exp"))
    own_weighted = lax.dynamic_slice_in_dim(summed, device * heads_here, heads_here, 2)
    own_sum = lax.dynamic_slice_in_dim(sum_all, device * heads_here, heads_here, 2)
    context = (own_weighted / own_sum[..., None]).astype(jnp.bfloat16)
    head_out = jnp.einsum(
        "rjhl,hlv->rjhv", context, value_up, preferred_element_type=jnp.float32
    ).astype(jnp.bfloat16)
    row_total = head_out.shape[0] * head_out.shape[1]
    head_out = head_out.reshape(row_total, heads_here * value_width)
    own_rows = residual.shape[0]
    owner_index = lax.axis_index("exp")
    attention_all = lax.psum(
        jnp.dot(head_out, out_proj, preferred_element_type=jnp.float32), ("ctx", "exp")
    )
    attention = lax.dynamic_slice_in_dim(attention_all, owner_index * own_rows, own_rows, 0)
    hidden = (residual.astype(jnp.float32) + attention).astype(jnp.bfloat16)
    hidden_wide = hidden.astype(jnp.float32)
    inverse = lax.rsqrt(jnp.mean(hidden_wide * hidden_wide, axis=-1, keepdims=True) + 1e-06)
    normed = (hidden_wide * inverse * norm_gain.astype(jnp.float32)).astype(jnp.bfloat16)
    affinity = jax.nn.sigmoid(jnp.dot(normed, router, preferred_element_type=jnp.float32))
    expert_count = router.shape[1]
    top_count = routes.shape[1]
    capacity = max(2, own_rows * top_count // expert_count)
    chosen = (
        routes[:, :, None] == jnp.arange(expert_count, dtype=jnp.int32)[None, None, :]
    ).astype(jnp.float32)
    picked = jnp.sum(chosen * affinity[:, None, :], axis=-1)
    gate_weights = route_scale * picked / jnp.sum(picked, axis=-1, keepdims=True)
    per_row = jnp.sum(chosen, axis=1)
    earlier = jnp.cumsum(per_row, axis=0) - per_row
    slot_index = jnp.sum(chosen * earlier[:, None, :], axis=-1)
    slot_hot = (
        slot_index[:, :, None] == jnp.arange(capacity, dtype=jnp.float32)[None, None, :]
    ).astype(jnp.float32)
    placement = chosen[:, :, :, None] * slot_hot[:, :, None, :]
    row_place = jnp.sum(placement, axis=1).reshape(own_rows, expert_count * capacity)
    gate_place = jnp.sum(placement * gate_weights[:, :, None, None], axis=1).reshape(
        own_rows, expert_count * capacity
    )
    model_width = normed.shape[1]
    outgoing = jnp.einsum(
        "rs,rd->sd", row_place.astype(jnp.bfloat16), normed, preferred_element_type=jnp.float32
    ).astype(jnp.bfloat16)
    outgoing = outgoing.reshape(expert_count, capacity, model_width)
    arrived = lax.all_to_all(outgoing, "exp", split_axis=0, concat_axis=0, tiled=True)
    gate_part = jnp.einsum(
        "scd,df->scf", arrived, expert_gate[0], preferred_element_type=jnp.float32
    )
    up_part = jnp.einsum("scd,df->scf", arrived, expert_up[0], preferred_element_type=jnp.float32)
    active = (jax.nn.silu(gate_part) * up_part).astype(jnp.bfloat16)
    partial_out = jnp.einsum(
        "scf,fd->scd", active, expert_down[0], preferred_element_type=jnp.float32
    )
    col_width = model_width // lax.axis_size("ctx")
    ctx_index = lax.axis_index("ctx")
    own_cols = lax.dynamic_slice_in_dim(hidden_wide, ctx_index * col_width, col_width, 1)
    full_sum = lax.psum(partial_out.astype(jnp.bfloat16), "ctx").astype(jnp.float32)
    returned = lax.all_to_all(
        full_sum.astype(jnp.bfloat16), "exp", split_axis=0, concat_axis=0, tiled=True
    ).astype(full_sum.dtype)
    returned = lax.dynamic_slice_in_dim(returned, ctx_index * col_width, col_width, 2)
    mixture = jnp.dot(
        gate_place,
        returned.reshape(expert_count * capacity, col_width),
        precision=lax.Precision.HIGHEST,
    )
    return (own_cols + mixture).astype(jnp.bfloat16)


MESH = pl.DeviceIdType.MESH
F32 = jnp.float32
BF16 = jnp.bfloat16
PAIR = 2
SLOTS = 5
BLOCKS = 8
PIECES = 2
AHEAD = 3


def lay_out(chunks):
    places, count = {}, 0
    for name, number in (
        ("own", 3), ("diag", 2), ("core", 4), ("stat", 7), ("fold", 1), ("cross", 2), ("last", 2),
    ):
        places[name] = (count, number)
        count += number * chunks
    for name, number in (
        ("route", 3), ("swap", 2 * PIECES), ("rows", 6 * PIECES), ("hid", 4 * PIECES),
        ("hidfwd", 3 * PIECES),
    ):
        places[name] = (count, number)
        count += number
    return places, count


def contract(a, b, da, db):
    return lax.dot_general(a, b, (((da,), (db,)), ((), ())), preferred_element_type=F32)


def layer_kernel(
    lens, q_hbm, cache_hbm, vu_hbm, op_hbm, res, gain, router, routes, eg_hbm, eu_hbm, ed_hbm,
    out,
    qbuf, cbuf, acc, mown, stat, norm, crx, x2, y2, x3, y3, ctx2, vu, ho, wslot, eg, eu,
    sbuf, wbuf, mz, spread, chosen, pbuf, prx, tsum, rrx, hid, xn, act, gcol,
    send, recv, csem, wsem, osem,
):
    chunks, _, heads_rows, width = q_hbm.shape
    heads = heads_rows // 2
    block_len, latent = cache_hbm.shape[3], vu.shape[1]
    vdim = vu.shape[2]
    places, _ = lay_out(chunks)
    scale = 1.0 / math.sqrt(vdim + width - latent)
    piece = hid.shape[4]
    half = piece * PIECES
    cols = half * 2 // BLOCKS
    per_half = BLOCKS // 2
    c = lax.axis_index("ctx")
    e = lax.axis_index("exp")
    ey, ex = e // 2, e % 2
    me = c * 4 + e
    ex_n = e + 1 - 2 * ex
    ey_n = e + 2 - 4 * ey
    ed_n = 3 - e
    others = (ex_n, ey_n, ed_n)
    peers = [(1 - c, e)] + [(c, o) for o in others] + [(1 - c, o) for o in others]

    def remote(kind, g, k, src, dst, to):
        first, stride = places[kind]
        place = first + g * stride + k
        return pltpu.make_async_remote_copy(
            src_ref=src, dst_ref=dst, send_sem=send.at[place], recv_sem=recv.at[place],
            device_id={"ctx": to[0], "exp": to[1]}, device_id_type=MESH,
        )

    core_to, x_to, y_to = (1 - c, e), (c, ex_n), (c, ey_n)

    def own_copy(g, k):
        return remote("own", g, k, q_hbm.at[g], qbuf.at[g, me], (core_to, x_to, y_to)[k])

    def diag_copy(g, k):
        source = c * 4 + (ex_n if k == 0 else ey_n)
        view = qbuf.at[g, source, k]
        return remote("diag", g, k, view, view, (y_to, x_to)[k])

    def core_copy(g, k):
        source = c * 4 + (ex_n, ey_n, ed_n, ed_n)[k]
        view = qbuf.at[g, source] if k < 2 else qbuf.at[g, source, k - 2]
        return remote("core", g, k, view, view, core_to)

    def stat_copy(g, k):
        return remote("stat", g, k, stat.at[g, me], stat.at[g, me], peers[k])

    def fold_copy(g):
        return remote("fold", g, 0, norm.at[g, 1 - c], crx.at[g], core_to)

    def cross_copy(g, k):
        if k == 0:
            return remote("cross", g, 0, crx.at[g, :, 1 - ex, 0], x2.at[g], x_to)
        return remote("cross", g, 1, crx.at[g, 1 - ey, :, 1], y2.at[g], y_to)

    def last_copy(g, k):
        if k == 0:
            return remote("last", g, 0, x2.at[g, 1 - ey], y3.at[g], y_to)
        return remote("last", g, 1, y2.at[g, 1 - ex], x3.at[g], x_to)

    def route_copy(k):
        return remote("route", 0, k, chosen.at[e], chosen.at[e], (c, others[k]))

    def swap_copy(p, j):
        return remote("swap", 0, p * PIECES + j, pbuf.at[p, 0, j], prx.at[p, j], core_to)

    def rows_copy(p, j, k):
        return remote(
            "rows", 0, (p * PIECES + j) * 3 + k, tsum.at[p, j, others[k]], rrx.at[p, j, k],
            (c, others[k]),
        )

    def hid_copy(j, k):
        to = (x_to, y_to, (c, ed_n), core_to)[k]
        return remote("hid", 0, j * 4 + k, hid.at[c, j, e], hid.at[c, j, e], to)

    def hidfwd_copy(j, k):
        view = hid.at[c, j, others[k]]
        return remote("hidfwd", 0, j * 3 + k, view, view, core_to)

    def cache_copy(g):
        return pltpu.make_async_copy(cache_hbm.at[g], cbuf.at[g % 2], csem.at[g % 2])

    def column(i):
        side = jnp.where(i < per_half, 1 - c, c)
        return pl.multiple_of((side * per_half + i % per_half) * cols, cols)

    def op_copy(i):
        return pltpu.make_async_copy(
            op_hbm.at[:, pl.ds(column(i), cols)], wslot.at[i % SLOTS], osem.at[i % SLOTS]
        )

    depth = ed_hbm.shape[0]

    def down_copy(i):
        place = pl.ds(pl.multiple_of((i % 4) * depth, depth), depth)
        return pltpu.make_async_copy(
            ed_hbm.at[:, pl.ds(column(i), cols)], wslot.at[3 + i // 4, place], wsem.at[4 + i]
        )

    own_q = pltpu.make_async_copy(q_hbm, qbuf.at[:, me], wsem.at[0])
    vu_copy = pltpu.make_async_copy(vu_hbm, vu, wsem.at[1])
    eg_copy = pltpu.make_async_copy(eg_hbm, eg, wsem.at[2])
    eu_copy = pltpu.make_async_copy(eu_hbm, eu, wsem.at[3])

    own_q.start()
    cache_copy(0).start()
    lanes = lax.broadcasted_iota(jnp.int32, chosen.shape[1:], 1)
    square = (routes.shape[1], routes.shape[1])
    diagonal = lax.broadcasted_iota(jnp.int32, square, 0) == lax.broadcasted_iota(jnp.int32, square, 1)
    named = jnp.zeros(lanes.shape, F32)
    for k in range(routes.shape[0]):
        choice = jnp.where(diagonal, routes[k : k + 1, :].astype(F32), 0.0)
        named = named + (jnp.sum(choice, axis=1, keepdims=True) == lanes.astype(F32)).astype(F32)
    chosen[e] = named

    barrier = pltpu.get_barrier_semaphore()
    for to in peers:
        pl.semaphore_signal(
            barrier, inc=1, device_id={"ctx": to[0], "exp": to[1]}, device_id_type=MESH
        )
    pl.semaphore_wait(barrier, len(peers))

    for g in range(AHEAD):
        for k in range(3):
            own_copy(g, k).start()
    for k in range(3):
        route_copy(k).start()
    vu_copy.start()
    lanes_of = piece // 128
    for i in range(2 * PIECES):
        spread[i] = gain[i * lanes_of : (i + 1) * lanes_of, :].astype(F32)
    own_q.wait()

    rows = 8 * heads_rows

    def attend(g):
        cache_copy(g).wait()

        @pl.when(g + 1 < chunks)
        def _():
            cache_copy(g + 1).start()

        first = lax.broadcasted_iota(jnp.int32, (heads_rows, 128), 1) < 64
        position = me * block_len + lax.broadcasted_iota(jnp.int32, (1, block_len), 1)
        for r in range(PAIR):
            q = qbuf[g, :, r].reshape(rows, width)
            sbuf[r] = jnp.dot(q, cbuf[g % 2, r], preferred_element_type=F32)
        for r in range(PAIR):
            length = lens[g * PAIR + r]
            bias = jnp.concatenate(
                [
                    jnp.broadcast_to(
                        jnp.where(position < length + j, 0.0, -1e30), (heads, block_len)
                    )
                    for j in range(2)
                ],
                axis=0,
            )
            for d in range(8):
                place = slice(d * heads_rows, (d + 1) * heads_rows)
                s = sbuf[r, place] + bias
                m = jnp.max(s, axis=1, keepdims=True)
                p = jnp.exp((s - m) * scale)
                total = jnp.sum(p, axis=1, keepdims=True)
                wbuf[r, place] = p.astype(BF16)
                m = m * scale
                z = jnp.where(m > -1e25, m + jnp.log(total), -1e30)
                mz[r, place] = jnp.where(first, jnp.where(m > -1e25, m, -1e30), z)
            acc[g % 2, r] = contract(wbuf[r], cbuf[g % 2, r, :latent], 1, 1)
            flat = jnp.transpose(mz[r])
            mown[g % 2, r : r + 1] = flat[0:1]
            stat[g, me, r : r + 1] = flat[64:65]
        for k in range(7):
            stat_copy(g, k).start()

    def normalise(g):
        for k in range(7):
            stat_copy(g, k).wait_recv()
        for r in range(PAIR):
            z = stat[g, :, r]
            top = jnp.max(z, axis=0, keepdims=True)
            whole = top + jnp.log(jnp.sum(jnp.exp(z - top), axis=0, keepdims=True))
            factor = jnp.exp(mown[g % 2, r : r + 1] - whole)
            factor = jnp.transpose(jnp.broadcast_to(factor, (128, rows)))
            for k in range(latent // 128):
                part = acc[g % 2, r, :, k * 128 : (k + 1) * 128] * factor
                norm[g, :, :, :, r, :, k * 128 : (k + 1) * 128] = part.astype(BF16).reshape(
                    2, 2, 2, heads_rows, 128
                )
        fold_copy(g).start()

    def fold(g):
        fold_copy(g).wait_recv()
        crx[g] = (crx[g].astype(F32) + norm[g, c].astype(F32)).astype(BF16)
        cross_copy(g, 0).start()
        cross_copy(g, 1).start()

    def cross(g):
        cross_copy(g, 0).wait_recv()
        x2[g] = (x2[g].astype(F32) + crx[g, :, ex, 0].astype(F32)).astype(BF16)
        last_copy(g, 0).start()
        cross_copy(g, 1).wait_recv()
        y2[g] = (y2[g].astype(F32) + crx[g, ey, :, 1].astype(F32)).astype(BF16)
        last_copy(g, 1).start()

    def last(g):
        last_copy(g, 0).wait_recv()
        ctx2[g % 2, 0] = (x2[g, ey].astype(F32) + y3[g].astype(F32)).astype(BF16)
        last_copy(g, 1).wait_recv()
        ctx2[g % 2, 1] = (y2[g, ex].astype(F32) + x3[g].astype(F32)).astype(BF16)

        @pl.when(g % 2 == 1)
        def _():
            both = ctx2[...].reshape(4 * heads_rows, latent)
            for h in range(heads):
                every = jnp.dot(both, vu[h], preferred_element_type=F32).reshape(8, heads, vdim)
                mine = lax.broadcasted_iota(jnp.int32, every.shape, 1) == h
                place = pl.ds(pl.multiple_of((g // 2) * 8, 8), 8)
                ho[place, h * vdim : (h + 1) * vdim] = jnp.sum(
                    jnp.where(mine, every, 0.0), axis=1
                )

    vu_copy.wait()

    def step(s, _):
        def at(lag, run):
            @pl.when((s >= lag) & (s < chunks + lag))
            def _():
                run(s - lag)

        def forward(g):
            own_copy(g, 1).wait_recv()
            diag_copy(g, 0).start()
            core_copy(g, 0).start()
            own_copy(g, 2).wait_recv()
            diag_copy(g, 1).start()
            core_copy(g, 1).start()

        def forward_diag(g):
            for k in range(2):
                diag_copy(g, k).wait_recv()
                core_copy(g, 2 + k).start()

        def attend_when_here(g):
            own_copy(g, 0).wait_recv()
            for k in range(4):
                core_copy(g, k).wait_recv()
            attend(g)

        at(0, forward)
        at(1, forward_diag)

        @pl.when(s + AHEAD < chunks)
        def _():
            for k in range(3):
                own_copy(s + AHEAD, k).start()

        at(4, normalise)
        at(5, fold)
        at(6, cross)
        at(7, last)
        at(2, attend_when_here)

        @pl.when(s < SLOTS)
        def _():
            op_copy(s).start()

        @pl.when(s == SLOTS)
        def _():
            eg_copy.start()

        @pl.when(s == SLOTS + 1)
        def _():
            eu_copy.start()

        return 0

    lax.fori_loop(0, chunks + 7, step, 0)

    own_rows = res.shape[0]

    per_piece = per_half // PIECES

    def put(p, i, part):
        place = slice(i % per_piece * cols, (i % per_piece + 1) * cols)
        j = i % per_half // per_piece
        pbuf[p, i // per_half, j, :, :, place] = part.astype(BF16).reshape(4, own_rows, cols)
        if i % per_piece == per_piece - 1:
            if i < per_half:
                swap_copy(p, j).start()
            else:
                swap_copy(p, j).wait_recv()
                total = prx[p, j].astype(F32) + pbuf[p, 1, j].astype(F32)
                tsum[p, j] = total.astype(BF16)
                for k in (2, 0, 1):
                    rows_copy(p, j, k).start()

    def rows_total(p, j):
        total = tsum[p, j, e].astype(F32)
        for k in range(3):
            rows_copy(p, j, k).wait_recv()
            total = total + rrx[p, j, k].astype(F32)
        return total

    head_out = ho[...].astype(BF16)
    for i in range(BLOCKS):
        op_copy(i).wait()
        put(0, i, jnp.dot(head_out, wslot[i % SLOTS], preferred_element_type=F32))
        if i + SLOTS < BLOCKS:
            op_copy(i + SLOTS).start()
    for i in range(BLOCKS):
        down_copy(i).start()

    for j in range(PIECES):
        own_cols = pl.ds(pl.multiple_of(c * half + j * piece, piece), piece)
        hid[c, j, e] = (res[:, own_cols].astype(F32) + rows_total(0, j)).astype(BF16)
        for k in (2, 0, 1, 3):
            hid_copy(j, k).start()
    eg_copy.wait()
    eu_copy.wait()

    squares, logits, gate_part, up_part = 0.0, 0.0, 0.0, 0.0
    for i in range(2 * PIECES):
        side, j = (c if i < PIECES else 1 - c), i % PIECES
        if i < PIECES:
            for k in range(3):
                hid_copy(j, k).wait_recv()
                hidfwd_copy(j, k).start()
        else:
            hid_copy(j, 3).wait_recv()
            for k in range(3):
                hidfwd_copy(j, k).wait_recv()
        wide = hid[side, j].astype(F32).reshape(4 * own_rows, piece)
        squares = squares + jnp.sum(wide * wide, axis=-1, keepdims=True)
        for k in range(piece // 128):
            lane = slice(k * 128, (k + 1) * 128)
            xn[i, :, lane] = (wide[:, lane] * spread[side * PIECES + j, k : k + 1]).astype(BF16)
        span = pl.ds(pl.multiple_of(side * half + j * piece, piece), piece)
        logits = logits + contract(xn[i], router[:, span], 1, 1)
        gate_part = gate_part + jnp.dot(xn[i], eg[span, :], preferred_element_type=F32)
        up_part = up_part + jnp.dot(xn[i], eu[span, :], preferred_element_type=F32)
    inverse = lax.rsqrt(squares / (2 * half) + 1e-06)
    gate_part, up_part = gate_part * inverse, up_part * inverse
    act[...] = (gate_part / (1.0 + jnp.exp(-gate_part)) * up_part).astype(BF16)
    for k in range(3):
        route_copy(k).wait_recv()
    affinity = jax.nn.sigmoid(logits * inverse)
    picked = affinity * chosen[...].reshape(4 * own_rows, 128)[:, : affinity.shape[1]]
    weights = route_scale * picked / jnp.sum(picked, axis=-1, keepdims=True)
    mine = lax.broadcasted_iota(jnp.int32, weights.shape, 1) == e
    gcol[...] = jnp.broadcast_to(
        jnp.sum(jnp.where(mine, weights, 0.0), axis=-1, keepdims=True), gcol.shape
    )

    for i in range(BLOCKS):
        down_copy(i).wait()
        block = wslot[3 + i // 4, (i % 4) * depth : (i % 4 + 1) * depth]
        put(1, i, jnp.dot(act[...], block, preferred_element_type=F32) * gcol[:, 0:1])
    for j in range(PIECES):
        total = hid[c, j, e].astype(F32) + rows_total(1, j)
        out[:, j * piece : (j + 1) * piece] = total.astype(BF16)

    def drain(g, _):
        for k in range(3):
            own_copy(g, k).wait_send()
        for k in range(2):
            diag_copy(g, k).wait_send()
            cross_copy(g, k).wait_send()
            last_copy(g, k).wait_send()
        for k in range(4):
            core_copy(g, k).wait_send()
        for k in range(7):
            stat_copy(g, k).wait_send()
        fold_copy(g).wait_send()
        return 0

    lax.fori_loop(0, chunks, drain, 0)
    for k in range(3):
        route_copy(k).wait_send()
        for j in range(PIECES):
            hidfwd_copy(j, k).wait_send()
            rows_copy(0, j, k).wait_send()
            rows_copy(1, j, k).wait_send()
    for j in range(PIECES):
        for k in range(4):
            hid_copy(j, k).wait_send()
        for p in range(2):
            swap_copy(p, j).wait_send()


def fused_on_device(
    queries, latent_cache, context_lengths, value_up, out_proj, residual, norm_gain, router,
    routes, expert_gate, expert_up, expert_down,
):
    reqs, verify, heads, width = queries.shape
    chunks = reqs // PAIR
    hr = verify * heads
    _, block_len, _ = latent_cache.shape
    _, latent, vdim = value_up.shape
    own_rows, model = residual.shape
    half = model // 2
    piece = half // PIECES
    ff = expert_down.shape[1]
    rows = 8 * hr
    _, count = lay_out(chunks)
    vmem, anywhere = pl.BlockSpec(memory_space=pltpu.VMEM), pl.BlockSpec(memory_space=pl.ANY)
    scratch = [
        pltpu.VMEM((chunks, 8, PAIR, hr, width), BF16),
        pltpu.VMEM((2, PAIR, width, block_len), BF16),
        pltpu.VMEM((2, PAIR, rows, latent), F32),
        pltpu.VMEM((2, PAIR, rows), F32),
        pltpu.VMEM((chunks, 8, PAIR, rows), F32),
        pltpu.VMEM((chunks, 2, 2, 2, PAIR, hr, latent), BF16),
        pltpu.VMEM((chunks, 2, 2, PAIR, hr, latent), BF16),
        pltpu.VMEM((chunks, 2, hr, latent), BF16),
        pltpu.VMEM((chunks, 2, hr, latent), BF16),
        pltpu.VMEM((chunks, hr, latent), BF16),
        pltpu.VMEM((chunks, hr, latent), BF16),
        pltpu.VMEM((2, PAIR, hr, latent), BF16),
        pltpu.VMEM((heads, latent, vdim), BF16),
        pltpu.VMEM((reqs * verify, heads * vdim), F32),
        pltpu.VMEM((SLOTS, heads * vdim, model // BLOCKS), BF16),
        pltpu.VMEM((model, ff), BF16),
        pltpu.VMEM((model, ff), BF16),
        pltpu.VMEM((PAIR, rows, block_len), F32),
        pltpu.VMEM((PAIR, rows, block_len), BF16),
        pltpu.VMEM((PAIR, rows, 128), F32),
        pltpu.VMEM((2 * PIECES, piece // 128, 128), F32),
        pltpu.VMEM((4, own_rows, 128), F32),
        pltpu.VMEM((2, 2, PIECES, 4, own_rows, piece), BF16),
        pltpu.VMEM((2, PIECES, 4, own_rows, piece), BF16),
        pltpu.VMEM((2, PIECES, 4, own_rows, piece), BF16),
        pltpu.VMEM((2, PIECES, 3, own_rows, piece), BF16),
        pltpu.VMEM((2, PIECES, 4, own_rows, piece), BF16),
        pltpu.VMEM((2 * PIECES, 4 * own_rows, piece), BF16),
        pltpu.VMEM((4 * own_rows, ff), BF16),
        pltpu.VMEM((4 * own_rows, 128), F32),
        pltpu.SemaphoreType.DMA((count,)),
        pltpu.SemaphoreType.DMA((count,)),
        pltpu.SemaphoreType.DMA((2,)),
        pltpu.SemaphoreType.DMA((4 + BLOCKS,)),
        pltpu.SemaphoreType.DMA((SLOTS,)),
    ]
    return pl.pallas_call(
        layer_kernel,
        out_shape=jax.ShapeDtypeStruct((own_rows, half), BF16),
        in_specs=[pl.BlockSpec(memory_space=pltpu.SMEM)] + [anywhere] * 4 + [vmem] * 2
        + [vmem] * 2 + [anywhere] * 3,
        out_specs=vmem,
        scratch_shapes=scratch,
        compiler_params=pltpu.CompilerParams(
            collective_id=0, has_side_effects=True, vmem_limit_bytes=62 * 1024 * 1024
        ),
        cost_estimate=pl.CostEstimate(
            flops=6_000_000_000, bytes_accessed=64_000_000, transcendentals=2_000_000
        ),
    )(
        context_lengths,
        queries.reshape(chunks, PAIR, hr, width),
        jnp.swapaxes(latent_cache, 1, 2).reshape(chunks, PAIR, width, block_len),
        value_up,
        out_proj,
        residual,
        norm_gain.reshape(model // 128, 128),
        router.T,
        routes.T,
        expert_gate[0],
        expert_up[0],
        expert_down[0],
    )


def solution(mesh):
    grouped = mesh.shape["ctx"] == 2 and mesh.shape["exp"] == 4
    body = fused_on_device if grouped else on_device
    return jax.shard_map(
        body,
        mesh=mesh,
        in_specs=(
            P("req", None, ("ctx", "exp"), None),
            P("req", ("ctx", "exp"), None),
            P("req"),
            P(("ctx", "exp"), None, None),
            P(("ctx", "exp"), None),
            P(("req", "exp"), None),
            P(),
            P(),
            P(("req", "exp"), None),
            P("exp", None, "ctx"),
            P("exp", None, "ctx"),
            P("exp", "ctx", None),
        ),
        out_specs=P(("req", "exp"), "ctx"),
        check_vma=False,
    )
```

```python
import functools
import math

import jax
import jax.numpy as jnp
from jax import lax
from jax.experimental import pallas as pl
from jax.experimental.pallas import tpu as pltpu
from jax.sharding import PartitionSpec as P

route_scale = 2.5


def on_device(
    queries,
    latent_cache,
    context_lengths,
    value_up,
    out_proj,
    residual,
    norm_gain,
    router,
    routes,
    expert_gate,
    expert_up,
    expert_down,
):
    latent_width = value_up.shape[1]
    value_width = value_up.shape[2]
    rope_width = queries.shape[3] - latent_width
    score_scale = 1.0 / math.sqrt(value_width + rope_width)
    heads_here = queries.shape[2]
    block_len = latent_cache.shape[1]
    device = lax.axis_index(("ctx", "exp"))
    all_queries = lax.all_gather(queries, ("ctx", "exp"), axis=2, tiled=True)
    scores = (
        jnp.einsum("rjhd,rtd->rjht", all_queries, latent_cache, preferred_element_type=jnp.float32)
        * score_scale
    )
    positions = device * block_len + jnp.arange(block_len, dtype=jnp.int32)
    visible_upto = context_lengths[:, None] + jnp.arange(2, dtype=jnp.int32)[None, :]
    visible = positions[None, None, None, :] < visible_upto[:, :, None, None]
    masked = jnp.where(visible, scores, -1e30)
    row_max = lax.pmax(jnp.max(masked, axis=-1), ("ctx", "exp"))
    weights = jnp.where(visible, jnp.exp(masked - row_max[..., None]), 0.0)
    weight_sum = jnp.sum(weights, axis=-1)
    latents = latent_cache[:, :, :latent_width]
    weighted = jnp.einsum(
        "rjht,rtl->rjhl", weights.astype(jnp.bfloat16), latents, preferred_element_type=jnp.float32
    )
    summed, sum_all = lax.psum((weighted, weight_sum), ("ctx", "exp"))
    own_weighted = lax.dynamic_slice_in_dim(summed, device * heads_here, heads_here, 2)
    own_sum = lax.dynamic_slice_in_dim(sum_all, device * heads_here, heads_here, 2)
    context = (own_weighted / own_sum[..., None]).astype(jnp.bfloat16)
    head_out = jnp.einsum(
        "rjhl,hlv->rjhv", context, value_up, preferred_element_type=jnp.float32
    ).astype(jnp.bfloat16)
    row_total = head_out.shape[0] * head_out.shape[1]
    head_out = head_out.reshape(row_total, heads_here * value_width)
    own_rows = residual.shape[0]
    owner_index = lax.axis_index("exp")
    attention_all = lax.psum(
        jnp.dot(head_out, out_proj, preferred_element_type=jnp.float32), ("ctx", "exp")
    )
    attention = lax.dynamic_slice_in_dim(attention_all, owner_index * own_rows, own_rows, 0)
    hidden = (residual.astype(jnp.float32) + attention).astype(jnp.bfloat16)
    hidden_wide = hidden.astype(jnp.float32)
    inverse = lax.rsqrt(jnp.mean(hidden_wide * hidden_wide, axis=-1, keepdims=True) + 1e-06)
    normed = (hidden_wide * inverse * norm_gain.astype(jnp.float32)).astype(jnp.bfloat16)
    affinity = jax.nn.sigmoid(jnp.dot(normed, router, preferred_element_type=jnp.float32))
    expert_count = router.shape[1]
    top_count = routes.shape[1]
    capacity = max(2, own_rows * top_count // expert_count)
    chosen = (
        routes[:, :, None] == jnp.arange(expert_count, dtype=jnp.int32)[None, None, :]
    ).astype(jnp.float32)
    picked = jnp.sum(chosen * affinity[:, None, :], axis=-1)
    gate_weights = route_scale * picked / jnp.sum(picked, axis=-1, keepdims=True)
    per_row = jnp.sum(chosen, axis=1)
    earlier = jnp.cumsum(per_row, axis=0) - per_row
    slot_index = jnp.sum(chosen * earlier[:, None, :], axis=-1)
    slot_hot = (
        slot_index[:, :, None] == jnp.arange(capacity, dtype=jnp.float32)[None, None, :]
    ).astype(jnp.float32)
    placement = chosen[:, :, :, None] * slot_hot[:, :, None, :]
    row_place = jnp.sum(placement, axis=1).reshape(own_rows, expert_count * capacity)
    gate_place = jnp.sum(placement * gate_weights[:, :, None, None], axis=1).reshape(
        own_rows, expert_count * capacity
    )
    model_width = normed.shape[1]
    outgoing = jnp.einsum(
        "rs,rd->sd", row_place.astype(jnp.bfloat16), normed, preferred_element_type=jnp.float32
    ).astype(jnp.bfloat16)
    outgoing = outgoing.reshape(expert_count, capacity, model_width)
    arrived = lax.all_to_all(outgoing, "exp", split_axis=0, concat_axis=0, tiled=True)
    gate_part = jnp.einsum(
        "scd,df->scf", arrived, expert_gate[0], preferred_element_type=jnp.float32
    )
    up_part = jnp.einsum("scd,df->scf", arrived, expert_up[0], preferred_element_type=jnp.float32)
    active = (jax.nn.silu(gate_part) * up_part).astype(jnp.bfloat16)
    partial_out = jnp.einsum(
        "scf,fd->scd", active, expert_down[0], preferred_element_type=jnp.float32
    )
    col_width = model_width // lax.axis_size("ctx")
    ctx_index = lax.axis_index("ctx")
    own_cols = lax.dynamic_slice_in_dim(hidden_wide, ctx_index * col_width, col_width, 1)
    full_sum = lax.psum(partial_out.astype(jnp.bfloat16), "ctx").astype(jnp.float32)
    returned = lax.all_to_all(
        full_sum.astype(jnp.bfloat16), "exp", split_axis=0, concat_axis=0, tiled=True
    ).astype(full_sum.dtype)
    returned = lax.dynamic_slice_in_dim(returned, ctx_index * col_width, col_width, 2)
    mixture = jnp.dot(
        gate_place,
        returned.reshape(expert_count * capacity, col_width),
        precision=lax.Precision.HIGHEST,
    )
    return (own_cols + mixture).astype(jnp.bfloat16)


MESH = pl.DeviceIdType.MESH
F32 = jnp.float32
BF16 = jnp.bfloat16
PAIR = 2
SLOTS = 3
BLOCKS = 4
PIECES = 2
AHEAD = 2


def lay_out(chunks):
    places, count = {}, 0
    for name, number in (
        ("own", 3), ("diag", 2), ("core", 4), ("stat", 7), ("fold", 1), ("cross", 2), ("last", 2),
    ):
        places[name] = (count, number)
        count += number * chunks
    for name, number in (
        ("route", 3), ("swap", 2 * PIECES), ("rows", 6 * PIECES), ("hid", 4 * PIECES),
        ("hidfwd", 3 * PIECES),
    ):
        places[name] = (count, number)
        count += number
    return places, count


def contract(a, b, da, db):
    return lax.dot_general(a, b, (((da,), (db,)), ((), ())), preferred_element_type=F32)


def layer_kernel(
    lens, q_hbm, cache_hbm, vu_hbm, op_hbm, res, gain, router, routes, eg_hbm, eu_hbm, ed_hbm,
    out,
    qbuf, cbuf, acc, mown, stat, norm, crx, x2, y2, x3, y3, ctx2, vu, ho, wslot, eg,
    sbuf, wbuf, mz, spread, chosen, pbuf, prx, tsum, rrx, hid, xn, act, gcol,
    send, recv, csem, wsem, osem,
):
    chunks, _, heads_rows, width = q_hbm.shape
    heads = heads_rows // 2
    block_len, latent = cache_hbm.shape[3], vu.shape[1]
    vdim = vu.shape[2]
    places, _ = lay_out(chunks)
    scale = 1.0 / math.sqrt(vdim + width - latent)
    piece = hid.shape[4]
    half = piece * PIECES
    cols = half * 2 // BLOCKS
    per_half = BLOCKS // 2
    c = lax.axis_index("ctx")
    e = lax.axis_index("exp")
    ey, ex = e // 2, e % 2
    me = c * 4 + e
    ex_n = e + 1 - 2 * ex
    ey_n = e + 2 - 4 * ey
    ed_n = 3 - e
    others = (ex_n, ey_n, ed_n)
    peers = [(1 - c, e)] + [(c, o) for o in others] + [(1 - c, o) for o in others]

    def remote(kind, g, k, src, dst, to):
        first, stride = places[kind]
        place = first + g * stride + k
        return pltpu.make_async_remote_copy(
            src_ref=src, dst_ref=dst, send_sem=send.at[place], recv_sem=recv.at[place],
            device_id={"ctx": to[0], "exp": to[1]}, device_id_type=MESH,
        )

    core_to, x_to, y_to = (1 - c, e), (c, ex_n), (c, ey_n)

    def own_copy(g, k):
        return remote("own", g, k, q_hbm.at[g], qbuf.at[g, me], (core_to, x_to, y_to)[k])

    def diag_copy(g, k):
        source = c * 4 + (ex_n if k == 0 else ey_n)
        view = qbuf.at[g, source, k]
        return remote("diag", g, k, view, view, (y_to, x_to)[k])

    def core_copy(g, k):
        source = c * 4 + (ex_n, ey_n, ed_n, ed_n)[k]
        view = qbuf.at[g, source] if k < 2 else qbuf.at[g, source, k - 2]
        return remote("core", g, k, view, view, core_to)

    def stat_copy(g, k):
        return remote("stat", g, k, stat.at[g, me], stat.at[g, me], peers[k])

    def fold_copy(g):
        return remote("fold", g, 0, norm.at[g, 1 - c], crx.at[g], core_to)

    def cross_copy(g, k):
        if k == 0:
            return remote("cross", g, 0, crx.at[g, :, 1 - ex, 0], x2.at[g], x_to)
        return remote("cross", g, 1, crx.at[g, 1 - ey, :, 1], y2.at[g], y_to)

    def last_copy(g, k):
        if k == 0:
            return remote("last", g, 0, x2.at[g, 1 - ey], y3.at[g], y_to)
        return remote("last", g, 1, y2.at[g, 1 - ex], x3.at[g], x_to)

    def route_copy(k):
        return remote("route", 0, k, chosen.at[e], chosen.at[e], (c, others[k]))

    def swap_copy(p, j):
        return remote("swap", 0, p * PIECES + j, pbuf.at[p, 0, j], prx.at[p, j], core_to)

    def rows_copy(p, j, k):
        return remote(
            "rows", 0, (p * PIECES + j) * 3 + k, tsum.at[p, j, others[k]], rrx.at[p, j, k],
            (c, others[k]),
        )

    def hid_copy(j, k):
        to = (x_to, y_to, (c, ed_n), core_to)[k]
        return remote("hid", 0, j * 4 + k, hid.at[c, j, e], hid.at[c, j, e], to)

    def hidfwd_copy(j, k):
        view = hid.at[c, j, others[k]]
        return remote("hidfwd", 0, j * 3 + k, view, view, core_to)

    def cache_copy(g):
        return pltpu.make_async_copy(cache_hbm.at[g], cbuf.at[g % 2], csem.at[g % 2])

    def column(i):
        side = jnp.where(i < per_half, 1 - c, c)
        return pl.multiple_of((side * per_half + i % per_half) * cols, cols)

    def op_copy(i):
        return pltpu.make_async_copy(
            op_hbm.at[:, pl.ds(column(i), cols)], wslot.at[i % SLOTS], osem.at[i % SLOTS]
        )

    depth = ed_hbm.shape[0]

    def down_copy(i):
        place = pl.ds(i * depth, depth)
        return pltpu.make_async_copy(
            ed_hbm.at[:, pl.ds(column(i), cols)], wslot.at[1, place], wsem.at[4 + i]
        )

    own_q = pltpu.make_async_copy(q_hbm, qbuf.at[:, me], wsem.at[0])
    vu_copy = pltpu.make_async_copy(vu_hbm, vu, wsem.at[1])
    eg_copy = pltpu.make_async_copy(eg_hbm, eg, wsem.at[2])

    def part_of(i):
        side, j = (c if i < PIECES else 1 - c), i % PIECES
        return side, j, pl.ds(pl.multiple_of(side * half + j * piece, piece), piece)

    def up_place(i):
        width = eu_hbm.shape[1]
        return wslot.at[2 if i < 3 else 0, 0:piece, i % 3 * width : (i % 3 + 1) * width]

    def up_copy(i):
        return pltpu.make_async_copy(
            eu_hbm.at[part_of(i)[2], :], up_place(i), wsem.at[4 + BLOCKS + i]
        )


    own_q.start()
    cache_copy(0).start()
    lanes = lax.broadcasted_iota(jnp.int32, chosen.shape[1:], 1)
    square = (routes.shape[1], routes.shape[1])
    diagonal = lax.broadcasted_iota(jnp.int32, square, 0) == lax.broadcasted_iota(jnp.int32, square, 1)
    named = jnp.zeros(lanes.shape, F32)
    for k in range(routes.shape[0]):
        choice = jnp.where(diagonal, routes[k : k + 1, :].astype(F32), 0.0)
        named = named + (jnp.sum(choice, axis=1, keepdims=True) == lanes.astype(F32)).astype(F32)
    chosen[e] = named

    barrier = pltpu.get_barrier_semaphore()
    for to in peers:
        pl.semaphore_signal(
            barrier, inc=1, device_id={"ctx": to[0], "exp": to[1]}, device_id_type=MESH
        )
    pl.semaphore_wait(barrier, len(peers))

    for g in range(AHEAD):
        for k in range(3):
            own_copy(g, k).start()
    for k in range(3):
        route_copy(k).start()
    vu_copy.start()
    lanes_of = piece // 128
    for i in range(2 * PIECES):
        spread[i] = gain[i * lanes_of : (i + 1) * lanes_of, :].astype(F32)
    own_q.wait()

    rows = 8 * heads_rows

    def attend(g):
        cache_copy(g).wait()

        @pl.when(g + 1 < chunks)
        def _():
            cache_copy(g + 1).start()

        first = lax.broadcasted_iota(jnp.int32, (heads_rows, 128), 1) < 64
        position = me * block_len + lax.broadcasted_iota(jnp.int32, (1, block_len), 1)
        for r in range(PAIR):
            q = qbuf[g, :, r].reshape(rows, width)
            sbuf[r] = jnp.dot(q, cbuf[g % 2, r], preferred_element_type=F32)
        for r in range(PAIR):
            length = lens[g * PAIR + r]
            bias = jnp.concatenate(
                [
                    jnp.broadcast_to(
                        jnp.where(position < length + j, 0.0, -1e30), (heads, block_len)
                    )
                    for j in range(2)
                ],
                axis=0,
            )
            for d in range(8):
                place = slice(d * heads_rows, (d + 1) * heads_rows)
                s = sbuf[r, place] + bias
                m = jnp.max(s, axis=1, keepdims=True)
                p = jnp.exp((s - m) * scale)
                total = jnp.sum(p, axis=1, keepdims=True)
                wbuf[r, place] = p.astype(BF16)
                m = m * scale
                z = jnp.where(m > -1e25, m + jnp.log(total), -1e30)
                mz[r, place] = jnp.where(first, jnp.where(m > -1e25, m, -1e30), z)
            flat = jnp.transpose(mz[r])
            mown[g % 2, r : r + 1] = flat[0:1]
            stat[g, me, r : r + 1] = flat[64:65]
        for k in range(7):
            stat_copy(g, k).start()
        for r in range(PAIR):
            acc[g % 2, r] = contract(wbuf[r], cbuf[g % 2, r, :latent], 1, 1)

    def normalise(g):
        for k in range(7):
            stat_copy(g, k).wait_recv()
        for r in range(PAIR):
            z = stat[g, :, r]
            top = jnp.max(z, axis=0, keepdims=True)
            whole = top + jnp.log(jnp.sum(jnp.exp(z - top), axis=0, keepdims=True))
            factor = jnp.exp(mown[g % 2, r : r + 1] - whole)
            factor = jnp.transpose(jnp.broadcast_to(factor, (128, rows)))
            for k in range(latent // 128):
                part = acc[g % 2, r, :, k * 128 : (k + 1) * 128] * factor
                norm[g, :, :, :, r, :, k * 128 : (k + 1) * 128] = part.astype(BF16).reshape(
                    2, 2, 2, heads_rows, 128
                )
        fold_copy(g).start()

    def fold(g):
        fold_copy(g).wait_recv()
        crx[g] = (crx[g].astype(F32) + norm[g, c].astype(F32)).astype(BF16)
        cross_copy(g, 0).start()
        cross_copy(g, 1).start()

    def cross(g):
        cross_copy(g, 0).wait_recv()
        x2[g] = (x2[g].astype(F32) + crx[g, :, ex, 0].astype(F32)).astype(BF16)
        last_copy(g, 0).start()
        cross_copy(g, 1).wait_recv()
        y2[g] = (y2[g].astype(F32) + crx[g, ey, :, 1].astype(F32)).astype(BF16)
        last_copy(g, 1).start()

    def last(g):
        last_copy(g, 0).wait_recv()
        ctx2[g % 2, 0] = (x2[g, ey].astype(F32) + y3[g].astype(F32)).astype(BF16)
        last_copy(g, 1).wait_recv()
        ctx2[g % 2, 1] = (y2[g, ex].astype(F32) + x3[g].astype(F32)).astype(BF16)

        @pl.when(g % 2 == 1)
        def _():
            both = ctx2[...].reshape(4 * heads_rows, latent)
            for h in range(heads):
                every = jnp.dot(both, vu[h], preferred_element_type=F32).reshape(8, heads, vdim)
                mine = lax.broadcasted_iota(jnp.int32, every.shape, 1) == h
                place = pl.ds(pl.multiple_of((g // 2) * 8, 8), 8)
                ho[place, h * vdim : (h + 1) * vdim] = jnp.sum(
                    jnp.where(mine, every, 0.0), axis=1
                )

    vu_copy.wait()

    def step(s, _):
        def at(lag, run):
            @pl.when((s >= lag) & (s < chunks + lag))
            def _():
                run(s - lag)

        def forward(g):
            own_copy(g, 1).wait_recv()
            diag_copy(g, 0).start()
            core_copy(g, 0).start()
            own_copy(g, 2).wait_recv()
            diag_copy(g, 1).start()
            core_copy(g, 1).start()

        def forward_diag(g):
            for k in range(2):
                diag_copy(g, k).wait_recv()
                core_copy(g, 2 + k).start()

        def attend_when_here(g):
            own_copy(g, 0).wait_recv()
            for k in range(4):
                core_copy(g, k).wait_recv()
            attend(g)

        at(0, forward)
        at(1, forward_diag)

        @pl.when(s + AHEAD < chunks)
        def _():
            for k in range(3):
                own_copy(s + AHEAD, k).start()

        at(4, normalise)
        at(5, fold)
        at(6, cross)
        at(7, last)
        at(2, attend_when_here)

        @pl.when(s < SLOTS)
        def _():
            op_copy(s).start()

        @pl.when(s == SLOTS)
        def _():
            eg_copy.start()

        return 0

    lax.fori_loop(0, chunks + 7, step, 0)

    own_rows = res.shape[0]

    per_piece = per_half // PIECES

    def put(p, i, part):
        place = slice(i % per_piece * cols, (i % per_piece + 1) * cols)
        j = i % per_half // per_piece
        pbuf[p, i // per_half, j, :, :, place] = part.astype(BF16).reshape(4, own_rows, cols)
        if i % per_piece == per_piece - 1:
            if i < per_half:
                swap_copy(p, j).start()
            else:
                swap_copy(p, j).wait_recv()
                total = prx[p, j].astype(F32) + pbuf[p, 1, j].astype(F32)
                tsum[p, j] = total.astype(BF16)
                for k in (2, 0, 1):
                    rows_copy(p, j, k).start()

    def rows_total(p, j):
        total = tsum[p, j, e].astype(F32)
        for k in range(3):
            rows_copy(p, j, k).wait_recv()
            total = total + rrx[p, j, k].astype(F32)
        return total

    head_out = ho[...].astype(BF16)
    for i in range(BLOCKS):
        op_copy(i).wait()
        put(0, i, jnp.dot(head_out, wslot[i % SLOTS], preferred_element_type=F32))
        if i + SLOTS < BLOCKS:
            op_copy(i + SLOTS).start()
        if i == 1:
            for k in range(BLOCKS):
                down_copy(k).start()
        if i >= 2:
            for k in range(3) if i == 2 else (3,):
                up_copy(k).start()

    for j in range(PIECES):
        own_cols = pl.ds(pl.multiple_of(c * half + j * piece, piece), piece)
        hid[c, j, e] = (res[:, own_cols].astype(F32) + rows_total(0, j)).astype(BF16)
        for k in (2, 0, 1, 3):
            hid_copy(j, k).start()
    eg_copy.wait()

    squares, logits, gate_part, up_part = 0.0, 0.0, 0.0, 0.0
    for i in range(2 * PIECES):
        side, j, span = part_of(i)
        if i < PIECES:
            for k in range(3):
                hid_copy(j, k).wait_recv()
                hidfwd_copy(j, k).start()
        else:
            hid_copy(j, 3).wait_recv()
            for k in range(3):
                hidfwd_copy(j, k).wait_recv()
        wide = hid[side, j].astype(F32).reshape(4 * own_rows, piece)
        squares = squares + jnp.sum(wide * wide, axis=-1, keepdims=True)
        for k in range(piece // 128):
            lane = slice(k * 128, (k + 1) * 128)
            xn[i, :, lane] = (wide[:, lane] * spread[side * PIECES + j, k : k + 1]).astype(BF16)
        logits = logits + contract(xn[i], router[:, span], 1, 1)
        gate_part = gate_part + jnp.dot(xn[i], eg[span, :], preferred_element_type=F32)
        up_copy(i).wait()
        up_part = up_part + jnp.dot(xn[i], up_place(i)[...], preferred_element_type=F32)
    inverse = lax.rsqrt(squares / (2 * half) + 1e-06)
    gate_part, up_part = gate_part * inverse, up_part * inverse
    act[...] = (gate_part / (1.0 + jnp.exp(-gate_part)) * up_part).astype(BF16)
    for k in range(3):
        route_copy(k).wait_recv()
    affinity = jax.nn.sigmoid(logits * inverse)
    picked = affinity * chosen[...].reshape(4 * own_rows, 128)[:, : affinity.shape[1]]
    weights = route_scale * picked / jnp.sum(picked, axis=-1, keepdims=True)
    mine = lax.broadcasted_iota(jnp.int32, weights.shape, 1) == e
    gcol[...] = jnp.broadcast_to(
        jnp.sum(jnp.where(mine, weights, 0.0), axis=-1, keepdims=True), gcol.shape
    )

    for i in range(BLOCKS):
        down_copy(i).wait()
        block = wslot[1, i * depth : (i + 1) * depth]
        put(1, i, jnp.dot(act[...], block, preferred_element_type=F32) * gcol[:, 0:1])
    for j in range(PIECES):
        total = hid[c, j, e].astype(F32) + rows_total(1, j)
        out[:, j * piece : (j + 1) * piece] = total.astype(BF16)

    def drain(g, _):
        for k in range(3):
            own_copy(g, k).wait_send()
        for k in range(2):
            diag_copy(g, k).wait_send()
            cross_copy(g, k).wait_send()
            last_copy(g, k).wait_send()
        for k in range(4):
            core_copy(g, k).wait_send()
        for k in range(7):
            stat_copy(g, k).wait_send()
        fold_copy(g).wait_send()
        return 0

    lax.fori_loop(0, chunks, drain, 0)
    for k in range(3):
        route_copy(k).wait_send()
        for j in range(PIECES):
            hidfwd_copy(j, k).wait_send()
            rows_copy(0, j, k).wait_send()
            rows_copy(1, j, k).wait_send()
    for j in range(PIECES):
        for k in range(4):
            hid_copy(j, k).wait_send()
        for p in range(2):
            swap_copy(p, j).wait_send()


def fused_on_device(
    queries, latent_cache, context_lengths, value_up, out_proj, residual, norm_gain, router,
    routes, expert_gate, expert_up, expert_down,
):
    reqs, verify, heads, width = queries.shape
    chunks = reqs // PAIR
    hr = verify * heads
    _, block_len, _ = latent_cache.shape
    _, latent, vdim = value_up.shape
    own_rows, model = residual.shape
    half = model // 2
    piece = half // PIECES
    ff = expert_down.shape[1]
    rows = 8 * hr
    _, count = lay_out(chunks)
    vmem, anywhere = pl.BlockSpec(memory_space=pltpu.VMEM), pl.BlockSpec(memory_space=pl.ANY)
    scratch = [
        pltpu.VMEM((chunks, 8, PAIR, hr, width), BF16),
        pltpu.VMEM((2, PAIR, width, block_len), BF16),
        pltpu.VMEM((2, PAIR, rows, latent), F32),
        pltpu.VMEM((2, PAIR, rows), F32),
        pltpu.VMEM((chunks, 8, PAIR, rows), F32),
        pltpu.VMEM((chunks, 2, 2, 2, PAIR, hr, latent), BF16),
        pltpu.VMEM((chunks, 2, 2, PAIR, hr, latent), BF16),
        pltpu.VMEM((chunks, 2, hr, latent), BF16),
        pltpu.VMEM((chunks, 2, hr, latent), BF16),
        pltpu.VMEM((chunks, hr, latent), BF16),
        pltpu.VMEM((chunks, hr, latent), BF16),
        pltpu.VMEM((2, PAIR, hr, latent), BF16),
        pltpu.VMEM((heads, latent, vdim), BF16),
        pltpu.VMEM((reqs * verify, heads * vdim), F32),
        pltpu.VMEM((SLOTS, heads * vdim, model // BLOCKS), BF16),
        pltpu.VMEM((model, ff), BF16),
        pltpu.VMEM((PAIR, rows, block_len), F32),
        pltpu.VMEM((PAIR, rows, block_len), BF16),
        pltpu.VMEM((PAIR, rows, 128), F32),
        pltpu.VMEM((2 * PIECES, piece // 128, 128), F32),
        pltpu.VMEM((4, own_rows, 128), F32),
        pltpu.VMEM((2, 2, PIECES, 4, own_rows, piece), BF16),
        pltpu.VMEM((2, PIECES, 4, own_rows, piece), BF16),
        pltpu.VMEM((2, PIECES, 4, own_rows, piece), BF16),
        pltpu.VMEM((2, PIECES, 3, own_rows, piece), BF16),
        pltpu.VMEM((2, PIECES, 4, own_rows, piece), BF16),
        pltpu.VMEM((2 * PIECES, 4 * own_rows, piece), BF16),
        pltpu.VMEM((4 * own_rows, ff), BF16),
        pltpu.VMEM((4 * own_rows, 128), F32),
        pltpu.SemaphoreType.DMA((count,)),
        pltpu.SemaphoreType.DMA((count,)),
        pltpu.SemaphoreType.DMA((2,)),
        pltpu.SemaphoreType.DMA((4 + BLOCKS + 2 * PIECES,)),
        pltpu.SemaphoreType.DMA((SLOTS,)),
    ]
    return pl.pallas_call(
        layer_kernel,
        out_shape=jax.ShapeDtypeStruct((own_rows, half), BF16),
        in_specs=[pl.BlockSpec(memory_space=pltpu.SMEM)] + [anywhere] * 4 + [vmem] * 2
        + [vmem] * 2 + [anywhere] * 3,
        out_specs=vmem,
        scratch_shapes=scratch,
        compiler_params=pltpu.CompilerParams(
            collective_id=0, has_side_effects=True, vmem_limit_bytes=62 * 1024 * 1024
        ),
        cost_estimate=pl.CostEstimate(
            flops=6_000_000_000, bytes_accessed=64_000_000, transcendentals=2_000_000
        ),
    )(
        context_lengths,
        queries.reshape(chunks, PAIR, hr, width),
        jnp.swapaxes(latent_cache, 1, 2).reshape(chunks, PAIR, width, block_len),
        value_up,
        out_proj,
        residual,
        norm_gain.reshape(model // 128, 128),
        router.T,
        routes.T,
        expert_gate[0],
        expert_up[0],
        expert_down[0],
    )


def solution(mesh):
    grouped = mesh.shape["ctx"] == 2 and mesh.shape["exp"] == 4
    body = fused_on_device if grouped else on_device
    return jax.shard_map(
        body,
        mesh=mesh,
        in_specs=(
            P("req", None, ("ctx", "exp"), None),
            P("req", ("ctx", "exp"), None),
            P("req"),
            P(("ctx", "exp"), None, None),
            P(("ctx", "exp"), None),
            P(("req", "exp"), None),
            P(),
            P(),
            P(("req", "exp"), None),
            P("exp", None, "ctx"),
            P("exp", None, "ctx"),
            P("exp", "ctx", None),
        ),
        out_specs=P(("req", "exp"), "ctx"),
        check_vma=False,
    )
```

```python
import functools
import math

import jax
import jax.numpy as jnp
from jax import lax
from jax.experimental import pallas as pl
from jax.experimental.pallas import tpu as pltpu
from jax.sharding import PartitionSpec as P

route_scale = 2.5


def on_device(
    queries,
    latent_cache,
    context_lengths,
    value_up,
    out_proj,
    residual,
    norm_gain,
    router,
    routes,
    expert_gate,
    expert_up,
    expert_down,
):
    latent_width = value_up.shape[1]
    value_width = value_up.shape[2]
    rope_width = queries.shape[3] - latent_width
    score_scale = 1.0 / math.sqrt(value_width + rope_width)
    heads_here = queries.shape[2]
    block_len = latent_cache.shape[1]
    device = lax.axis_index(("ctx", "exp"))
    all_queries = lax.all_gather(queries, ("ctx", "exp"), axis=2, tiled=True)
    scores = (
        jnp.einsum("rjhd,rtd->rjht", all_queries, latent_cache, preferred_element_type=jnp.float32)
        * score_scale
    )
    positions = device * block_len + jnp.arange(block_len, dtype=jnp.int32)
    visible_upto = context_lengths[:, None] + jnp.arange(2, dtype=jnp.int32)[None, :]
    visible = positions[None, None, None, :] < visible_upto[:, :, None, None]
    masked = jnp.where(visible, scores, -1e30)
    row_max = lax.pmax(jnp.max(masked, axis=-1), ("ctx", "exp"))
    weights = jnp.where(visible, jnp.exp(masked - row_max[..., None]), 0.0)
    weight_sum = jnp.sum(weights, axis=-1)
    latents = latent_cache[:, :, :latent_width]
    weighted = jnp.einsum(
        "rjht,rtl->rjhl", weights.astype(jnp.bfloat16), latents, preferred_element_type=jnp.float32
    )
    summed, sum_all = lax.psum((weighted, weight_sum), ("ctx", "exp"))
    own_weighted = lax.dynamic_slice_in_dim(summed, device * heads_here, heads_here, 2)
    own_sum = lax.dynamic_slice_in_dim(sum_all, device * heads_here, heads_here, 2)
    context = (own_weighted / own_sum[..., None]).astype(jnp.bfloat16)
    head_out = jnp.einsum(
        "rjhl,hlv->rjhv", context, value_up, preferred_element_type=jnp.float32
    ).astype(jnp.bfloat16)
    row_total = head_out.shape[0] * head_out.shape[1]
    head_out = head_out.reshape(row_total, heads_here * value_width)
    own_rows = residual.shape[0]
    owner_index = lax.axis_index("exp")
    attention_all = lax.psum(
        jnp.dot(head_out, out_proj, preferred_element_type=jnp.float32), ("ctx", "exp")
    )
    attention = lax.dynamic_slice_in_dim(attention_all, owner_index * own_rows, own_rows, 0)
    hidden = (residual.astype(jnp.float32) + attention).astype(jnp.bfloat16)
    hidden_wide = hidden.astype(jnp.float32)
    inverse = lax.rsqrt(jnp.mean(hidden_wide * hidden_wide, axis=-1, keepdims=True) + 1e-06)
    normed = (hidden_wide * inverse * norm_gain.astype(jnp.float32)).astype(jnp.bfloat16)
    affinity = jax.nn.sigmoid(jnp.dot(normed, router, preferred_element_type=jnp.float32))
    expert_count = router.shape[1]
    top_count = routes.shape[1]
    capacity = max(2, own_rows * top_count // expert_count)
    chosen = (
        routes[:, :, None] == jnp.arange(expert_count, dtype=jnp.int32)[None, None, :]
    ).astype(jnp.float32)
    picked = jnp.sum(chosen * affinity[:, None, :], axis=-1)
    gate_weights = route_scale * picked / jnp.sum(picked, axis=-1, keepdims=True)
    per_row = jnp.sum(chosen, axis=1)
    earlier = jnp.cumsum(per_row, axis=0) - per_row
    slot_index = jnp.sum(chosen * earlier[:, None, :], axis=-1)
    slot_hot = (
        slot_index[:, :, None] == jnp.arange(capacity, dtype=jnp.float32)[None, None, :]
    ).astype(jnp.float32)
    placement = chosen[:, :, :, None] * slot_hot[:, :, None, :]
    row_place = jnp.sum(placement, axis=1).reshape(own_rows, expert_count * capacity)
    gate_place = jnp.sum(placement * gate_weights[:, :, None, None], axis=1).reshape(
        own_rows, expert_count * capacity
    )
    model_width = normed.shape[1]
    outgoing = jnp.einsum(
        "rs,rd->sd", row_place.astype(jnp.bfloat16), normed, preferred_element_type=jnp.float32
    ).astype(jnp.bfloat16)
    outgoing = outgoing.reshape(expert_count, capacity, model_width)
    arrived = lax.all_to_all(outgoing, "exp", split_axis=0, concat_axis=0, tiled=True)
    gate_part = jnp.einsum(
        "scd,df->scf", arrived, expert_gate[0], preferred_element_type=jnp.float32
    )
    up_part = jnp.einsum("scd,df->scf", arrived, expert_up[0], preferred_element_type=jnp.float32)
    active = (jax.nn.silu(gate_part) * up_part).astype(jnp.bfloat16)
    partial_out = jnp.einsum(
        "scf,fd->scd", active, expert_down[0], preferred_element_type=jnp.float32
    )
    col_width = model_width // lax.axis_size("ctx")
    ctx_index = lax.axis_index("ctx")
    own_cols = lax.dynamic_slice_in_dim(hidden_wide, ctx_index * col_width, col_width, 1)
    full_sum = lax.psum(partial_out.astype(jnp.bfloat16), "ctx").astype(jnp.float32)
    returned = lax.all_to_all(
        full_sum.astype(jnp.bfloat16), "exp", split_axis=0, concat_axis=0, tiled=True
    ).astype(full_sum.dtype)
    returned = lax.dynamic_slice_in_dim(returned, ctx_index * col_width, col_width, 2)
    mixture = jnp.dot(
        gate_place,
        returned.reshape(expert_count * capacity, col_width),
        precision=lax.Precision.HIGHEST,
    )
    return (own_cols + mixture).astype(jnp.bfloat16)


MESH = pl.DeviceIdType.MESH
F32 = jnp.float32
BF16 = jnp.bfloat16
PAIR = 2
SLOTS = 3
BLOCKS = 4
PIECES = 2
AHEAD = 2


def lay_out(chunks):
    places, count = {}, 0
    for name, number in (
        ("own", 3), ("diag", 2), ("core", 4), ("stat", 7), ("fold", 1), ("cross", 2), ("last", 2),
    ):
        places[name] = (count, number)
        count += number * chunks
    for name, number in (
        ("route", 3), ("swap", 2 * PIECES), ("rows", 6 * PIECES), ("hid", 4 * PIECES),
        ("hidfwd", 3 * PIECES),
    ):
        places[name] = (count, number)
        count += number
    return places, count


def contract(a, b, da, db):
    return lax.dot_general(a, b, (((da,), (db,)), ((), ())), preferred_element_type=F32)


def layer_kernel(
    lens, q_hbm, cache_hbm, vu_hbm, op_hbm, res, gain, router, routes, eg_hbm, eu_hbm, ed_hbm,
    out,
    qbuf, cbuf, acc, mown, stat, norm, crx, x2, y2, x3, y3, ctx2, vu, ho, wslot, eg,
    sbuf, wbuf, mz, spread, chosen, pbuf, prx, tsum, rrx, hid, xn, act, gcol,
    send, recv, csem, wsem, osem,
):
    chunks, _, heads_rows, width = q_hbm.shape
    heads = heads_rows // 2
    block_len, latent = cache_hbm.shape[3], vu.shape[1]
    vdim = vu.shape[2]
    places, _ = lay_out(chunks)
    scale = 1.0 / math.sqrt(vdim + width - latent)
    piece = hid.shape[4]
    half = piece * PIECES
    cols = half * 2 // BLOCKS
    per_half = BLOCKS // 2
    c = lax.axis_index("ctx")
    e = lax.axis_index("exp")
    ey, ex = e // 2, e % 2
    me = c * 4 + e
    ex_n = e + 1 - 2 * ex
    ey_n = e + 2 - 4 * ey
    ed_n = 3 - e
    others = (ex_n, ey_n, ed_n)
    peers = [(1 - c, e)] + [(c, o) for o in others] + [(1 - c, o) for o in others]

    def remote(kind, g, k, src, dst, to):
        first, stride = places[kind]
        place = first + g * stride + k
        return pltpu.make_async_remote_copy(
            src_ref=src, dst_ref=dst, send_sem=send.at[place], recv_sem=recv.at[place],
            device_id={"ctx": to[0], "exp": to[1]}, device_id_type=MESH,
        )

    core_to, x_to, y_to = (1 - c, e), (c, ex_n), (c, ey_n)

    def own_copy(g, k):
        return remote("own", g, k, q_hbm.at[g], qbuf.at[g, me], (core_to, x_to, y_to)[k])

    def diag_copy(g, k):
        source = c * 4 + (ex_n if k == 0 else ey_n)
        view = qbuf.at[g, source, k]
        return remote("diag", g, k, view, view, (y_to, x_to)[k])

    def core_copy(g, k):
        source = c * 4 + (ex_n, ey_n, ed_n, ed_n)[k]
        view = qbuf.at[g, source] if k < 2 else qbuf.at[g, source, k - 2]
        return remote("core", g, k, view, view, core_to)

    def stat_copy(g, k):
        return remote("stat", g, k, stat.at[g, me], stat.at[g, me], peers[k])

    def fold_copy(g):
        return remote("fold", g, 0, norm.at[g, 1 - c], crx.at[g], core_to)

    def cross_copy(g, k):
        if k == 0:
            return remote("cross", g, 0, crx.at[g, :, 1 - ex, 0], x2.at[g], x_to)
        return remote("cross", g, 1, crx.at[g, 1 - ey, :, 1], y2.at[g], y_to)

    def last_copy(g, k):
        if k == 0:
            return remote("last", g, 0, x2.at[g, 1 - ey], y3.at[g], y_to)
        return remote("last", g, 1, y2.at[g, 1 - ex], x3.at[g], x_to)

    def route_copy(k):
        return remote("route", 0, k, chosen.at[e], chosen.at[e], (c, others[k]))

    def swap_copy(p, j):
        return remote("swap", 0, p * PIECES + j, pbuf.at[p, 0, j], prx.at[p, j], core_to)

    def rows_copy(p, j, k):
        return remote(
            "rows", 0, (p * PIECES + j) * 3 + k, tsum.at[p, j, others[k]], rrx.at[p, j, k],
            (c, others[k]),
        )

    def hid_copy(j, k):
        to = (x_to, y_to, (c, ed_n), core_to)[k]
        return remote("hid", 0, j * 4 + k, hid.at[c, j, e], hid.at[c, j, e], to)

    def hidfwd_copy(j, k):
        view = hid.at[c, j, others[k]]
        return remote("hidfwd", 0, j * 3 + k, view, view, core_to)

    def cache_copy(g):
        return pltpu.make_async_copy(cache_hbm.at[g], cbuf.at[g % 2], csem.at[g % 2])

    def column(i):
        side = jnp.where(i < per_half, 1 - c, c)
        return pl.multiple_of((side * per_half + i % per_half) * cols, cols)

    def op_copy(i):
        return pltpu.make_async_copy(
            op_hbm.at[:, pl.ds(column(i), cols)], wslot.at[i % SLOTS], osem.at[i % SLOTS]
        )

    depth = ed_hbm.shape[0]

    def down_copy(i):
        place = pl.ds(i * depth, depth)
        return pltpu.make_async_copy(
            ed_hbm.at[:, pl.ds(column(i), cols)], wslot.at[1, place], wsem.at[4 + i]
        )

    own_q = pltpu.make_async_copy(q_hbm, qbuf.at[:, me], wsem.at[0])
    vu_copy = pltpu.make_async_copy(vu_hbm, vu, wsem.at[1])
    eg_copy = pltpu.make_async_copy(eg_hbm, eg, wsem.at[2])

    def part_of(i):
        side, j = (c if i < PIECES else 1 - c), i % PIECES
        return side, j, pl.ds(pl.multiple_of(side * half + j * piece, piece), piece)

    def up_place(i):
        width = eu_hbm.shape[1]
        return wslot.at[2 if i < 3 else 0, 0:piece, i % 3 * width : (i % 3 + 1) * width]

    def up_copy(i):
        return pltpu.make_async_copy(
            eu_hbm.at[part_of(i)[2], :], up_place(i), wsem.at[4 + BLOCKS + i]
        )


    own_q.start()
    cache_copy(0).start()
    lanes = lax.broadcasted_iota(jnp.int32, chosen.shape[1:], 1)
    square = (routes.shape[1], routes.shape[1])
    diagonal = lax.broadcasted_iota(jnp.int32, square, 0) == lax.broadcasted_iota(jnp.int32, square, 1)
    named = jnp.zeros(lanes.shape, F32)
    for k in range(routes.shape[0]):
        choice = jnp.where(diagonal, routes[k : k + 1, :].astype(F32), 0.0)
        named = named + (jnp.sum(choice, axis=1, keepdims=True) == lanes.astype(F32)).astype(F32)
    chosen[e] = named

    barrier = pltpu.get_barrier_semaphore()
    for to in peers:
        pl.semaphore_signal(
            barrier, inc=1, device_id={"ctx": to[0], "exp": to[1]}, device_id_type=MESH
        )
    pl.semaphore_wait(barrier, len(peers))

    for g in range(AHEAD):
        for k in range(3):
            own_copy(g, k).start()
    for k in range(3):
        route_copy(k).start()
    vu_copy.start()
    lanes_of = piece // 128
    for i in range(2 * PIECES):
        spread[i] = gain[i * lanes_of : (i + 1) * lanes_of, :].astype(F32)
    own_q.wait()

    rows = 8 * heads_rows

    def attend(g):
        cache_copy(g).wait()

        @pl.when(g + 1 < chunks)
        def _():
            cache_copy(g + 1).start()

        first = lax.broadcasted_iota(jnp.int32, (heads_rows, 128), 1) < 64
        position = me * block_len + lax.broadcasted_iota(jnp.int32, (1, block_len), 1)
        for r in range(PAIR):
            q = qbuf[g, :, r].reshape(rows, width)
            sbuf[r] = jnp.dot(q, cbuf[g % 2, r], preferred_element_type=F32)
        for r in range(PAIR):
            length = lens[g * PAIR + r]
            bias = jnp.concatenate(
                [
                    jnp.broadcast_to(
                        jnp.where(position < length + j, 0.0, -1e30), (heads, block_len)
                    )
                    for j in range(2)
                ],
                axis=0,
            )
            for d in range(8):
                place = slice(d * heads_rows, (d + 1) * heads_rows)
                s = sbuf[r, place] + bias
                m = jnp.max(s, axis=1, keepdims=True)
                p = jnp.exp((s - m) * scale)
                total = jnp.sum(p, axis=1, keepdims=True)
                wbuf[r, place] = p.astype(BF16)
                m = m * scale
                z = jnp.where(m > -1e25, m + jnp.log(total), -1e30)
                mz[r, place] = jnp.where(first, jnp.where(m > -1e25, m, -1e30), z)
            flat = jnp.transpose(mz[r])
            mown[g % 2, r : r + 1] = flat[0:1]
            stat[g, me, r : r + 1] = flat[64:65]
        for k in range(7):
            stat_copy(g, k).start()
        for r in range(PAIR):
            acc[g % 2, r] = contract(wbuf[r], cbuf[g % 2, r, :latent], 1, 1)

    def normalise(g):
        for k in range(7):
            stat_copy(g, k).wait_recv()
        for r in range(PAIR):
            z = stat[g, :, r]
            top = jnp.max(z, axis=0, keepdims=True)
            whole = top + jnp.log(jnp.sum(jnp.exp(z - top), axis=0, keepdims=True))
            factor = jnp.exp(mown[g % 2, r : r + 1] - whole)
            factor = jnp.transpose(jnp.broadcast_to(factor, (128, rows)))
            for k in range(latent // 128):
                part = acc[g % 2, r, :, k * 128 : (k + 1) * 128] * factor
                norm[g, :, :, :, r, :, k * 128 : (k + 1) * 128] = part.astype(BF16).reshape(
                    2, 2, 2, heads_rows, 128
                )
        fold_copy(g).start()

    def fold(g):
        fold_copy(g).wait_recv()
        crx[g] = (crx[g].astype(F32) + norm[g, c].astype(F32)).astype(BF16)
        cross_copy(g, 0).start()
        cross_copy(g, 1).start()

    def cross(g):
        cross_copy(g, 0).wait_recv()
        x2[g] = (x2[g].astype(F32) + crx[g, :, ex, 0].astype(F32)).astype(BF16)
        last_copy(g, 0).start()
        cross_copy(g, 1).wait_recv()
        y2[g] = (y2[g].astype(F32) + crx[g, ey, :, 1].astype(F32)).astype(BF16)
        last_copy(g, 1).start()

    def last(g):
        last_copy(g, 0).wait_recv()
        ctx2[g % 2, 0] = (x2[g, ey].astype(F32) + y3[g].astype(F32)).astype(BF16)
        last_copy(g, 1).wait_recv()
        ctx2[g % 2, 1] = (y2[g, ex].astype(F32) + x3[g].astype(F32)).astype(BF16)

        @pl.when(g % 2 == 1)
        def _():
            both = ctx2[...].reshape(4 * heads_rows, latent)
            for h in range(heads):
                every = jnp.dot(both, vu[h], preferred_element_type=F32).reshape(8, heads, vdim)
                mine = lax.broadcasted_iota(jnp.int32, every.shape, 1) == h
                place = pl.ds(pl.multiple_of((g // 2) * 8, 8), 8)
                ho[place, h * vdim : (h + 1) * vdim] = jnp.sum(
                    jnp.where(mine, every, 0.0), axis=1
                )

    vu_copy.wait()

    def step(s, _):
        def at(lag, run):
            @pl.when((s >= lag) & (s < chunks + lag))
            def _():
                run(s - lag)

        def forward(g):
            own_copy(g, 1).wait_recv()
            diag_copy(g, 0).start()
            core_copy(g, 0).start()
            own_copy(g, 2).wait_recv()
            diag_copy(g, 1).start()
            core_copy(g, 1).start()

        def forward_diag(g):
            for k in range(2):
                diag_copy(g, k).wait_recv()
                core_copy(g, 2 + k).start()

        def attend_when_here(g):
            own_copy(g, 0).wait_recv()
            for k in range(4):
                core_copy(g, k).wait_recv()
            attend(g)

        at(0, forward)
        at(1, forward_diag)

        at(4, normalise)
        at(5, fold)
        at(6, cross)
        at(7, last)

        @pl.when(s + AHEAD < chunks)
        def _():
            for k in range(3):
                own_copy(s + AHEAD, k).start()

        at(2, attend_when_here)

        @pl.when(s < SLOTS)
        def _():
            op_copy(s).start()

        @pl.when(s == SLOTS)
        def _():
            eg_copy.start()

        return 0

    lax.fori_loop(0, chunks + 7, step, 0)

    own_rows = res.shape[0]

    per_piece = per_half // PIECES

    def put(p, i, part):
        place = slice(i % per_piece * cols, (i % per_piece + 1) * cols)
        j = i % per_half // per_piece
        pbuf[p, i // per_half, j, :, :, place] = part.astype(BF16).reshape(4, own_rows, cols)
        if i % per_piece == per_piece - 1:
            if i < per_half:
                swap_copy(p, j).start()
            else:
                swap_copy(p, j).wait_recv()
                total = prx[p, j].astype(F32) + pbuf[p, 1, j].astype(F32)
                tsum[p, j] = total.astype(BF16)
                for k in (2, 0, 1):
                    rows_copy(p, j, k).start()

    def rows_total(p, j):
        total = tsum[p, j, e].astype(F32)
        for k in range(3):
            rows_copy(p, j, k).wait_recv()
            total = total + rrx[p, j, k].astype(F32)
        return total

    head_out = ho[...].astype(BF16)
    for i in range(BLOCKS):
        op_copy(i).wait()
        put(0, i, jnp.dot(head_out, wslot[i % SLOTS], preferred_element_type=F32))
        if i + SLOTS < BLOCKS:
            op_copy(i + SLOTS).start()
        if i == 1:
            for k in range(BLOCKS):
                down_copy(k).start()
        if i >= 2:
            for k in range(3) if i == 2 else (3,):
                up_copy(k).start()

    for j in range(PIECES):
        own_cols = pl.ds(pl.multiple_of(c * half + j * piece, piece), piece)
        hid[c, j, e] = (res[:, own_cols].astype(F32) + rows_total(0, j)).astype(BF16)
        for k in (2, 0, 1, 3):
            hid_copy(j, k).start()
    eg_copy.wait()

    squares, logits, gate_part, up_part = 0.0, 0.0, 0.0, 0.0
    for i in range(2 * PIECES):
        side, j, span = part_of(i)
        if i < PIECES:
            for k in range(3):
                hid_copy(j, k).wait_recv()
                hidfwd_copy(j, k).start()
        else:
            hid_copy(j, 3).wait_recv()
            for k in range(3):
                hidfwd_copy(j, k).wait_recv()
        wide = hid[side, j].astype(F32).reshape(4 * own_rows, piece)
        squares = squares + jnp.sum(wide * wide, axis=-1, keepdims=True)
        for k in range(piece // 128):
            lane = slice(k * 128, (k + 1) * 128)
            xn[i, :, lane] = (wide[:, lane] * spread[side * PIECES + j, k : k + 1]).astype(BF16)
        logits = logits + contract(xn[i], router[:, span], 1, 1)
        gate_part = gate_part + jnp.dot(xn[i], eg[span, :], preferred_element_type=F32)
        up_copy(i).wait()
        up_part = up_part + jnp.dot(xn[i], up_place(i)[...], preferred_element_type=F32)
    inverse = lax.rsqrt(squares / (2 * half) + 1e-06)
    gate_part, up_part = gate_part * inverse, up_part * inverse
    act[...] = (gate_part / (1.0 + jnp.exp(-gate_part)) * up_part).astype(BF16)
    for k in range(3):
        route_copy(k).wait_recv()
    affinity = jax.nn.sigmoid(logits * inverse)
    picked = affinity * chosen[...].reshape(4 * own_rows, 128)[:, : affinity.shape[1]]
    weights = route_scale * picked / jnp.sum(picked, axis=-1, keepdims=True)
    mine = lax.broadcasted_iota(jnp.int32, weights.shape, 1) == e
    gcol[...] = jnp.broadcast_to(
        jnp.sum(jnp.where(mine, weights, 0.0), axis=-1, keepdims=True), gcol.shape
    )

    for i in range(BLOCKS):
        down_copy(i).wait()
        block = wslot[1, i * depth : (i + 1) * depth]
        put(1, i, jnp.dot(act[...], block, preferred_element_type=F32) * gcol[:, 0:1])
    for j in range(PIECES):
        total = hid[c, j, e].astype(F32) + rows_total(1, j)
        out[:, j * piece : (j + 1) * piece] = total.astype(BF16)

    def drain(g, _):
        for k in range(3):
            own_copy(g, k).wait_send()
        for k in range(2):
            diag_copy(g, k).wait_send()
            cross_copy(g, k).wait_send()
            last_copy(g, k).wait_send()
        for k in range(4):
            core_copy(g, k).wait_send()
        for k in range(7):
            stat_copy(g, k).wait_send()
        fold_copy(g).wait_send()
        return 0

    lax.fori_loop(0, chunks, drain, 0)
    for k in range(3):
        route_copy(k).wait_send()
        for j in range(PIECES):
            hidfwd_copy(j, k).wait_send()
            rows_copy(0, j, k).wait_send()
            rows_copy(1, j, k).wait_send()
    for j in range(PIECES):
        for k in range(4):
            hid_copy(j, k).wait_send()
        for p in range(2):
            swap_copy(p, j).wait_send()


def fused_on_device(
    queries, latent_cache, context_lengths, value_up, out_proj, residual, norm_gain, router,
    routes, expert_gate, expert_up, expert_down,
):
    reqs, verify, heads, width = queries.shape
    chunks = reqs // PAIR
    hr = verify * heads
    _, block_len, _ = latent_cache.shape
    _, latent, vdim = value_up.shape
    own_rows, model = residual.shape
    half = model // 2
    piece = half // PIECES
    ff = expert_down.shape[1]
    rows = 8 * hr
    _, count = lay_out(chunks)
    vmem, anywhere = pl.BlockSpec(memory_space=pltpu.VMEM), pl.BlockSpec(memory_space=pl.ANY)
    scratch = [
        pltpu.VMEM((chunks, 8, PAIR, hr, width), BF16),
        pltpu.VMEM((2, PAIR, width, block_len), BF16),
        pltpu.VMEM((2, PAIR, rows, latent), F32),
        pltpu.VMEM((2, PAIR, rows), F32),
        pltpu.VMEM((chunks, 8, PAIR, rows), F32),
        pltpu.VMEM((chunks, 2, 2, 2, PAIR, hr, latent), BF16),
        pltpu.VMEM((chunks, 2, 2, PAIR, hr, latent), BF16),
        pltpu.VMEM((chunks, 2, hr, latent), BF16),
        pltpu.VMEM((chunks, 2, hr, latent), BF16),
        pltpu.VMEM((chunks, hr, latent), BF16),
        pltpu.VMEM((chunks, hr, latent), BF16),
        pltpu.VMEM((2, PAIR, hr, latent), BF16),
        pltpu.VMEM((heads, latent, vdim), BF16),
        pltpu.VMEM((reqs * verify, heads * vdim), F32),
        pltpu.VMEM((SLOTS, heads * vdim, model // BLOCKS), BF16),
        pltpu.VMEM((model, ff), BF16),
        pltpu.VMEM((PAIR, rows, block_len), F32),
        pltpu.VMEM((PAIR, rows, block_len), BF16),
        pltpu.VMEM((PAIR, rows, 128), F32),
        pltpu.VMEM((2 * PIECES, piece // 128, 128), F32),
        pltpu.VMEM((4, own_rows, 128), F32),
        pltpu.VMEM((2, 2, PIECES, 4, own_rows, piece), BF16),
        pltpu.VMEM((2, PIECES, 4, own_rows, piece), BF16),
        pltpu.VMEM((2, PIECES, 4, own_rows, piece), BF16),
        pltpu.VMEM((2, PIECES, 3, own_rows, piece), BF16),
        pltpu.VMEM((2, PIECES, 4, own_rows, piece), BF16),
        pltpu.VMEM((2 * PIECES, 4 * own_rows, piece), BF16),
        pltpu.VMEM((4 * own_rows, ff), BF16),
        pltpu.VMEM((4 * own_rows, 128), F32),
        pltpu.SemaphoreType.DMA((count,)),
        pltpu.SemaphoreType.DMA((count,)),
        pltpu.SemaphoreType.DMA((2,)),
        pltpu.SemaphoreType.DMA((4 + BLOCKS + 2 * PIECES,)),
        pltpu.SemaphoreType.DMA((SLOTS,)),
    ]
    return pl.pallas_call(
        layer_kernel,
        out_shape=jax.ShapeDtypeStruct((own_rows, half), BF16),
        in_specs=[pl.BlockSpec(memory_space=pltpu.SMEM)] + [anywhere] * 4 + [vmem] * 2
        + [vmem] * 2 + [anywhere] * 3,
        out_specs=vmem,
        scratch_shapes=scratch,
        compiler_params=pltpu.CompilerParams(
            collective_id=0, has_side_effects=True, vmem_limit_bytes=62 * 1024 * 1024
        ),
        cost_estimate=pl.CostEstimate(
            flops=6_000_000_000, bytes_accessed=64_000_000, transcendentals=2_000_000
        ),
    )(
        context_lengths,
        queries.reshape(chunks, PAIR, hr, width),
        jnp.swapaxes(latent_cache, 1, 2).reshape(chunks, PAIR, width, block_len),
        value_up,
        out_proj,
        residual,
        norm_gain.reshape(model // 128, 128),
        router.T,
        routes.T,
        expert_gate[0],
        expert_up[0],
        expert_down[0],
    )


def solution(mesh):
    grouped = mesh.shape["ctx"] == 2 and mesh.shape["exp"] == 4
    body = fused_on_device if grouped else on_device
    return jax.shard_map(
        body,
        mesh=mesh,
        in_specs=(
            P("req", None, ("ctx", "exp"), None),
            P("req", ("ctx", "exp"), None),
            P("req"),
            P(("ctx", "exp"), None, None),
            P(("ctx", "exp"), None),
            P(("req", "exp"), None),
            P(),
            P(),
            P(("req", "exp"), None),
            P("exp", None, "ctx"),
            P("exp", None, "ctx"),
            P("exp", "ctx", None),
        ),
        out_specs=P(("req", "exp"), "ctx"),
        check_vma=False,
    )
```
